32 devices in a mesh: clips: 8 (over y, x, core), seq: 4 (over z).
Axes of the slice: x: 2, y: 2, z: 4, core: 2. Of those that a mesh axis runs over, the one named last changes fastest.
Arguments:
- features: bfloat16 [32, 512, 256], P('clips', 'seq'), may hold values from -6 to 6
- clip_kind: int32 [32], P('clips'), may hold values from 0 to 1, as said below
- masked_positions: int32 [32, 400], P('clips'), may hold values from 0 to 511, as said below
- frame_proj: bfloat16 [256, 768], replicated, may hold values from -0.375 to 0.375
- patch_proj: bfloat16 [256, 768], replicated, may hold values from -0.375 to 0.375
- mask_embed: bfloat16 [768], replicated, may hold values from -5 to 5
- norm1_gain: bfloat16 [768], replicated, may hold values from 0.5 to 1.5
- norm1_bias: bfloat16 [768], replicated, may hold values from -1.5 to 1.5
- w_qkv: bfloat16 [768, 2304], replicated, may hold values from -0.21875 to 0.21875
- q_bias: bfloat16 [768], replicated, may hold values from -1.5 to 1.5
- v_bias: bfloat16 [768], replicated, may hold values from -1.5 to 1.5
- w_out: bfloat16 [768, 768], replicated, may hold values from -1.25 to 1.25
- out_bias: bfloat16 [768], replicated, may hold values from -1.5 to 1.5
- norm2_gain: bfloat16 [768], replicated, may hold values from 0.5 to 1.5
- norm2_bias: bfloat16 [768], replicated, may hold values from -1.5 to 1.5
- w_up: bfloat16 [768, 3072], replicated, may hold values from -0.21875 to 0.21875
- up_bias: bfloat16 [3072], replicated, may hold values from -1.5 to 1.5
- w_down: bfloat16 [3072, 768], replicated, may hold values from -0.109375 to 0.109375
- down_bias: bfloat16 [768], replicated, may hold values from -1.5 to 1.5
- cotangent: bfloat16 [32, 512, 768], P('clips', 'seq'), may hold values from -6 to 6
Outputs:
- layer_output: bfloat16 [32, 512, 768], P('clips', 'seq')
- features_grad: bfloat16 [32, 512, 256], P('clips', 'seq')
- frame_proj_grad: float32 [256, 768], P('clips')
- patch_proj_grad: float32 [256, 768], P('clips')
- mask_embed_grad: float32 [768], P('clips')
- norm1_gain_grad: float32 [768], P('clips')
- norm1_bias_grad: float32 [768], P('clips')
- w_qkv_grad: float32 [768, 2304], P('clips')
- q_bias_grad: float32 [768], P('clips')
- v_bias_grad: float32 [768], P('clips')
- w_out_grad: float32 [768, 768], P('clips')
- out_bias_grad: float32 [768], P('clips')
- norm2_gain_grad: float32 [768], P('clips')
- norm2_bias_grad: float32 [768], P('clips')
- w_up_grad: float32 [768, 3072], P('clips')
- up_bias_grad: float32 [3072], P('clips')
- w_down_grad: float32 [3072, 768], P('clips')
- down_bias_grad: float32 [768], P('clips')
The draws below stay inside these ranges and needn't reach their ends.
Inputs may be any that keep to these rules, and one draw needn't show every extreme that they name: `clip_kind`: exactly half of the 32 clips have kind 1. `masked_positions`: each row holds 400 different positions.
All inputs are finite; a program needn't handle non-finite values.
Results may differ from the reference program's by a relative error of at most 0.014.
Values may be sent and summed in bfloat16 or wider, within the bound.
No kernel may reach another device: no remote copies, remote signals or barrier semaphores. Data moves between devices by JAX's collectives and lax.ppermute only.
A program may use at most 128 MiB of HBM per device.

```python
import math
import jax
import jax.numpy as jnp
from jax import lax

HEADS = 12
HEAD_DIM = 64
D = 768
FF = 3072
FEAT = 256
LEN = 512
CLIPS = 32
NMASK = 400


def draw_clip_kind(key, part):
    key = jax.random.fold_in(key, 3)
    order = jax.random.permutation(key, CLIPS)
    return (order % 2).astype(jnp.int32)


def draw_masked_positions(key, part):
    key = jax.random.fold_in(key, 7)
    ordered = jnp.broadcast_to(jnp.arange(LEN, dtype=jnp.int32), (CLIPS, LEN))
    mixed = jax.random.permutation(key, ordered, axis=1, independent=True)
    return mixed[:, :NMASK].astype(jnp.int32)


def shard_levels(stream_key, extent, pieces, low, top_value):
    level = 1.0
    for dim, shards_of in pieces:
        steps = jax.random.uniform(jax.random.fold_in(jax.random.fold_in(stream_key, 6), dim), (shards_of,), jnp.float32, low / len(pieces), top_value / len(pieces))
        level = level * jnp.repeat(jnp.exp(steps), extent[dim] // shards_of).reshape((-1,) + (1,) * (len(extent) - 1 - dim))
    return level


def noise(rng, extent, scale, bound, cuts=(), held_as=jnp.bfloat16):
    values = jax.random.normal(rng, extent, jnp.float32) * scale
    if len(cuts) > 0:
        values = shard_levels(rng, extent, cuts, -0.22, 0.18) * values
    return jnp.clip(values, min=-bound, max=bound).astype(held_as)


def setup_inputs(seed: int = 0) -> dict:
    key_list = jax.random.split(jax.random.key(seed), 21)
    features = noise(key_list[0], (CLIPS, LEN, FEAT), 1.0, 6.0, ((0, 8), (1, 4)))
    clip_kind = draw_clip_kind(jax.random.fold_in(key_list[20], 71), 0)
    masked_positions = draw_masked_positions(jax.random.fold_in(key_list[20], 71), 0)
    frame_proj = noise(key_list[3], (FEAT, D), FEAT ** -0.5, 0.375)
    patch_proj = noise(key_list[4], (FEAT, D), FEAT ** -0.5, 0.375)
    mask_embed = noise(key_list[5], (D,), 1.0, 5.0)
    norm1_gain = jnp.clip(1.0 + 0.1 * jax.random.normal(key_list[6], (D,), jnp.float32), 0.5, 1.5).astype(jnp.bfloat16)
    norm1_bias = noise(key_list[7], (D,), 0.3, 1.5)
    w_qkv = noise(key_list[8], (D, 3 * D), D ** -0.5, 0.21875)
    q_bias = noise(key_list[9], (D,), 0.3, 1.5)
    v_bias = noise(key_list[10], (D,), 0.3, 1.5)
    w_out = noise(key_list[11], (D, D), (D // 32) ** -0.5, 1.25)
    out_bias = noise(key_list[12], (D,), 0.3, 1.5)
    norm2_gain = jnp.clip(1.0 + 0.1 * jax.random.normal(key_list[13], (D,), jnp.float32), 0.5, 1.5).astype(jnp.bfloat16)
    norm2_bias = noise(key_list[14], (D,), 0.3, 1.5)
    w_up = noise(key_list[15], (D, FF), D ** -0.5, 0.21875)
    up_bias = noise(key_list[16], (FF,), 0.3, 1.5)
    w_down = noise(key_list[17], (FF, D), FF ** -0.5, 0.109375)
    down_bias = noise(key_list[18], (D,), 0.3, 1.5)
    cotangent = noise(key_list[19], (CLIPS, LEN, D), 1.0, 6.0, ((0, 8), (1, 4)))
    return {"features": features, "clip_kind": clip_kind, "masked_positions": masked_positions, "frame_proj": frame_proj, "patch_proj": patch_proj, "mask_embed": mask_embed, "norm1_gain": norm1_gain, "norm1_bias": norm1_bias, "w_qkv": w_qkv, "q_bias": q_bias, "v_bias": v_bias, "w_out": w_out, "out_bias": out_bias, "norm2_gain": norm2_gain, "norm2_bias": norm2_bias, "w_up": w_up, "up_bias": up_bias, "w_down": w_down, "down_bias": down_bias, "cotangent": cotangent}


@jax.custom_vjp
def low(v):
    return lax.optimization_barrier(v.astype(jnp.bfloat16)).astype(jnp.float32)

@jax.custom_vjp
def low_back(v):
    return v

def low_keep(v):
    return (low(v), None)

def low_pass(kept, grad):
    return (grad,)

def back_keep(v):
    return (v, None)

def back_low(kept, grad):
    return (low(grad),)
low.defvjp(low_keep, low_pass)
low_back.defvjp(back_keep, back_low)
EPSILON = 1e-06
HIGHEST = lax.Precision.HIGHEST

def layer_norm(values_in, gain, shift):
    centre = values_in - lax.optimization_barrier(jnp.mean(values_in, axis=-1, keepdims=True))
    spread = lax.optimization_barrier(jnp.mean(centre * centre, axis=-1, keepdims=True))
    return centre * lax.rsqrt(spread + EPSILON) * gain + shift

def forward(params, features, clip_kind, is_masked):
    frame_proj, patch_proj, mask_embed, norm1_gain, norm1_bias, w_qkv, q_bias, v_bias, w_out, out_bias, norm2_gain, norm2_bias, w_up, up_bias, w_down, down_bias = params
    count = features.shape[0]
    length = features.shape[1]
    width = w_out.shape[0]
    chosen = jnp.where((clip_kind == 1)[:, None, None], patch_proj[None], frame_proj[None])
    embedded = low_back(jnp.einsum('ctf,cfd->ctd', features, chosen, precision=HIGHEST))
    start = jnp.where(is_masked[:, :, None], mask_embed[None, None, :], embedded)
    normed_one = low(layer_norm(start, norm1_gain, norm1_bias))
    qkv_bias = jnp.concatenate([q_bias, jnp.zeros_like(q_bias), v_bias])
    projected = jnp.einsum('ctd,de->cte', normed_one, w_qkv, precision=HIGHEST) + qkv_bias
    query = low(low_back(projected[..., :width])).reshape(count, length, HEADS, HEAD_DIM)
    keys = low(low_back(projected[..., width:2 * width])).reshape(count, length, HEADS, HEAD_DIM)
    values = low(low_back(projected[..., 2 * width:])).reshape(count, length, HEADS, HEAD_DIM)
    scores = low_back(jnp.einsum('cqhe,ckhe->chqk', query, keys, precision=HIGHEST) * HEAD_DIM ** (-0.5))
    row_top = lax.optimization_barrier(jnp.max(scores, axis=-1, keepdims=True))
    exponent = jnp.exp(scores - row_top)
    probs = low(exponent / lax.optimization_barrier(jnp.sum(exponent, axis=-1, keepdims=True)))
    attended = jnp.einsum('chqk,ckhe->cqhe', probs, values, precision=HIGHEST)
    attended = low(low_back(attended)).reshape(count, length, width)
    branch = low_back(jnp.einsum('ctd,de->cte', attended, w_out, precision=HIGHEST) + out_bias)
    middle = start + branch
    normed_two = low(layer_norm(middle, norm2_gain, norm2_bias))
    hidden_pre = low_back(jnp.einsum('ctd,df->ctf', normed_two, w_up, precision=HIGHEST) + up_bias)
    active = low(jax.nn.gelu(hidden_pre, approximate=False))
    return middle + jnp.einsum('ctf,fd->ctd', active, w_down, precision=HIGHEST) + down_bias

def add_pair(first_term, second_term):
    return first_term + second_term

def reference(features, clip_kind, masked_positions, frame_proj, patch_proj, mask_embed, norm1_gain, norm1_bias, w_qkv, q_bias, v_bias, w_out, out_bias, norm2_gain, norm2_bias, w_up, up_bias, w_down, down_bias, cotangent):
    params = tuple((p.astype(jnp.float32) for p in (frame_proj, patch_proj, mask_embed, norm1_gain, norm1_bias, w_qkv, q_bias, v_bias, w_out, out_bias, norm2_gain, norm2_bias, w_up, up_bias, w_down, down_bias)))
    positions = lax.iota(jnp.int32, LEN)
    is_masked = jnp.any(masked_positions[:, :, None] == positions[None, None, :], axis=1)
    group = math.gcd(CLIPS, 8)
    rounds = CLIPS // group

    def regroup(array):
        return array.reshape((rounds, group) + array.shape[1:])

    def one_group(carry, inputs):
        feats_now, kind_now, mask_now, cot_now = inputs

        def run(weights, feats_in):
            return forward(weights, feats_in, kind_now, mask_now)
        result, pull = jax.vjp(run, params, feats_now.astype(jnp.float32))
        weight_grads, feat_grads = pull(cot_now.astype(jnp.float32))
        carry = jax.tree.map(add_pair, carry, weight_grads)
        return (carry, (result.astype(jnp.bfloat16), feat_grads.astype(jnp.bfloat16)))
    initial = tuple((jnp.zeros_like(p) for p in params))
    totals, (outputs, feat_grads) = lax.scan(one_group, initial, (regroup(features), regroup(clip_kind), regroup(is_masked), regroup(cotangent)))
    layer_output = outputs.reshape(CLIPS, LEN, D)
    features_grad = feat_grads.reshape(CLIPS, LEN, FEAT)
    return (layer_output, features_grad, totals[0], totals[1], totals[2], totals[3], totals[4], totals[5], totals[6], totals[7], totals[8], totals[9], totals[10], totals[11], totals[12], totals[13], totals[14], totals[15])
```

```python
import jax
import jax.numpy as jnp
from jax import lax
from jax.sharding import PartitionSpec as P

HEADS = 12
HEAD_DIM = 64
EPSILON = 1e-06
F32 = jnp.float32
BF16 = jnp.bfloat16


def norm_stats(values_in):
    centre = values_in - jnp.mean(values_in, axis=-1, keepdims=True)
    inverse = lax.rsqrt(jnp.mean(centre * centre, axis=-1, keepdims=True) + EPSILON)
    return (centre * inverse, inverse)


def norm_back(grad_normed, centred, inverse, gain):
    scaled = grad_normed * gain
    return inverse * (
        scaled
        - jnp.mean(scaled, axis=-1, keepdims=True)
        - centred * jnp.mean(scaled * centred, axis=-1, keepdims=True)
    )


def gelu_slope(values_in):
    return (
        0.5 * (1.0 + lax.erf(values_in * 0.7071067811865476))
        + values_in * jnp.exp(-0.5 * values_in * values_in) * 0.3989422804014327
    )


def swap(block, axis, size, flip):
    return lax.ppermute(block, axis, [(i, i ^ flip) for i in range(size)])


def to_clip(pieces, me, size):
    out = [lax.dynamic_index_in_dim(pieces, me, 0, keepdims=False)]
    for d in range(1, size):
        out.append(swap(lax.dynamic_index_in_dim(pieces, me ^ d, 0, keepdims=False), "seq", size, d))
    return jnp.concatenate(out, axis=0)


def to_pieces(clip_rows, me, size):
    rel = clip_rows.reshape(size, -1, clip_rows.shape[-1])
    got = [rel[0]] + [swap(rel[d], "seq", size, d) for d in range(1, size)]
    return jnp.take(jnp.stack(got), lax.iota(jnp.int32, size) ^ me, axis=0)


def bits_of(n):
    return n.bit_length() - 1


def fold_clips(grad, order, n):
    count = bits_of(n)
    me = lax.axis_index("clips")
    rows, width = grad.shape
    held = grad.reshape((2,) * count + (rows // n, width))
    left = list(range(count - 1, -1, -1))
    for bit in order:
        axis = left.index(bit)
        mine = (me >> bit) & 1
        send = lax.dynamic_index_in_dim(held, 1 - mine, axis, keepdims=False)
        keep = lax.dynamic_index_in_dim(held, mine, axis, keepdims=False)
        held = keep + swap(send, "clips", n, 1 << bit)
        left.pop(axis)
    return held


def sum_seq(part, size):
    me = lax.axis_index("seq")
    rows, width = part.shape
    count = bits_of(size)
    held = part
    for bit in range(count):
        half = held.shape[1] // 2
        mine = (me >> bit) & 1
        send = lax.dynamic_slice_in_dim(held, (1 - mine) * half, half, 1)
        keep = lax.dynamic_slice_in_dim(held, mine * half, half, 1)
        held = keep + swap(send, "seq", size, 1 << bit)
    for bit in reversed(range(count)):
        got = swap(held, "seq", size, 1 << bit)
        mine = (me >> bit) & 1
        held = jnp.where(
            mine == 0, jnp.concatenate([held, got], axis=1), jnp.concatenate([got, held], axis=1)
        )
    return held


def clip_orders(n):
    count = bits_of(n)
    low = [0] if count else []
    rest = list(range(1, count))
    return low + rest, low + rest[::-1]


def reduce_grad(grad, n, size):
    first, second = clip_orders(n)
    half = grad.shape[1] // 2
    a = fold_clips(grad[:, :half].astype(BF16), first, n)
    b = fold_clips(grad[:, half:].astype(BF16), second, n)
    return sum_seq(jnp.concatenate([a, b], axis=1), size).astype(F32)


def body(
    features,
    clip_kind,
    masked_positions,
    frame_proj,
    patch_proj,
    mask_embed,
    norm1_gain,
    norm1_bias,
    w_qkv,
    q_bias,
    v_bias,
    w_out,
    out_bias,
    norm2_gain,
    norm2_bias,
    w_up,
    up_bias,
    w_down,
    down_bias,
    cotangent,
):
    n = lax.axis_size("clips")
    size = lax.axis_size("seq")
    me = lax.axis_index("seq")
    clips_here, rows_here, _ = features.shape
    assert clips_here == size
    width = w_out.shape[0]
    length = rows_here * size

    feats = to_clip(features, me, size)
    dy = to_clip(cotangent, me, size)
    kind = lax.dynamic_index_in_dim(clip_kind, me, 0, keepdims=False)
    masked = lax.dynamic_index_in_dim(masked_positions, me, 0, keepdims=False)
    token = lax.iota(jnp.int32, length)
    positions = ((token // rows_here) ^ me) * rows_here + token % rows_here
    is_masked = jnp.any(masked[None, :] == positions[:, None], axis=1)[:, None]

    is_patch = kind == 1
    chosen = jnp.where(is_patch, patch_proj, frame_proj)
    embedded = jnp.dot(feats, chosen, preferred_element_type=F32)
    residual_in = jnp.where(is_masked, mask_embed.astype(F32)[None, :], embedded)
    centred_one, inverse_one = norm_stats(residual_in)
    gain_one = norm1_gain.astype(F32)
    normed_one = (centred_one * gain_one + norm1_bias.astype(F32)).astype(BF16)
    qkv_bias = jnp.concatenate([q_bias, jnp.zeros_like(q_bias), v_bias]).astype(F32)
    projected = (jnp.dot(normed_one, w_qkv, preferred_element_type=F32) + qkv_bias).astype(BF16)
    heads = projected.reshape(length, 3, HEADS, HEAD_DIM)
    query, keys, values = heads[:, 0], heads[:, 1], heads[:, 2]
    scale = HEAD_DIM ** (-0.5)
    scores = jnp.einsum("qhe,khe->hqk", query, keys, preferred_element_type=F32) * scale
    top = jnp.max(scores, axis=-1, keepdims=True)
    exponent = jnp.exp(scores - top)
    probs = exponent / jnp.sum(exponent, axis=-1, keepdims=True)
    probs_low = probs.astype(BF16)
    attended = jnp.einsum("hqk,khe->qhe", probs_low, values, preferred_element_type=F32)
    attended = attended.reshape(length, width).astype(BF16)
    middle = residual_in + jnp.dot(attended, w_out, preferred_element_type=F32) + out_bias.astype(F32)
    centred_two, inverse_two = norm_stats(middle)
    gain_two = norm2_gain.astype(F32)
    normed_two = (centred_two * gain_two + norm2_bias.astype(F32)).astype(BF16)
    hidden_pre = jnp.dot(normed_two, w_up, preferred_element_type=F32) + up_bias.astype(F32)
    active = jax.nn.gelu(hidden_pre, approximate=False).astype(BF16)
    output = middle + jnp.dot(active, w_down, preferred_element_type=F32) + down_bias.astype(F32)
    output = to_pieces(output.astype(BF16), me, size)

    dy_float = dy.astype(F32)
    down_grad = reduce_grad(jnp.dot(active.T, dy, preferred_element_type=F32), n, size)
    down_bias_grad = jnp.sum(dy_float, axis=0)
    grad_active = jnp.dot(dy, w_down.T, preferred_element_type=F32)
    grad_hidden = (grad_active * gelu_slope(hidden_pre)).astype(BF16)
    up_grad = reduce_grad(jnp.dot(normed_two.T, grad_hidden, preferred_element_type=F32), n, size)
    up_bias_grad = jnp.sum(grad_hidden.astype(F32), axis=0)
    grad_normed_two = jnp.dot(grad_hidden, w_up.T, preferred_element_type=F32)
    norm2_gain_grad = jnp.sum(grad_normed_two * centred_two, axis=0)
    norm2_bias_grad = jnp.sum(grad_normed_two, axis=0)
    grad_middle = dy_float + norm_back(grad_normed_two, centred_two, inverse_two, gain_two)
    grad_branch = grad_middle.astype(BF16)
    out_bias_grad = jnp.sum(grad_branch.astype(F32), axis=0)
    out_grad = reduce_grad(jnp.dot(attended.T, grad_branch, preferred_element_type=F32), n, size)
    grad_attended = jnp.dot(grad_branch, w_out.T, preferred_element_type=F32).astype(BF16)
    grad_attended = grad_attended.reshape(length, HEADS, HEAD_DIM)
    grad_probs = jnp.einsum("qhe,khe->hqk", grad_attended, values, preferred_element_type=F32)
    inner = jnp.sum(grad_probs * probs, axis=-1, keepdims=True)
    grad_scores = (probs * (grad_probs - inner)).astype(BF16)
    grad_query = jnp.einsum("hqk,khe->qhe", grad_scores, keys, preferred_element_type=F32) * scale
    grad_keys = jnp.einsum("hqk,qhe->khe", grad_scores, query, preferred_element_type=F32) * scale
    grad_values = jnp.einsum("hqk,qhe->khe", probs_low, grad_attended, preferred_element_type=F32)
    grad_qkv = jnp.concatenate(
        [g.reshape(length, width).astype(BF16) for g in (grad_query, grad_keys, grad_values)], axis=-1
    )
    qkv_grad = reduce_grad(jnp.dot(normed_one.T, grad_qkv, preferred_element_type=F32), n, size)
    bias_sums = jnp.sum(grad_qkv.astype(F32), axis=0)
    grad_normed_one = jnp.dot(grad_qkv, w_qkv.T, preferred_element_type=F32)
    norm1_gain_grad = jnp.sum(grad_normed_one * centred_one, axis=0)
    norm1_bias_grad = jnp.sum(grad_normed_one, axis=0)
    grad_start = grad_middle + norm_back(grad_normed_one, centred_one, inverse_one, gain_one)
    mask_grad = jnp.sum(jnp.where(is_masked, grad_start, 0.0), axis=0)
    grad_embed = jnp.where(is_masked, 0.0, grad_start).astype(BF16)
    chosen_grad = jnp.dot(feats.T, grad_embed, preferred_element_type=F32).astype(BF16)
    features_grad = jnp.dot(grad_embed, chosen.T, preferred_element_type=F32).astype(BF16)
    features_grad = to_pieces(features_grad, me, size)

    vectors = (
        mask_grad,
        norm1_gain_grad,
        norm1_bias_grad,
        bias_sums[:width],
        bias_sums[2 * width :],
        out_bias_grad,
        norm2_gain_grad,
        norm2_bias_grad,
        up_bias_grad,
        down_bias_grad,
    )
    flat = jnp.concatenate([v.reshape(n, -1) for v in vectors], axis=1)
    feat_rows = frame_proj.shape[0] // n
    lanes = -(-flat.shape[1] // (feat_rows * 128)) * 128
    small = jnp.pad(flat, ((0, 0), (0, feat_rows * lanes - flat.shape[1])))
    small = small.reshape(n * feat_rows, lanes).astype(BF16)
    none = jnp.zeros_like(chosen_grad)
    last = jnp.concatenate(
        [jnp.where(is_patch, none, chosen_grad), jnp.where(is_patch, chosen_grad, none), small], axis=1
    )
    last = sum_seq(fold_clips(last, clip_orders(n)[0], n), size).astype(F32)
    frame_grad = last[:, :width]
    patch_grad = last[:, width : 2 * width]
    flat = last[:, 2 * width :].reshape(-1)
    small_out = []
    at = 0
    for v in vectors:
        small_out.append(flat[at : at + v.shape[0] // n])
        at += v.shape[0] // n
    (
        mask_out,
        gain1_out,
        bias1_out,
        q_out,
        v_out,
        outb_out,
        gain2_out,
        bias2_out,
        upb_out,
        downb_out,
    ) = small_out
    return (
        output,
        features_grad,
        frame_grad,
        patch_grad,
        mask_out,
        gain1_out,
        bias1_out,
        qkv_grad,
        q_out,
        v_out,
        out_grad,
        outb_out,
        gain2_out,
        bias2_out,
        up_grad,
        upb_out,
        down_grad,
        downb_out,
    )


def solution(mesh):
    tokens = P("clips", "seq", None)
    rows = P("clips", None)
    vec = P("clips")
    return jax.shard_map(
        body,
        mesh=mesh,
        in_specs=(tokens, P("clips"), rows) + (P(),) * 16 + (tokens,),
        out_specs=(tokens, tokens, rows, rows, vec, vec, vec, rows, vec, vec, rows, vec, vec, vec, rows, vec, rows, vec),
        check_vma=False,
    )
```

```python
import functools

import jax
import jax.numpy as jnp
from jax import lax
from jax.experimental import pallas as pl
from jax.experimental.pallas import tpu as pltpu
from jax.sharding import PartitionSpec as P

HEADS = 12
HEAD_DIM = 64
EPSILON = 1e-06
F32 = jnp.float32
BF16 = jnp.bfloat16
MIB = 1 << 20
SCALE = HEAD_DIM ** (-0.5)
Q_BIAS, NO_BIAS, V_BIAS, MASK_EMBED, GAIN_ONE, BIAS_ONE, OUT_BIAS, GAIN_TWO, BIAS_TWO, DOWN_BIAS = range(10)
PAIR = 2 * HEAD_DIM


def norm_stats(values_in):
    centre = values_in - jnp.mean(values_in, axis=-1, keepdims=True)
    inverse = lax.rsqrt(jnp.mean(centre * centre, axis=-1, keepdims=True) + EPSILON)
    return (centre * inverse, inverse)


def norm_back(grad_normed, centred, inverse, gain):
    scaled = grad_normed * gain
    return inverse * (
        scaled
        - jnp.mean(scaled, axis=-1, keepdims=True)
        - centred * jnp.mean(scaled * centred, axis=-1, keepdims=True)
    )


def mm(a, b):
    return jnp.dot(a, b, preferred_element_type=F32)


def mm_nt(a, b):
    return lax.dot_general(a, b, (((1,), (1,)), ((), ())), preferred_element_type=F32)


def whole(shape):
    return pl.BlockSpec(shape, lambda *_: (0,) * len(shape))


def masked_column(place, masked_ref, size, rows):
    marks = masked_ref[...]
    cols = []
    for d in range(size):
        spot = (place ^ d) * rows + lax.broadcasted_iota(jnp.int32, (rows, marks.shape[1]), 0)
        cols.append(jnp.max(jnp.where(spot == marks, 1.0, 0.0), axis=1, keepdims=True))
    return jnp.concatenate(cols, axis=0) > 0.5


def half_of(pair_block, h):
    lane = lax.broadcasted_iota(jnp.int32, pair_block.shape, 1)
    inside = (lane < HEAD_DIM) if h == 0 else (lane >= HEAD_DIM)
    return jnp.where(inside, pair_block, jnp.zeros_like(pair_block))


def embed_kernel(size, rows, info, masked, feats, frame, patch, table, w, start, normed_t, qkv, normed):
    j = pl.program_id(0)

    @pl.when(j == 0)
    def _():
        chosen = jnp.where(info[1] == 1, patch[...], frame[...])
        embedded = mm(feats[...], chosen)
        is_masked = masked_column(info[0], masked, size, rows)
        start_now = jnp.where(is_masked, table[MASK_EMBED : MASK_EMBED + 1, :], embedded)
        start[...] = start_now
        centred, _inv = norm_stats(start_now)
        out = (centred * table[GAIN_ONE : GAIN_ONE + 1, :] + table[BIAS_ONE : BIAS_ONE + 1, :]).astype(BF16)
        normed[...] = out
        normed_t[...] = out.T

    projected = mm(normed[...], w[...]) + table[pl.ds(j, 1), :]
    qkv[...] = (projected * jnp.where(j == 0, SCALE, 1.0)).astype(BF16)


def embed_call(info, masked, feats, frame, patch, table, w_qkv, size, rows):
    t, f = feats.shape
    d = frame.shape[1]
    smem = pl.BlockSpec(memory_space=pltpu.SMEM)
    return pl.pallas_call(
        functools.partial(embed_kernel, size, rows),
        grid=(3,),
        in_specs=[
            smem,
            whole(masked.shape),
            whole((t, f)),
            whole((f, d)),
            whole((f, d)),
            whole(table.shape),
            pl.BlockSpec((d, d), lambda j: (0, j)),
        ],
        out_specs=[whole((t, d)), whole((d, t)), pl.BlockSpec((t, d), lambda j: (0, j))],
        out_shape=[
            jax.ShapeDtypeStruct((t, d), F32),
            jax.ShapeDtypeStruct((d, t), BF16),
            jax.ShapeDtypeStruct((t, 3 * d), BF16),
        ],
        scratch_shapes=[pltpu.VMEM((t, d), BF16)],
        compiler_params=pltpu.CompilerParams(vmem_limit_bytes=40 * MIB),
        cost_estimate=pl.CostEstimate(flops=2 * t * d * (f + 3 * d), bytes_accessed=12 * MIB, transcendentals=0),
        name="embed",
    )(info, masked, feats, frame, patch, table, w_qkv)


def attend_kernel(q, k, v, start, table, w_out, probs, att_t, middle, normed, normed_t, att):
    p = pl.program_id(0)
    v_t = v[...].T
    parts = []
    for h in range(2):
        scores = mm_nt(k[...], half_of(q[...], h))
        top = jnp.max(scores, axis=0, keepdims=True)
        e = jnp.exp(scores - top)
        total = jnp.sum(e, axis=0, keepdims=True)
        low = (e * (1.0 / total)).astype(BF16)
        probs[h] = low
        parts.append(mm(v_t[h * HEAD_DIM : (h + 1) * HEAD_DIM, :], low))
    out_t = jnp.concatenate(parts, axis=0)
    att_t[...] = out_t.astype(BF16)
    att[:, pl.ds(pl.multiple_of(p * PAIR, PAIR), PAIR)] = out_t.T.astype(BF16)

    @pl.when(p == pl.num_programs(0) - 1)
    def _():
        mid = start[...] + mm(att[...], w_out[...]) + table[OUT_BIAS : OUT_BIAS + 1, :]
        middle[...] = mid
        centred, _inv = norm_stats(mid)
        out = (centred * table[GAIN_TWO : GAIN_TWO + 1, :] + table[BIAS_TWO : BIAS_TWO + 1, :]).astype(BF16)
        normed[...] = out
        normed_t[...] = out.T


def attend_call(qkv, start, table, w_out):
    t, d = start.shape
    pairs = HEADS // 2

    def block(base):
        return pl.BlockSpec((t, PAIR), lambda p: (0, base + p))

    return pl.pallas_call(
        attend_kernel,
        grid=(pairs,),
        in_specs=[
            block(0),
            block(pairs),
            block(2 * pairs),
            whole((t, d)),
            whole(table.shape),
            whole((d, d)),
        ],
        out_specs=[
            pl.BlockSpec((2, t, t), lambda p: (p, 0, 0)),
            pl.BlockSpec((PAIR, t), lambda p: (p, 0)),
            whole((t, d)),
            whole((t, d)),
            whole((d, t)),
        ],
        out_shape=[
            jax.ShapeDtypeStruct((HEADS, t, t), BF16),
            jax.ShapeDtypeStruct((d, t), BF16),
            jax.ShapeDtypeStruct((t, d), F32),
            jax.ShapeDtypeStruct((t, d), BF16),
            jax.ShapeDtypeStruct((d, t), BF16),
        ],
        scratch_shapes=[pltpu.VMEM((t, d), BF16)],
        compiler_params=pltpu.CompilerParams(vmem_limit_bytes=40 * MIB),
        cost_estimate=pl.CostEstimate(
            flops=2 * t * d * (8 * t + d), bytes_accessed=20 * MIB, transcendentals=HEADS * t * t
        ),
        name="attend",
    )(qkv, qkv, qkv, start, table, w_out)


def feed_kernel(normed, normed_t, dy, middle, table, w_up, b_up, w_down, out, grad_n, down_g, up_g, up_b, total):
    c = pl.program_id(0)

    @pl.when(c == 0)
    def _():
        total[...] = middle[...] + table[DOWN_BIAS : DOWN_BIAS + 1, :]
        grad_n[...] = jnp.zeros_like(grad_n)

    hidden = mm(normed[...], w_up[...]) + b_up[...]
    phi = 0.5 * (1.0 + lax.erf(hidden * 0.7071067811865476))
    slope = phi + hidden * jnp.exp(-0.5 * hidden * hidden) * 0.3989422804014327
    active = (hidden * phi).astype(BF16)
    total[...] += mm(active, w_down[...])
    down_g[...] = mm(active.T, dy[...]).astype(BF16)
    grad_h = mm_nt(dy[...], w_down[...]) * slope
    low = grad_h.astype(BF16)
    up_b[...] = jnp.sum(low.astype(F32), axis=0, keepdims=True)
    up_g[...] = mm(normed_t[...], low).astype(BF16)
    grad_n[...] += mm_nt(low, w_up[...])

    @pl.when(c == pl.num_programs(0) - 1)
    def _():
        out[...] = total[...].astype(BF16)


def feed_call(normed, normed_t, dy, middle, table, w_up, b_up, w_down, step):
    t, d = normed.shape
    ff = w_up.shape[1]
    return pl.pallas_call(
        feed_kernel,
        grid=(ff // step,),
        in_specs=[
            whole((t, d)),
            whole((d, t)),
            whole((t, d)),
            whole((t, d)),
            whole(table.shape),
            pl.BlockSpec((d, step), lambda c: (0, c)),
            pl.BlockSpec((1, step), lambda c: (0, c)),
            pl.BlockSpec((step, d), lambda c: (c, 0)),
        ],
        out_specs=[
            whole((t, d)),
            whole((t, d)),
            pl.BlockSpec((step, d), lambda c: (c, 0)),
            pl.BlockSpec((d, step), lambda c: (0, c)),
            pl.BlockSpec((1, step), lambda c: (0, c)),
        ],
        out_shape=[
            jax.ShapeDtypeStruct((t, d), BF16),
            jax.ShapeDtypeStruct((t, d), F32),
            jax.ShapeDtypeStruct((ff, d), BF16),
            jax.ShapeDtypeStruct((d, ff), BF16),
            jax.ShapeDtypeStruct((1, ff), F32),
        ],
        scratch_shapes=[pltpu.VMEM((t, d), F32)],
        compiler_params=pltpu.CompilerParams(vmem_limit_bytes=44 * MIB),
        cost_estimate=pl.CostEstimate(flops=12 * t * d * ff, bytes_accessed=26 * MIB, transcendentals=2 * t * ff),
        name="feed",
    )(normed, normed_t, dy, middle, table, w_up, b_up, w_down)


def middle_kernel(grad_n, middle, dy, att_t, table, w_out, grad_mid, grad_att, out_g, sums):
    centred, inverse = norm_stats(middle[...])
    grad = grad_n[...]
    dy_f = dy[...].astype(F32)
    mid = dy_f + norm_back(grad, centred, inverse, table[GAIN_TWO : GAIN_TWO + 1, :])
    grad_mid[...] = mid
    low = mid.astype(BF16)
    sums[...] = jnp.concatenate(
        [
            jnp.sum(low.astype(F32), axis=0, keepdims=True),
            jnp.sum(grad * centred, axis=0, keepdims=True),
            jnp.sum(grad, axis=0, keepdims=True),
            jnp.sum(dy_f, axis=0, keepdims=True),
            jnp.zeros((4, mid.shape[1]), F32),
        ],
        axis=0,
    )
    grad_att[...] = mm_nt(low, w_out[...]).astype(BF16)
    out_g[...] = mm(att_t[...], low).astype(BF16)


def middle_call(grad_n, middle, dy, att_t, table, w_out):
    t, d = middle.shape
    return pl.pallas_call(
        middle_kernel,
        out_shape=[
            jax.ShapeDtypeStruct((t, d), F32),
            jax.ShapeDtypeStruct((t, d), BF16),
            jax.ShapeDtypeStruct((d, d), BF16),
            jax.ShapeDtypeStruct((8, d), F32),
        ],
        compiler_params=pltpu.CompilerParams(vmem_limit_bytes=40 * MIB),
        cost_estimate=pl.CostEstimate(flops=4 * t * d * d, bytes_accessed=10 * MIB, transcendentals=0),
        name="middle",
    )(grad_n, middle, dy, att_t, table, w_out)


def back_kernel(q, k, v, probs, grad_a, normed_t, wq, wk, wv, gq, gk, gv, grad_n, sums):
    p = pl.program_id(0)

    @pl.when(p == 0)
    def _():
        grad_n[...] = jnp.zeros_like(grad_n)

    k_t = k[...].T
    dk = dv = None
    dq_t = []
    for h in range(2):
        low = probs[h]
        grad_h = half_of(grad_a[...], h)
        grad_p = mm_nt(v[...], grad_h)
        wide = low.astype(F32)
        inner = jnp.sum(wide * grad_p, axis=0, keepdims=True)
        grad_s = (wide * (grad_p - inner)).astype(BF16)
        dv_h = mm(low, grad_h)
        dk_h = mm(grad_s, half_of(q[...], h))
        dv = dv_h if dv is None else dv + dv_h
        dk = dk_h if dk is None else dk + dk_h
        dq_t.append(mm(k_t[h * HEAD_DIM : (h + 1) * HEAD_DIM, :], grad_s))
    dq = (jnp.concatenate(dq_t, axis=0).T * SCALE).astype(BF16)
    grads = jnp.concatenate([dq, dk.astype(BF16), dv.astype(BF16)], axis=1)
    weights = jnp.concatenate([wq[...], wk[...], wv[...]], axis=1)
    sums[...] = jnp.sum(grads.astype(F32), axis=0, keepdims=True)[None]
    g = mm(normed_t[...], grads).astype(BF16)
    gq[...] = g[:, :PAIR]
    gk[...] = g[:, PAIR : 2 * PAIR]
    gv[...] = g[:, 2 * PAIR :]
    grad_n[...] += mm_nt(grads, weights)


def back_call(qkv, probs, grad_att, normed_t, w_qkv):
    t, d = grad_att.shape
    pairs = HEADS // 2

    def block(rows, base):
        return pl.BlockSpec((rows, PAIR), lambda p: (0, base + p))

    return pl.pallas_call(
        back_kernel,
        grid=(pairs,),
        in_specs=[
            block(t, 0),
            block(t, pairs),
            block(t, 2 * pairs),
            pl.BlockSpec((2, t, t), lambda p: (p, 0, 0)),
            block(t, 0),
            whole((d, t)),
            block(d, 0),
            block(d, pairs),
            block(d, 2 * pairs),
        ],
        out_specs=[
            block(d, 0),
            block(d, 0),
            block(d, 0),
            whole((t, d)),
            pl.BlockSpec((1, 1, 3 * PAIR), lambda p: (p, 0, 0)),
        ],
        out_shape=[jax.ShapeDtypeStruct((d, d), BF16)] * 3
        + [jax.ShapeDtypeStruct((t, d), F32), jax.ShapeDtypeStruct((pairs, 1, 3 * PAIR), F32)],
        compiler_params=pltpu.CompilerParams(vmem_limit_bytes=40 * MIB),
        cost_estimate=pl.CostEstimate(flops=2 * t * d * (16 * t + 6 * d), bytes_accessed=24 * MIB, transcendentals=0),
        name="back",
    )(qkv, qkv, qkv, probs, grad_att, normed_t, w_qkv, w_qkv, w_qkv)


def last_kernel(size, rows, info, masked, grad_n, start, grad_mid, feats, frame, patch, table, feats_g, chosen_g, sums):
    centred, inverse = norm_stats(start[...])
    grad = grad_n[...]
    total = grad_mid[...] + norm_back(grad, centred, inverse, table[GAIN_ONE : GAIN_ONE + 1, :])
    is_masked = masked_column(info[0], masked, size, rows)
    kept = jnp.where(is_masked, 0.0, total)
    sums[...] = jnp.concatenate(
        [
            jnp.sum(jnp.where(is_masked, total, 0.0), axis=0, keepdims=True),
            jnp.sum(grad * centred, axis=0, keepdims=True),
            jnp.sum(grad, axis=0, keepdims=True),
            jnp.zeros((5, total.shape[1]), F32),
        ],
        axis=0,
    )
    low = kept.astype(BF16)
    chosen = jnp.where(info[1] == 1, patch[...], frame[...])
    feats_g[...] = mm_nt(low, chosen).astype(BF16)
    chosen_g[...] = mm(feats[...].T, low).astype(BF16)


def last_call(info, masked, grad_n, start, grad_mid, feats, frame, patch, table, size, rows):
    t, d = start.shape
    f = feats.shape[1]
    vmem = pl.BlockSpec(memory_space=pltpu.VMEM)
    return pl.pallas_call(
        functools.partial(last_kernel, size, rows),
        in_specs=[pl.BlockSpec(memory_space=pltpu.SMEM)] + [vmem] * 8,
        out_shape=[
            jax.ShapeDtypeStruct((t, f), BF16),
            jax.ShapeDtypeStruct((f, d), BF16),
            jax.ShapeDtypeStruct((8, d), F32),
        ],
        compiler_params=pltpu.CompilerParams(vmem_limit_bytes=40 * MIB),
        cost_estimate=pl.CostEstimate(flops=4 * t * d * f, bytes_accessed=6 * MIB, transcendentals=0),
        name="last",
    )(info, masked, grad_n, start, grad_mid, feats, frame, patch, table)


LANES = 256
SEGMENT = 128
SMEM = pl.BlockSpec(memory_space=pltpu.SMEM)
HBM = pl.BlockSpec(memory_space=pltpu.HBM)


def pinned(array):
    return pltpu.with_memory_space_constraint(array, pltpu.HBM)


def place_of(info, chip, x_first):
    rel = jnp.bitwise_xor(chip, info[1] // 2)
    return (rel % 2) * 2 + rel // 2 if x_first else rel


def is_first_core(info):
    return info[1] % 2 == 0


def spread(value, rows, at, send, keep, info, x_first):
    first = is_first_core(info)
    for chip in range(4):
        even = value[2 * chip * rows : (2 * chip + 1) * rows]
        odd = value[(2 * chip + 1) * rows : (2 * chip + 2) * rows]
        place = place_of(info, chip, x_first)
        keep[pl.ds(place, 1), at : at + rows, :] = jnp.where(first, even, odd)[None]
        send[pl.ds(place, 1), at : at + rows, :] = jnp.where(first, odd, even)[None]


def spread_halves(value, at, send, keep, info):
    first = is_first_core(info)
    rows = value.shape[0] // 8
    half = rows // 2
    for i in range(2):
        for chip in range(4):
            begin = 2 * chip * rows + i * half
            even, odd = value[begin : begin + half], value[begin + rows : begin + rows + half]
            place = pl.ds(place_of(info, chip, i == 0), 1)
            keep[i, place, at : at + half, :] = jnp.where(first, even, odd)[None]
            send[i, place, at : at + half, :] = jnp.where(first, odd, even)[None]


def stacked(refs):
    return jnp.concatenate([r[...] for r in refs], axis=0)


def clip_mask(info, masked, size, rows):
    return masked_column(info[0], masked.at[pl.ds(info[0], 1)], size, rows)


def forward_kernel(
    size, rows, info, kinds, masked, *refs,
):
    feats, refs = refs[:size], refs[size:]
    (
        table, frame, patch, w_qkv, w_out,
        hat, inverse_t, normed_t, qkv_a, qkv_b, qkv_c, probs_a, probs_b, probs_c, att_t,
        middle, normed_two, normed_two_t, feats_t,
        start, normed, att, projs, w_in, w_back, sems,
    ) = refs
    qkvs, all_probs = (qkv_a, qkv_b, qkv_c), (probs_a, probs_b, probs_c)
    s = pl.program_id(0)
    d = att.shape[1]
    third = d // LANES

    def weight_copy(group, i):
        cols = pl.ds(pl.multiple_of(i * d + group * LANES, LANES), LANES)
        return pltpu.make_async_copy(w_qkv.at[:, cols], w_in.at[group, :, pl.ds(i * LANES, LANES)], sems.at[group, i])

    proj_copies = [pltpu.make_async_copy(p, projs.at[i], sems.at[third, i]) for i, p in enumerate((frame, patch))]
    out_copy = pltpu.make_async_copy(w_out, w_back, sems.at[third, 2])

    @pl.when(s == 0)
    def _():
        for copy in proj_copies:
            copy.start()
        for group in range(third):
            for i in range(3):
                weight_copy(group, i).start()
        out_copy.start()
        is_masked = clip_mask(info, masked, size, rows)
        features = stacked(feats)
        feats_t[...] = features.T
        for copy in proj_copies:
            copy.wait()
        chosen = jnp.where(kinds[info[0]] == 1, projs[1], projs[0])
        start_now = jnp.where(is_masked, table[MASK_EMBED : MASK_EMBED + 1, :], mm(features, chosen))
        start[...] = start_now
        centred, inverse = norm_stats(start_now)
        hat[...] = centred.astype(BF16)
        inverse_t[...] = jnp.broadcast_to(inverse, inverse_t.shape)
        out = (centred * table[GAIN_ONE : GAIN_ONE + 1, :] + table[BIAS_ONE : BIAS_ONE + 1, :]).astype(BF16)
        normed[...] = out
        normed_t[...] = out.T

    for i in range(3):
        weight_copy(s, i).wait()
    lanes = pl.ds(pl.multiple_of(s * LANES, LANES), LANES)
    projected = mm(normed[...], w_in[s])
    q = ((projected[:, :LANES] + table[Q_BIAS : Q_BIAS + 1, lanes]) * SCALE).astype(BF16)
    k = projected[:, LANES : 2 * LANES].astype(BF16)
    v = (projected[:, 2 * LANES :] + table[V_BIAS : V_BIAS + 1, lanes]).astype(BF16)
    v_t = v.T
    parts, lows = [], []
    for h in range(4):
        pair = slice((h // 2) * PAIR, (h // 2 + 1) * PAIR)
        scores = mm_nt(k[:, pair], half_of(q[:, pair], h % 2))
        top = jnp.max(scores, axis=0, keepdims=True)
        e = jnp.exp(scores - top)
        total = jnp.sum(e, axis=0, keepdims=True)
        low = (e * (1.0 / total)).astype(BF16)
        lows.append(low)
        parts.append(mm(v_t[h * HEAD_DIM : (h + 1) * HEAD_DIM, :], low))
    for group in range(third):

        @pl.when(s == group)
        def _():
            for i, value in enumerate((q, k, v)):
                qkvs[group][:, i * LANES : (i + 1) * LANES] = value
            for h in range(4):
                all_probs[group][h] = lows[h]

    out_t = jnp.concatenate(parts, axis=0).astype(BF16)
    att_t[...] = out_t
    att[:, lanes] = out_t.T

    @pl.when(s == pl.num_programs(0) - 1)
    def _():
        out_copy.wait()
        mid = start[...] + mm(att[...], w_back[...]) + table[OUT_BIAS : OUT_BIAS + 1, :]
        middle[...] = mid
        centred, _inv = norm_stats(mid)
        out = (centred * table[GAIN_TWO : GAIN_TWO + 1, :] + table[BIAS_TWO : BIAS_TWO + 1, :]).astype(BF16)
        normed_two[...] = out
        normed_two_t[...] = out.T


def forward_call(info, kinds, masked, feats, frame, patch, table, w_qkv, w_out, size, rows):
    f, d = frame.shape
    t = size * rows
    third = d // LANES
    return pl.pallas_call(
        functools.partial(forward_kernel, size, rows),
        grid=(third,),
        in_specs=[SMEM, SMEM, whole(masked.shape)] + [whole((rows, f))] * size + [whole(table.shape)] + [HBM] * 4,
        out_specs=[
            whole((t, d)),
            whole((t, 128)),
            whole((d, t)),
            *([whole((t, 3 * LANES))] * third),
            *([whole((4, t, t))] * third),
            pl.BlockSpec((LANES, t), lambda s: (s, 0)),
            whole((t, d)),
            whole((t, d)),
            whole((d, t)),
            whole((f, t)),
        ],
        out_shape=[
            jax.ShapeDtypeStruct((t, d), BF16),
            jax.ShapeDtypeStruct((t, 128), F32),
            jax.ShapeDtypeStruct((d, t), BF16),
            *([jax.ShapeDtypeStruct((t, 3 * LANES), BF16)] * third),
            *([jax.ShapeDtypeStruct((4, t, t), BF16)] * third),
            jax.ShapeDtypeStruct((d, t), BF16),
            jax.ShapeDtypeStruct((t, d), F32),
            jax.ShapeDtypeStruct((t, d), BF16),
            jax.ShapeDtypeStruct((d, t), BF16),
            jax.ShapeDtypeStruct((f, t), BF16),
        ],
        scratch_shapes=[
            pltpu.VMEM((t, d), F32),
            pltpu.VMEM((t, d), BF16),
            pltpu.VMEM((t, d), BF16),
            pltpu.VMEM((2, f, d), BF16),
            pltpu.VMEM((third, d, 3 * LANES), BF16),
            pltpu.VMEM((d, d), BF16),
            pltpu.SemaphoreType.DMA((third + 1, 3)),
        ],
        compiler_params=pltpu.CompilerParams(vmem_limit_bytes=FORWARD_MIB * MIB),
        cost_estimate=pl.CostEstimate(
            flops=2 * t * d * (f + 4 * d + 8 * t), bytes_accessed=24 * MIB, transcendentals=HEADS * t * t
        ),
        name="forward",
    )(info, kinds, masked, *feats, table, *(pinned(w) for w in (frame, patch, w_qkv, w_out)))


def weight_copies(w_up, w_down, ups, downs, sems, c):
    step = downs.shape[0] // 4
    at = pl.ds(c * step, step)
    return (
        pltpu.make_async_copy(w_up.at[:, at], ups.at[:, at], sems.at[0, c]),
        pltpu.make_async_copy(w_down.at[at], downs.at[at], sems.at[1, c]),
    )


def feed_forward_kernel(size, info, normed, middle, table, b_up, w_up, w_down, *refs):
    dy_pieces, (out, slopes, dy, send, keep, ups, downs, sems) = refs[:size], refs[size:]
    first = is_first_core(info)
    step = downs.shape[0] // 4
    for c in range(4):
        for copy in weight_copies(w_up, w_down, ups, downs, sems, c):
            copy.start()
    dy[...] = stacked(dy_pieces)
    total = middle[...] + table[DOWN_BIAS : DOWN_BIAS + 1, :]
    half = step // 4
    for c in range(4):
        cols = slice(c * step, (c + 1) * step)
        for copy in weight_copies(w_up, w_down, ups, downs, sems, c):
            copy.wait()
        hidden = mm(normed[...], ups[:, cols]) + b_up[:, cols]
        phi = 0.5 * (1.0 + lax.erf(hidden * 0.7071067811865476))
        slopes[:, cols] = (phi + hidden * jnp.exp(-0.5 * hidden * hidden) * 0.3989422804014327).astype(BF16)
        active = (hidden * phi).astype(BF16)
        total = total + mm(active, downs[cols])
        down_g = mm(active.T, dy[...]).astype(BF16)
        for i in range(2):
            even = down_g[i * half : (i + 1) * half]
            odd = down_g[(2 + i) * half : (3 + i) * half]
            place = pl.ds(place_of(info, c, i == 0), 1)
            keep[i, place] = jnp.where(first, even, odd)[None]
            send[i, place] = jnp.where(first, odd, even)[None]
    out[...] = total.astype(BF16)


def feed_back_kernel(info, normed_t, dy, slopes, w_up, w_down, grad_n, send, keep, up_b, ups, downs, sems):
    first = is_first_core(info)
    step = downs.shape[0] // 4
    for c in range(4):
        for copy in weight_copies(w_up, w_down, ups, downs, sems, c):
            copy.start()
    grad = None
    rows = normed_t.shape[0] // 8
    for c in range(4):
        cols = slice(c * step, (c + 1) * step)
        for copy in weight_copies(w_up, w_down, ups, downs, sems, c):
            copy.wait()
        low = (mm_nt(dy[...], downs[cols]) * slopes[:, cols].astype(F32)).astype(BF16)
        up_b[:, cols] = jnp.sum(low.astype(F32), axis=0, keepdims=True)
        up_g = mm(normed_t[...], low).astype(BF16)
        at = (c % 2) * rows
        for chip in range(4):
            even = up_g[2 * chip * rows : (2 * chip + 1) * rows]
            odd = up_g[(2 * chip + 1) * rows : (2 * chip + 2) * rows]
            place = pl.ds(place_of(info, chip, c < 2), 1)
            keep[c // 2, place, at : at + rows, :] = jnp.where(first, even, odd)[None]
            send[c // 2, place, at : at + rows, :] = jnp.where(first, odd, even)[None]
        more = mm_nt(low, ups[:, cols])
        grad = more if grad is None else grad + more
    grad_n[...] = grad


def feed_scratch(d, ff):
    return [pltpu.VMEM((d, ff), BF16), pltpu.VMEM((ff, d), BF16), pltpu.SemaphoreType.DMA((2, 4))]


def feed_forward_call(info, normed, middle, table, b_up, w_up, w_down, dy):
    t, d = normed.shape
    ff = w_up.shape[1]
    vmem = pl.BlockSpec(memory_space=pltpu.VMEM)
    held = jax.ShapeDtypeStruct((2, 4, ff // 16, d), BF16)
    return pl.pallas_call(
        functools.partial(feed_forward_kernel, len(dy)),
        in_specs=[SMEM] + [vmem] * 4 + [HBM] * 2 + [vmem] * len(dy),
        out_shape=[
            jax.ShapeDtypeStruct((t, d), BF16),
            jax.ShapeDtypeStruct((t, ff), BF16),
            jax.ShapeDtypeStruct((t, d), BF16),
            held,
            held,
        ],
        scratch_shapes=feed_scratch(d, ff),
        compiler_params=pltpu.CompilerParams(vmem_limit_bytes=FEED_MIB * MIB),
        cost_estimate=pl.CostEstimate(flops=6 * t * d * ff, bytes_accessed=18 * MIB, transcendentals=2 * t * ff),
        name="feed_forward",
    )(info, normed, middle, table, b_up, pinned(w_up), pinned(w_down), *dy)


def feed_back_call(info, normed_t, dy, slopes, w_up, w_down):
    d, t = normed_t.shape
    ff = w_up.shape[1]
    vmem = pl.BlockSpec(memory_space=pltpu.VMEM)
    held = jax.ShapeDtypeStruct((2, 4, 2 * d // 8, ff // 4), BF16)
    return pl.pallas_call(
        feed_back_kernel,
        in_specs=[SMEM] + [vmem] * 3 + [HBM] * 2,
        out_shape=[
            jax.ShapeDtypeStruct((t, d), F32),
            held,
            held,
            jax.ShapeDtypeStruct((1, ff), F32),
        ],
        scratch_shapes=feed_scratch(d, ff),
        compiler_params=pltpu.CompilerParams(vmem_limit_bytes=FEED_MIB * MIB),
        cost_estimate=pl.CostEstimate(flops=6 * t * d * ff, bytes_accessed=18 * MIB, transcendentals=0),
        name="feed_back",
    )(info, normed_t, dy, slopes, pinned(w_up), pinned(w_down))


def middle_kernel_fast(info, grad_n, middle, dy, att_t, table, w_out, grad_mid, grad_att, send, keep, sums, w, sem):
    copy = pltpu.make_async_copy(w_out, w, sem)
    copy.start()
    centred, inverse = norm_stats(middle[...])
    grad = grad_n[...]
    dy_f = dy[...].astype(F32)
    mid = dy_f + norm_back(grad, centred, inverse, table[GAIN_TWO : GAIN_TWO + 1, :])
    grad_mid[...] = mid.astype(BF16)
    low = mid.astype(BF16)
    sums[...] = jnp.concatenate(
        [
            jnp.sum(low.astype(F32), axis=0, keepdims=True),
            jnp.sum(grad * centred, axis=0, keepdims=True),
            jnp.sum(grad, axis=0, keepdims=True),
            jnp.sum(dy_f, axis=0, keepdims=True),
            jnp.zeros((4, mid.shape[1]), F32),
        ],
        axis=0,
    )
    out_g = mm(att_t[...], low).astype(BF16)
    spread(out_g, out_g.shape[0] // 8, 0, send, keep, info, True)
    copy.wait()
    grad_att[...] = mm_nt(low, w[...]).astype(BF16)


def middle_call_fast(info, grad_n, middle, dy, att_t, table, w_out):
    t, d = middle.shape
    vmem = pl.BlockSpec(memory_space=pltpu.VMEM)
    held = jax.ShapeDtypeStruct((4, d // 8, d), BF16)
    return pl.pallas_call(
        middle_kernel_fast,
        in_specs=[SMEM] + [vmem] * 5 + [HBM],
        out_shape=[
            jax.ShapeDtypeStruct((t, d), BF16),
            jax.ShapeDtypeStruct((t, d), BF16),
            held,
            held,
            jax.ShapeDtypeStruct((8, d), F32),
        ],
        scratch_shapes=[pltpu.VMEM((d, d), BF16), pltpu.SemaphoreType.DMA],
        compiler_params=pltpu.CompilerParams(vmem_limit_bytes=OTHER_MIB * MIB),
        cost_estimate=pl.CostEstimate(flops=4 * t * d * d, bytes_accessed=10 * MIB, transcendentals=0),
        name="middle",
    )(info, grad_n, middle, dy, att_t, table, pinned(w_out))


def back_group(group, qkv, probs, grad_a, normed_t, w_qkv, w, sems):
    d = w.shape[0]
    copies = [
        pltpu.make_async_copy(
            w_qkv.at[:, pl.ds(i * d + group * LANES, LANES)], w.at[:, pl.ds(i * LANES, LANES)], sems.at[i]
        )
        for i in range(3)
    ]
    for copy in copies:
        copy.start()
    q, k, v = (qkv[:, i * LANES : (i + 1) * LANES] for i in range(3))
    k_t = k.T
    dq_t, dks, dvs = [], [], []
    for pair in range(2):
        lanes = slice(pair * PAIR, (pair + 1) * PAIR)
        qp, vp, gp = q[:, lanes], v[:, lanes], grad_a[:, lanes]
        dk = dv = None
        for h in range(2):
            low = probs[2 * pair + h]
            grad_h = half_of(gp, h)
            grad_p = mm_nt(vp, grad_h)
            wide = low.astype(F32)
            inner = jnp.sum(wide * grad_p, axis=0, keepdims=True)
            grad_s = (wide * (grad_p - inner)).astype(BF16)
            dv_h = mm(low, grad_h)
            dk_h = mm(grad_s, half_of(qp, h))
            dv = dv_h if dv is None else dv + dv_h
            dk = dk_h if dk is None else dk + dk_h
            head = 2 * pair + h
            dq_t.append(mm(k_t[head * HEAD_DIM : (head + 1) * HEAD_DIM, :], grad_s))
        dks.append(dk.astype(BF16))
        dvs.append(dv.astype(BF16))
    dq = (jnp.concatenate(dq_t, axis=0) * SCALE).astype(BF16).T
    grads = jnp.concatenate([dq] + dks + dvs, axis=1)
    sums = jnp.sum(grads.astype(F32), axis=0, keepdims=True)
    weight_grad = mm(normed_t[...], grads).astype(BF16)
    for copy in copies:
        copy.wait()
    return weight_grad, mm_nt(grads, w[...]), sums


def back_kernel_fast(group, info, qkv, probs, grad_a, normed_t, w_qkv, *refs):
    opens = group == 0
    if not opens:
        grad_in, send_o, keep_o, send_a, keep_a, *refs = refs
    grad_n, sums, send, keep, w, sems = refs
    g, grad, total = back_group(group, qkv, probs, grad_a, normed_t, w_qkv, w, sems)
    grad_n[...] = grad if opens else grad_in[...] + grad
    sums[...] = total
    if opens:
        spread(g, g.shape[0] // 8, 0, send, keep, info, False)
    else:
        rows = g.shape[0] // 8
        for ref, one, two in ((send, send_o, send_a), (keep, keep_o, keep_a)):
            ref[0, :, :rows] = one[...]
            ref[1, :, :rows] = two[...]
        spread_halves(g, rows, send, keep, info)


def back_specs(t, d, group):
    return [
        SMEM,
        whole((t, 3 * LANES)),
        whole((4, t, t)),
        pl.BlockSpec((t, LANES), lambda s: (0, group)),
        whole((d, t)),
        HBM,
    ]


def back_scratch(d):
    return [pltpu.VMEM((d, 3 * LANES), BF16), pltpu.SemaphoreType.DMA((3,))]


def back_call_fast(info, qkv, probs, grad_att, normed_t, w_qkv, group, carried):
    t, d = grad_att.shape
    held = (4, d // 8, d) if group == 0 else (2, 4, 3 * d // 16, d)
    return pl.pallas_call(
        functools.partial(back_kernel_fast, group),
        grid=(1,),
        in_specs=back_specs(t, d, group) + [whole(a.shape) for a in carried],
        out_specs=[whole((t, d)), whole((1, d)), whole(held), whole(held)],
        out_shape=[
            jax.ShapeDtypeStruct((t, d), F32),
            jax.ShapeDtypeStruct((1, d), F32),
            jax.ShapeDtypeStruct(held, BF16),
            jax.ShapeDtypeStruct(held, BF16),
        ],
        scratch_shapes=back_scratch(d),
        compiler_params=pltpu.CompilerParams(vmem_limit_bytes=OTHER_MIB * MIB),
        cost_estimate=pl.CostEstimate(flops=2 * t * d * (16 * t + 6 * d) // 3, bytes_accessed=9 * MIB, transcendentals=0),
        name="back",
    )(info, qkv, probs, grad_att, normed_t, pinned(w_qkv), *carried)


def last_kernel_fast(
    size, rows, group, info, qkv, probs, grad_a, normed_t, w_qkv, grad_in, kinds, masked, hat, inverse_t, grad_mid, *refs
):
    feats_t, frame, patch, table, sums_two, sums_a, sums_b, *refs = refs
    up_b, feats_g, send, keep, w, sems = refs
    g, grad, sums_c = back_group(group, qkv, probs, grad_a, normed_t, w_qkv, w, sems)
    d = g.shape[0]
    half = d // 16
    (send_x, send_y), (keep_x, keep_y) = ((r.at[0], r.at[1]) for r in (send, keep))
    spread_halves(g, 0, send, keep, info)
    grad = grad_in[...] + grad
    centred, inverse = hat[...].astype(F32), inverse_t[:, :1]
    total = grad_mid[...].astype(F32) + norm_back(grad, centred, inverse, table[GAIN_ONE : GAIN_ONE + 1, :])
    is_masked = clip_mask(info, masked, size, rows)
    low = jnp.where(is_masked, 0.0, total).astype(BF16)
    is_patch = kinds[info[0]] == 1
    chosen = jnp.where(is_patch, patch[...], frame[...])
    feats_g[...] = mm_nt(low, chosen).astype(BF16)
    g = mm(feats_t[...], low).astype(BF16)
    none = jnp.zeros_like(g)
    b = g.shape[0] // 8
    spread(jnp.where(is_patch, none, g), b, half, send_x, keep_x, info, True)
    spread(jnp.where(is_patch, g, none), b, half, send_y, keep_y, info, False)
    for ref in (send_y, keep_y):
        ref[:, half + b :, :] = jnp.zeros((4, 16, d), BF16)
    sums = [sums_a[...], sums_b[...], sums_c]
    vectors = jnp.concatenate(
        [
            jnp.sum(jnp.where(is_masked, total, 0.0), axis=0, keepdims=True),
            jnp.sum(grad * centred, axis=0, keepdims=True),
            jnp.sum(grad, axis=0, keepdims=True),
            jnp.concatenate([s[:, :LANES] for s in sums], axis=1),
            jnp.concatenate([s[:, 2 * LANES :] for s in sums], axis=1),
            sums_two[0:4, :],
            jnp.zeros((7, d), F32),
        ],
        axis=0,
    )
    width = d // 8
    wide = up_b.shape[1] // 8
    blocks = []
    for r in range(8):
        rolled = vectors if r == 0 else pltpu.roll(vectors, d - r * width, 1)
        up = jnp.concatenate([up_b[:, r * wide : (r + 1) * wide], jnp.zeros((1, d - wide), F32)], axis=1)
        blocks.append(jnp.concatenate([rolled[:9], up, jnp.zeros((6, d), F32)], axis=0))
    spread(jnp.concatenate(blocks, axis=0).astype(BF16), 16, half + b, send_x, keep_x, info, True)


def last_call_fast(
    info, qkv, probs, grad_att, normed_t, w_qkv, carried, kinds, masked, hat, inverse_t, grad_mid, feats_t, frame, patch, table,
    sums_two, sums_a, sums_b, up_b, size, rows,
):
    t, d = grad_att.shape
    f = frame.shape[0]
    held = (2, 4, d // 16 + f // 8 + 16, d)
    more = (masked, hat, inverse_t, grad_mid, feats_t, frame, patch, table, sums_two, sums_a, sums_b, up_b)
    group = d // LANES - 1
    return pl.pallas_call(
        functools.partial(last_kernel_fast, size, rows, group),
        grid=(1,),
        in_specs=back_specs(t, d, group) + [whole(carried.shape), SMEM] + [whole(a.shape) for a in more],
        out_specs=[whole((t, f)), whole(held), whole(held)],
        out_shape=[
            jax.ShapeDtypeStruct((t, f), BF16),
            jax.ShapeDtypeStruct(held, BF16),
            jax.ShapeDtypeStruct(held, BF16),
        ],
        scratch_shapes=back_scratch(d),
        compiler_params=pltpu.CompilerParams(vmem_limit_bytes=OTHER_MIB * MIB),
        cost_estimate=pl.CostEstimate(flops=2 * t * d * (16 * t + 6 * d) // 3, bytes_accessed=16 * MIB, transcendentals=0),
        name="last",
    )(info, qkv, probs, grad_att, normed_t, pinned(w_qkv), carried, kinds, *more)


def settle_kernel(one, two, down, up):
    down[...] = one[...].astype(F32)
    b = up.shape[0]
    for c in range(4):
        up[:, c * two.shape[1] : (c + 1) * two.shape[1]] = two[c * b : (c + 1) * b].astype(F32)


def settle(one, two, b):
    d = one.shape[1]
    vmem = pl.BlockSpec(memory_space=pltpu.VMEM)
    return pl.pallas_call(
        settle_kernel,
        in_specs=[vmem] * 2,
        out_shape=[jax.ShapeDtypeStruct(one.shape, F32), jax.ShapeDtypeStruct((b, 4 * d), F32)],
        cost_estimate=pl.CostEstimate(flops=0, bytes_accessed=6 * MIB, transcendentals=0),
        compiler_params=pltpu.CompilerParams(vmem_limit_bytes=8 * MIB),
        name="settle",
    )(one, two)


def settle_last_kernel(za, zb, out_g, qkv_g, frame_g, patch_g, vec):
    b, d = out_g.shape
    fr = frame_g.shape[0]
    one, two = za[...].astype(F32), zb[...].astype(F32)
    x1, y1 = one[: one.shape[0] // 2], one[one.shape[0] // 2 :]
    x2, y2 = two[: two.shape[0] // 2], two[two.shape[0] // 2 :]
    out_g[...] = x1[:b]
    half = b // 2
    groups = (y1[:b],), (x1[b:], y1[b:]), (x2[:half], y2[:half])
    for s, pieces in enumerate(groups):
        at = 0
        for value in pieces:
            for i in range(3):
                lane = i * d + s * LANES
                qkv_g[at : at + value.shape[0], lane : lane + LANES] = value[:, i * LANES : (i + 1) * LANES]
            at += value.shape[0]
    frame_g[...] = x2[half : half + fr]
    patch_g[...] = y2[half : half + fr]
    vec[...] = x2[half + fr :]


def settle_last(za, zb, b, fr):
    d = za.shape[1]
    vmem = pl.BlockSpec(memory_space=pltpu.VMEM)
    return pl.pallas_call(
        settle_last_kernel,
        in_specs=[vmem] * 2,
        out_shape=[
            jax.ShapeDtypeStruct((b, d), F32),
            jax.ShapeDtypeStruct((b, 3 * d), F32),
            jax.ShapeDtypeStruct((fr, d), F32),
            jax.ShapeDtypeStruct((fr, d), F32),
            jax.ShapeDtypeStruct((16, d), F32),
        ],
        cost_estimate=pl.CostEstimate(flops=0, bytes_accessed=4 * MIB, transcendentals=0),
        compiler_params=pltpu.CompilerParams(vmem_limit_bytes=8 * MIB),
        name="settle_last",
    )(za, zb)


def place_kernel(size, info, *refs):
    out = refs[size]
    for i in range(size):

        @pl.when(pl.program_id(0) == i)
        def _():
            out[0] = refs[i][...]


def place(info, pieces):
    size = len(pieces)
    shape = pieces[0].shape
    return pl.pallas_call(
        functools.partial(place_kernel, size),
        grid_spec=pltpu.PrefetchScalarGridSpec(
            num_scalar_prefetch=1,
            grid=(size,),
            in_specs=[pl.BlockSpec(shape, lambda i, info: (0, 0))] * size,
            out_specs=pl.BlockSpec((1,) + shape, lambda i, info: (jnp.bitwise_xor(info[0], i), 0, 0)),
        ),
        out_shape=jax.ShapeDtypeStruct((size,) + shape, pieces[0].dtype),
        cost_estimate=pl.CostEstimate(flops=0, bytes_accessed=4 * size * pieces[0].size, transcendentals=0),
        compiler_params=pltpu.CompilerParams(vmem_limit_bytes=8 * MIB),
        name="place",
    )(info, *pieces)


def swap(block, axis, size, flip):
    return lax.ppermute(block, axis, [(i, i ^ flip) for i in range(size)])


def to_clip(pieces, me, size):
    out = [lax.dynamic_index_in_dim(pieces, me, 0, keepdims=False)]
    for d in range(1, size):
        out.append(swap(lax.dynamic_index_in_dim(pieces, me ^ d, 0, keepdims=False), "seq", size, d))
    return jnp.concatenate(out, axis=0)


def to_pieces(clip_rows, me, size):
    rel = clip_rows.reshape(size, -1, clip_rows.shape[-1])
    got = [rel[0]] + [swap(rel[d], "seq", size, d) for d in range(1, size)]
    out = jnp.zeros_like(rel)
    for d in range(size):
        out = lax.dynamic_update_index_in_dim(out, got[d], me ^ d, 0)
    return out


def bits_of(n):
    return n.bit_length() - 1


def fold_clips(grad, order, n):
    count = bits_of(n)
    me = lax.axis_index("clips")
    rows, width = grad.shape
    held = grad.reshape((2,) * count + (rows // n, width))
    left = list(range(count - 1, -1, -1))
    for bit in order:
        axis = left.index(bit)
        mine = (me >> bit) & 1
        send = lax.dynamic_index_in_dim(held, 1 - mine, axis, keepdims=False)
        keep = lax.dynamic_index_in_dim(held, mine, axis, keepdims=False)
        held = keep + swap(send, "clips", n, 1 << bit)
        left.pop(axis)
    return held


def sum_seq(part, size):
    me = lax.axis_index("seq")
    count = bits_of(size)
    held = part
    for bit in range(count):
        half = held.shape[1] // 2
        mine = (me >> bit) & 1
        send = lax.dynamic_slice_in_dim(held, (1 - mine) * half, half, 1)
        keep = lax.dynamic_slice_in_dim(held, mine * half, half, 1)
        held = keep + swap(send, "seq", size, 1 << bit)
    for bit in reversed(range(count)):
        got = swap(held, "seq", size, 1 << bit)
        mine = (me >> bit) & 1
        held = jnp.where(
            mine == 0, jnp.concatenate([held, got], axis=1), jnp.concatenate([got, held], axis=1)
        )
    return held


def clip_orders(n):
    count = bits_of(n)
    low = [0] if count else []
    rest = list(range(1, count))
    return low + rest, low + rest[::-1]


def reduce_grad(grad, n, size):
    first, second = clip_orders(n)
    half = grad.shape[1] // 2
    a = fold_clips(grad[:, :half], first, n)
    b = fold_clips(grad[:, half:], second, n)
    return sum_seq(jnp.concatenate([a, b], axis=1), size).astype(F32)


FORWARD_MIB, FEED_MIB, OTHER_MIB = 20, 26, 14


def tie(*values):
    return lax.optimization_barrier(values)


def over(block, bit):
    return swap(block, "clips", 8, 1 << bit)


def hop(block, pairs):
    return lax.ppermute(block, "seq", pairs)


INWARD, ACROSS, OUTWARD = [(0, 1), (3, 2)], [(1, 2), (2, 1)], [(1, 0), (2, 3)]
NEAR, FAR = [(i, i ^ 1) for i in range(4)], [(i, i ^ 2) for i in range(4)]


def add(*terms):
    total = terms[0].astype(F32)
    for term in terms[1:]:
        total = total + term.astype(F32)
    return total.astype(BF16)


class Item:
    def __init__(self, send, keep):
        self.keep = keep
        self.got = over(send, 0)

    def first(self):
        self.rest = [add(self.keep[i, :2], self.got[i, :2]) for i in range(2)]
        return [add(self.keep[i, 2:], self.got[i, 2:]) for i in range(2)]

    def send_first(self, parts):
        self.one = (over(parts[0], 1), over(parts[1], 2))

    def second(self):
        self.mine = [add(self.rest[i][0], self.one[i][0]) for i in range(2)]
        return [add(self.rest[i][1], self.one[i][1]) for i in range(2)]

    def send_second(self, parts):
        self.two = (over(parts[0], 2), over(parts[1], 1))

    def line(self):
        return jnp.concatenate([add(self.mine[i], self.two[i]) for i in range(2)], axis=0)


def fast_path(features, clip_kind, masked_positions, weights, cotangent):
    (
        frame_proj,
        patch_proj,
        mask_embed,
        norm1_gain,
        norm1_bias,
        w_qkv,
        q_bias,
        v_bias,
        w_out,
        out_bias,
        norm2_gain,
        norm2_bias,
        w_up,
        up_bias,
        w_down,
        down_bias,
    ) = weights
    size = 4
    me = lax.axis_index("seq")
    rows = features.shape[1]
    d = w_out.shape[0]

    def from_pieces(array):
        mine = [lax.dynamic_index_in_dim(array, me ^ i, 0, keepdims=False) for i in range(size)]
        return [mine[0]] + [swap(mine[i], "seq", size, i) for i in range(1, size)]

    def to_owners(array):
        rel = array.reshape(size, rows, -1)
        return [rel[0]] + [swap(rel[i], "seq", size, i) for i in range(1, size)]

    info = jnp.stack([me, lax.axis_index("clips")])
    outer = (me == 0) | (me == 3)
    features, info, outer = tie(features, info, outer)
    feats = from_pieces(features)
    dy = from_pieces(cotangent)
    zero = jnp.zeros_like(q_bias)
    table = jnp.stack(
        [q_bias, zero, v_bias, mask_embed, norm1_gain, norm1_bias, out_bias, norm2_gain, norm2_bias, down_bias]
        + [zero] * 6
    ).astype(F32)
    b_up = up_bias.astype(F32)[None, :]

    hat, inverse_t, normed_one_t, *groups, att_t, middle, normed_two, normed_two_t, feats_t = forward_call(
        info, clip_kind, masked_positions, feats, frame_proj, patch_proj, table, w_qkv, w_out, size, rows
    )
    output, slopes, dy, send, keep = feed_forward_call(info, normed_two, middle, table, b_up, w_up, w_down, dy)
    i1 = Item(send, keep)
    out_pieces = to_owners(output)
    p = i1.first()
    info, slopes, p, i1.rest = tie(info, slopes, p, i1.rest)
    i1.send_first(p)
    grad_n2, send, keep, up_b = feed_back_call(info, normed_two_t, dy, slopes, w_up, w_down)

    info, send, grad_n2, out_pieces, i1.one = tie(info, send, grad_n2, out_pieces, i1.one)
    i1.send_second(i1.second())
    i2 = Item(send, keep)
    grad_mid, grad_att, send_o, keep_o, sums_two = middle_call_fast(info, grad_n2, middle, dy, att_t, table, w_out)
    p = i2.first()
    info, grad_att, p, i2.rest, i1.two = tie(info, grad_att, p, i2.rest, i1.two)
    i2.send_first(p)
    z1 = i1.line()
    got1 = hop(z1, INWARD)
    grad_a, sums_a, send_a, keep_a = back_call_fast(info, groups[0], groups[3], grad_att, normed_one_t, w_qkv, 0, ())
    grad_b, sums_b, send, keep = back_call_fast(
        info, groups[1], groups[4], grad_att, normed_one_t, w_qkv, 1, (grad_a, send_o, keep_o, send_a, keep_a)
    )

    info, send, i2.one, got1 = tie(info, send, i2.one, got1)
    i4 = Item(send, keep)
    i2.send_second(i2.second())
    z1 = add(z1, got1)
    got1 = hop(z1, ACROSS)
    p = i4.first()
    info, grad_b, p, i4.rest = tie(info, grad_b, p, i4.rest)
    i4.send_first(p)
    feats_grad, send, keep = last_call_fast(
        info, groups[2], groups[5], grad_att, normed_one_t, w_qkv, grad_b, clip_kind, masked_positions, hat, inverse_t,
        grad_mid, feats_t, frame_proj, patch_proj, table, sums_two, sums_a, sums_b, up_b, size, rows,
    )

    info, send, feats_grad, i2.two, got1 = tie(info, send, feats_grad, i2.two, got1)
    i5 = Item(send, keep)
    z2 = i2.line()
    z1 = add(z1, got1)
    both = hop(jnp.where(outer, z2, z1), INWARD + OUTWARD)
    p = i5.first()
    info, p, i5.rest, i4.one = tie(info, p, i5.rest, i4.one)
    i5.send_first(p)
    i4.send_second(i4.second())
    output = place(info, out_pieces)
    info, i4.two, output = tie(info, i4.two, output)
    z4 = i4.line()
    info, i5.one, both = tie(info, i5.one, both)
    i5.send_second(i5.second())
    z1 = jnp.where(outer, both, z1)
    z2 = jnp.where(outer, z2, add(z2, both))
    got2 = hop(z2, ACROSS)
    got4 = hop(z4, INWARD)
    info, i5.two, got2, got4 = tie(info, i5.two, got2, got4)
    z5 = i5.line()
    got5 = hop(z5, NEAR)
    z4 = add(z4, got4)
    got4 = hop(z4, ACROSS)
    z2 = add(z2, got2)
    got2 = hop(z2, OUTWARD)
    info, feats_grad, got4, got5 = tie(info, feats_grad, got4, got5)
    z4 = add(z4, got4)
    got4 = hop(z4, OUTWARD)
    z5 = add(z5, got5)
    got5 = hop(z5, FAR)
    feat_pieces = to_owners(feats_grad)
    info, got2, feat_pieces = tie(info, got2, feat_pieces)
    down_grad, up_grad = settle(z1, jnp.where(outer, got2, z2), d // 8)
    features_grad = place(info, feat_pieces)
    info, features_grad, down_grad, got4, got5 = tie(info, features_grad, down_grad, got4, got5)
    out_grad, qkv_grad, frame_grad, patch_grad, vec = settle_last(
        jnp.where(outer, got4, z4), add(z5, got5), d // 8, frame_proj.shape[0] // 8
    )
    b = d // 8
    return (
        output,
        features_grad,
        frame_grad,
        patch_grad,
        vec[0, :b],
        vec[1, :b],
        vec[2, :b],
        qkv_grad,
        vec[3, :b],
        vec[4, :b],
        out_grad,
        vec[5, :b],
        vec[6, :b],
        vec[7, :b],
        up_grad,
        vec[9, : up_bias.shape[0] // 8],
        down_grad,
        vec[8, :b],
    )


def body(
    features,
    clip_kind,
    masked_positions,
    frame_proj,
    patch_proj,
    mask_embed,
    norm1_gain,
    norm1_bias,
    w_qkv,
    q_bias,
    v_bias,
    w_out,
    out_bias,
    norm2_gain,
    norm2_bias,
    w_up,
    up_bias,
    w_down,
    down_bias,
    cotangent,
):
    n = lax.axis_size("clips")
    size = lax.axis_size("seq")
    me = lax.axis_index("seq")
    clips_here, rows, _ = features.shape
    assert clips_here == size
    d = w_out.shape[0]
    if n == 8 and size == 4:
        weights = (
            frame_proj,
            patch_proj,
            mask_embed,
            norm1_gain,
            norm1_bias,
            w_qkv,
            q_bias,
            v_bias,
            w_out,
            out_bias,
            norm2_gain,
            norm2_bias,
            w_up,
            up_bias,
            w_down,
            down_bias,
        )
        return fast_path(features, clip_kind, masked_positions, weights, cotangent)

    feats = to_clip(features, me, size)
    dy = to_clip(cotangent, me, size)
    kind = lax.dynamic_index_in_dim(clip_kind, me, 0, keepdims=False)
    info = jnp.stack([me, kind])
    masked = lax.dynamic_index_in_dim(masked_positions, me, 0, keepdims=True)
    zero = jnp.zeros_like(q_bias)
    table = jnp.stack(
        [q_bias, zero, v_bias, mask_embed, norm1_gain, norm1_bias, out_bias, norm2_gain, norm2_bias, down_bias]
        + [zero] * 6
    ).astype(F32)
    b_up = up_bias.astype(F32)[None, :]

    start, normed_one_t, qkv = embed_call(info, masked, feats, frame_proj, patch_proj, table, w_qkv, size, rows)
    probs, att_t, middle, normed_two, normed_two_t = attend_call(qkv, start, table, w_out)
    output, grad_n2, down_grad, up_grad, up_b = feed_call(
        normed_two, normed_two_t, dy, middle, table, w_up, b_up, w_down, 512
    )
    down_grad = reduce_grad(down_grad, n, size)
    up_grad = reduce_grad(up_grad, n, size)
    output = to_pieces(output, me, size)
    grad_mid, grad_att, out_grad, sums_two = middle_call(grad_n2, middle, dy, att_t, table, w_out)
    out_grad = reduce_grad(out_grad, n, size)
    gq, gk, gv, grad_n1, sums_qkv = back_call(qkv, probs, grad_att, normed_one_t, w_qkv)
    qkv_grad = reduce_grad(jnp.concatenate([gq, gk, gv], axis=1), n, size)
    feats_grad, chosen_grad, sums_one = last_call(
        info, masked, grad_n1, start, grad_mid, feats, frame_proj, patch_proj, table, size, rows
    )
    features_grad = to_pieces(feats_grad, me, size)

    vectors = (
        sums_one[0],
        sums_one[1],
        sums_one[2],
        sums_qkv[:, 0, :PAIR].reshape(-1),
        sums_qkv[:, 0, 2 * PAIR :].reshape(-1),
        sums_two[0],
        sums_two[1],
        sums_two[2],
        up_b[0],
        sums_two[3],
    )
    flat = jnp.concatenate([v.reshape(n, -1) for v in vectors], axis=1)
    feat_rows = frame_proj.shape[0] // n
    lanes = -(-flat.shape[1] // (feat_rows * 128)) * 128
    small = jnp.pad(flat, ((0, 0), (0, feat_rows * lanes - flat.shape[1])))
    small = small.reshape(n * feat_rows, lanes).astype(BF16)
    none = jnp.zeros_like(chosen_grad)
    is_patch = kind == 1
    last = jnp.concatenate(
        [jnp.where(is_patch, none, chosen_grad), jnp.where(is_patch, chosen_grad, none), small], axis=1
    )
    last = sum_seq(fold_clips(last, clip_orders(n)[0], n), size).astype(F32)
    frame_grad = last[:, :d]
    patch_grad = last[:, d : 2 * d]
    flat = last[:, 2 * d :].reshape(-1)
    small_out = []
    at = 0
    for v in vectors:
        small_out.append(flat[at : at + v.shape[0] // n])
        at += v.shape[0] // n
    (
        mask_out,
        gain1_out,
        bias1_out,
        q_out,
        v_out,
        outb_out,
        gain2_out,
        bias2_out,
        upb_out,
        downb_out,
    ) = small_out
    return (
        output,
        features_grad,
        frame_grad,
        patch_grad,
        mask_out,
        gain1_out,
        bias1_out,
        qkv_grad,
        q_out,
        v_out,
        out_grad,
        outb_out,
        gain2_out,
        bias2_out,
        up_grad,
        upb_out,
        down_grad,
        downb_out,
    )


def solution(mesh):
    tokens = P("clips", "seq", None)
    rows = P("clips", None)
    vec = P("clips")
    return jax.shard_map(
        body,
        mesh=mesh,
        in_specs=(tokens, P("clips"), rows) + (P(),) * 16 + (tokens,),
        out_specs=(tokens, tokens, rows, rows, vec, vec, vec, rows, vec, vec, rows, vec, vec, vec, rows, vec, rows, vec),
        check_vma=False,
    )
```

```python
import functools

import jax
import jax.numpy as jnp
from jax import lax
from jax.experimental import pallas as pl
from jax.experimental.pallas import tpu as pltpu
from jax.sharding import PartitionSpec as P

HEADS = 12
HEAD_DIM = 64
EPSILON = 1e-06
F32 = jnp.float32
BF16 = jnp.bfloat16
MIB = 1 << 20
SCALE = HEAD_DIM ** (-0.5)
Q_BIAS, NO_BIAS, V_BIAS, MASK_EMBED, GAIN_ONE, BIAS_ONE, OUT_BIAS, GAIN_TWO, BIAS_TWO, DOWN_BIAS = range(10)
PAIR = 2 * HEAD_DIM


def norm_stats(values_in):
    centre = values_in - jnp.mean(values_in, axis=-1, keepdims=True)
    inverse = lax.rsqrt(jnp.mean(centre * centre, axis=-1, keepdims=True) + EPSILON)
    return (centre * inverse, inverse)


def norm_back(grad_normed, centred, inverse, gain):
    scaled = grad_normed * gain
    return inverse * (
        scaled
        - jnp.mean(scaled, axis=-1, keepdims=True)
        - centred * jnp.mean(scaled * centred, axis=-1, keepdims=True)
    )


def mm(a, b):
    return jnp.dot(a, b, preferred_element_type=F32)


def mm_nt(a, b):
    return lax.dot_general(a, b, (((1,), (1,)), ((), ())), preferred_element_type=F32)


def whole(shape):
    return pl.BlockSpec(shape, lambda *_: (0,) * len(shape))


def masked_column(place, masked_ref, size, rows):
    marks = masked_ref[...]
    cols = []
    for d in range(size):
        spot = (place ^ d) * rows + lax.broadcasted_iota(jnp.int32, (rows, marks.shape[1]), 0)
        cols.append(jnp.max(jnp.where(spot == marks, 1.0, 0.0), axis=1, keepdims=True))
    return jnp.concatenate(cols, axis=0) > 0.5


def half_of(pair_block, h):
    lane = lax.broadcasted_iota(jnp.int32, pair_block.shape, 1)
    inside = (lane < HEAD_DIM) if h == 0 else (lane >= HEAD_DIM)
    return jnp.where(inside, pair_block, jnp.zeros_like(pair_block))


def embed_kernel(size, rows, info, masked, feats, frame, patch, table, w, start, normed_t, qkv, normed):
    j = pl.program_id(0)

    @pl.when(j == 0)
    def _():
        chosen = jnp.where(info[1] == 1, patch[...], frame[...])
        embedded = mm(feats[...], chosen)
        is_masked = masked_column(info[0], masked, size, rows)
        start_now = jnp.where(is_masked, table[MASK_EMBED : MASK_EMBED + 1, :], embedded)
        start[...] = start_now
        centred, _inv = norm_stats(start_now)
        out = (centred * table[GAIN_ONE : GAIN_ONE + 1, :] + table[BIAS_ONE : BIAS_ONE + 1, :]).astype(BF16)
        normed[...] = out
        normed_t[...] = out.T

    projected = mm(normed[...], w[...]) + table[pl.ds(j, 1), :]
    qkv[...] = (projected * jnp.where(j == 0, SCALE, 1.0)).astype(BF16)


def embed_call(info, masked, feats, frame, patch, table, w_qkv, size, rows):
    t, f = feats.shape
    d = frame.shape[1]
    smem = pl.BlockSpec(memory_space=pltpu.SMEM)
    return pl.pallas_call(
        functools.partial(embed_kernel, size, rows),
        grid=(3,),
        in_specs=[
            smem,
            whole(masked.shape),
            whole((t, f)),
            whole((f, d)),
            whole((f, d)),
            whole(table.shape),
            pl.BlockSpec((d, d), lambda j: (0, j)),
        ],
        out_specs=[whole((t, d)), whole((d, t)), pl.BlockSpec((t, d), lambda j: (0, j))],
        out_shape=[
            jax.ShapeDtypeStruct((t, d), F32),
            jax.ShapeDtypeStruct((d, t), BF16),
            jax.ShapeDtypeStruct((t, 3 * d), BF16),
        ],
        scratch_shapes=[pltpu.VMEM((t, d), BF16)],
        compiler_params=pltpu.CompilerParams(vmem_limit_bytes=40 * MIB),
        cost_estimate=pl.CostEstimate(flops=2 * t * d * (f + 3 * d), bytes_accessed=12 * MIB, transcendentals=0),
        name="embed",
    )(info, masked, feats, frame, patch, table, w_qkv)


def attend_kernel(q, k, v, start, table, w_out, probs, att_t, middle, normed, normed_t, att):
    p = pl.program_id(0)
    v_t = v[...].T
    parts = []
    for h in range(2):
        scores = mm_nt(k[...], half_of(q[...], h))
        top = jnp.max(scores, axis=0, keepdims=True)
        e = jnp.exp(scores - top)
        total = jnp.sum(e, axis=0, keepdims=True)
        low = (e * (1.0 / total)).astype(BF16)
        probs[h] = low
        parts.append(mm(v_t[h * HEAD_DIM : (h + 1) * HEAD_DIM, :], low))
    out_t = jnp.concatenate(parts, axis=0)
    att_t[...] = out_t.astype(BF16)
    att[:, pl.ds(pl.multiple_of(p * PAIR, PAIR), PAIR)] = out_t.T.astype(BF16)

    @pl.when(p == pl.num_programs(0) - 1)
    def _():
        mid = start[...] + mm(att[...], w_out[...]) + table[OUT_BIAS : OUT_BIAS + 1, :]
        middle[...] = mid
        centred, _inv = norm_stats(mid)
        out = (centred * table[GAIN_TWO : GAIN_TWO + 1, :] + table[BIAS_TWO : BIAS_TWO + 1, :]).astype(BF16)
        normed[...] = out
        normed_t[...] = out.T


def attend_call(qkv, start, table, w_out):
    t, d = start.shape
    pairs = HEADS // 2

    def block(base):
        return pl.BlockSpec((t, PAIR), lambda p: (0, base + p))

    return pl.pallas_call(
        attend_kernel,
        grid=(pairs,),
        in_specs=[
            block(0),
            block(pairs),
            block(2 * pairs),
            whole((t, d)),
            whole(table.shape),
            whole((d, d)),
        ],
        out_specs=[
            pl.BlockSpec((2, t, t), lambda p: (p, 0, 0)),
            pl.BlockSpec((PAIR, t), lambda p: (p, 0)),
            whole((t, d)),
            whole((t, d)),
            whole((d, t)),
        ],
        out_shape=[
            jax.ShapeDtypeStruct((HEADS, t, t), BF16),
            jax.ShapeDtypeStruct((d, t), BF16),
            jax.ShapeDtypeStruct((t, d), F32),
            jax.ShapeDtypeStruct((t, d), BF16),
            jax.ShapeDtypeStruct((d, t), BF16),
        ],
        scratch_shapes=[pltpu.VMEM((t, d), BF16)],
        compiler_params=pltpu.CompilerParams(vmem_limit_bytes=40 * MIB),
        cost_estimate=pl.CostEstimate(
            flops=2 * t * d * (8 * t + d), bytes_accessed=20 * MIB, transcendentals=HEADS * t * t
        ),
        name="attend",
    )(qkv, qkv, qkv, start, table, w_out)


def feed_kernel(normed, normed_t, dy, middle, table, w_up, b_up, w_down, out, grad_n, down_g, up_g, up_b, total):
    c = pl.program_id(0)

    @pl.when(c == 0)
    def _():
        total[...] = middle[...] + table[DOWN_BIAS : DOWN_BIAS + 1, :]
        grad_n[...] = jnp.zeros_like(grad_n)

    hidden = mm(normed[...], w_up[...]) + b_up[...]
    phi = 0.5 * (1.0 + lax.erf(hidden * 0.7071067811865476))
    slope = phi + hidden * jnp.exp(-0.5 * hidden * hidden) * 0.3989422804014327
    active = (hidden * phi).astype(BF16)
    total[...] += mm(active, w_down[...])
    down_g[...] = mm(active.T, dy[...]).astype(BF16)
    grad_h = mm_nt(dy[...], w_down[...]) * slope
    low = grad_h.astype(BF16)
    up_b[...] = jnp.sum(low.astype(F32), axis=0, keepdims=True)
    up_g[...] = mm(normed_t[...], low).astype(BF16)
    grad_n[...] += mm_nt(low, w_up[...])

    @pl.when(c == pl.num_programs(0) - 1)
    def _():
        out[...] = total[...].astype(BF16)


def feed_call(normed, normed_t, dy, middle, table, w_up, b_up, w_down, step):
    t, d = normed.shape
    ff = w_up.shape[1]
    return pl.pallas_call(
        feed_kernel,
        grid=(ff // step,),
        in_specs=[
            whole((t, d)),
            whole((d, t)),
            whole((t, d)),
            whole((t, d)),
            whole(table.shape),
            pl.BlockSpec((d, step), lambda c: (0, c)),
            pl.BlockSpec((1, step), lambda c: (0, c)),
            pl.BlockSpec((step, d), lambda c: (c, 0)),
        ],
        out_specs=[
            whole((t, d)),
            whole((t, d)),
            pl.BlockSpec((step, d), lambda c: (c, 0)),
            pl.BlockSpec((d, step), lambda c: (0, c)),
            pl.BlockSpec((1, step), lambda c: (0, c)),
        ],
        out_shape=[
            jax.ShapeDtypeStruct((t, d), BF16),
            jax.ShapeDtypeStruct((t, d), F32),
            jax.ShapeDtypeStruct((ff, d), BF16),
            jax.ShapeDtypeStruct((d, ff), BF16),
            jax.ShapeDtypeStruct((1, ff), F32),
        ],
        scratch_shapes=[pltpu.VMEM((t, d), F32)],
        compiler_params=pltpu.CompilerParams(vmem_limit_bytes=44 * MIB),
        cost_estimate=pl.CostEstimate(flops=12 * t * d * ff, bytes_accessed=26 * MIB, transcendentals=2 * t * ff),
        name="feed",
    )(normed, normed_t, dy, middle, table, w_up, b_up, w_down)


def middle_kernel(grad_n, middle, dy, att_t, table, w_out, grad_mid, grad_att, out_g, sums):
    centred, inverse = norm_stats(middle[...])
    grad = grad_n[...]
    dy_f = dy[...].astype(F32)
    mid = dy_f + norm_back(grad, centred, inverse, table[GAIN_TWO : GAIN_TWO + 1, :])
    grad_mid[...] = mid
    low = mid.astype(BF16)
    sums[...] = jnp.concatenate(
        [
            jnp.sum(low.astype(F32), axis=0, keepdims=True),
            jnp.sum(grad * centred, axis=0, keepdims=True),
            jnp.sum(grad, axis=0, keepdims=True),
            jnp.sum(dy_f, axis=0, keepdims=True),
            jnp.zeros((4, mid.shape[1]), F32),
        ],
        axis=0,
    )
    grad_att[...] = mm_nt(low, w_out[...]).astype(BF16)
    out_g[...] = mm(att_t[...], low).astype(BF16)


def middle_call(grad_n, middle, dy, att_t, table, w_out):
    t, d = middle.shape
    return pl.pallas_call(
        middle_kernel,
        out_shape=[
            jax.ShapeDtypeStruct((t, d), F32),
            jax.ShapeDtypeStruct((t, d), BF16),
            jax.ShapeDtypeStruct((d, d), BF16),
            jax.ShapeDtypeStruct((8, d), F32),
        ],
        compiler_params=pltpu.CompilerParams(vmem_limit_bytes=40 * MIB),
        cost_estimate=pl.CostEstimate(flops=4 * t * d * d, bytes_accessed=10 * MIB, transcendentals=0),
        name="middle",
    )(grad_n, middle, dy, att_t, table, w_out)


def back_kernel(q, k, v, probs, grad_a, normed_t, wq, wk, wv, gq, gk, gv, grad_n, sums):
    p = pl.program_id(0)

    @pl.when(p == 0)
    def _():
        grad_n[...] = jnp.zeros_like(grad_n)

    k_t = k[...].T
    dk = dv = None
    dq_t = []
    for h in range(2):
        low = probs[h]
        grad_h = half_of(grad_a[...], h)
        grad_p = mm_nt(v[...], grad_h)
        wide = low.astype(F32)
        inner = jnp.sum(wide * grad_p, axis=0, keepdims=True)
        grad_s = (wide * (grad_p - inner)).astype(BF16)
        dv_h = mm(low, grad_h)
        dk_h = mm(grad_s, half_of(q[...], h))
        dv = dv_h if dv is None else dv + dv_h
        dk = dk_h if dk is None else dk + dk_h
        dq_t.append(mm(k_t[h * HEAD_DIM : (h + 1) * HEAD_DIM, :], grad_s))
    dq = (jnp.concatenate(dq_t, axis=0).T * SCALE).astype(BF16)
    grads = jnp.concatenate([dq, dk.astype(BF16), dv.astype(BF16)], axis=1)
    weights = jnp.concatenate([wq[...], wk[...], wv[...]], axis=1)
    sums[...] = jnp.sum(grads.astype(F32), axis=0, keepdims=True)[None]
    g = mm(normed_t[...], grads).astype(BF16)
    gq[...] = g[:, :PAIR]
    gk[...] = g[:, PAIR : 2 * PAIR]
    gv[...] = g[:, 2 * PAIR :]
    grad_n[...] += mm_nt(grads, weights)


def back_call(qkv, probs, grad_att, normed_t, w_qkv):
    t, d = grad_att.shape
    pairs = HEADS // 2

    def block(rows, base):
        return pl.BlockSpec((rows, PAIR), lambda p: (0, base + p))

    return pl.pallas_call(
        back_kernel,
        grid=(pairs,),
        in_specs=[
            block(t, 0),
            block(t, pairs),
            block(t, 2 * pairs),
            pl.BlockSpec((2, t, t), lambda p: (p, 0, 0)),
            block(t, 0),
            whole((d, t)),
            block(d, 0),
            block(d, pairs),
            block(d, 2 * pairs),
        ],
        out_specs=[
            block(d, 0),
            block(d, 0),
            block(d, 0),
            whole((t, d)),
            pl.BlockSpec((1, 1, 3 * PAIR), lambda p: (p, 0, 0)),
        ],
        out_shape=[jax.ShapeDtypeStruct((d, d), BF16)] * 3
        + [jax.ShapeDtypeStruct((t, d), F32), jax.ShapeDtypeStruct((pairs, 1, 3 * PAIR), F32)],
        compiler_params=pltpu.CompilerParams(vmem_limit_bytes=40 * MIB),
        cost_estimate=pl.CostEstimate(flops=2 * t * d * (16 * t + 6 * d), bytes_accessed=24 * MIB, transcendentals=0),
        name="back",
    )(qkv, qkv, qkv, probs, grad_att, normed_t, w_qkv, w_qkv, w_qkv)


def last_kernel(size, rows, info, masked, grad_n, start, grad_mid, feats, frame, patch, table, feats_g, chosen_g, sums):
    centred, inverse = norm_stats(start[...])
    grad = grad_n[...]
    total = grad_mid[...] + norm_back(grad, centred, inverse, table[GAIN_ONE : GAIN_ONE + 1, :])
    is_masked = masked_column(info[0], masked, size, rows)
    kept = jnp.where(is_masked, 0.0, total)
    sums[...] = jnp.concatenate(
        [
            jnp.sum(jnp.where(is_masked, total, 0.0), axis=0, keepdims=True),
            jnp.sum(grad * centred, axis=0, keepdims=True),
            jnp.sum(grad, axis=0, keepdims=True),
            jnp.zeros((5, total.shape[1]), F32),
        ],
        axis=0,
    )
    low = kept.astype(BF16)
    chosen = jnp.where(info[1] == 1, patch[...], frame[...])
    feats_g[...] = mm_nt(low, chosen).astype(BF16)
    chosen_g[...] = mm(feats[...].T, low).astype(BF16)


def last_call(info, masked, grad_n, start, grad_mid, feats, frame, patch, table, size, rows):
    t, d = start.shape
    f = feats.shape[1]
    vmem = pl.BlockSpec(memory_space=pltpu.VMEM)
    return pl.pallas_call(
        functools.partial(last_kernel, size, rows),
        in_specs=[pl.BlockSpec(memory_space=pltpu.SMEM)] + [vmem] * 8,
        out_shape=[
            jax.ShapeDtypeStruct((t, f), BF16),
            jax.ShapeDtypeStruct((f, d), BF16),
            jax.ShapeDtypeStruct((8, d), F32),
        ],
        compiler_params=pltpu.CompilerParams(vmem_limit_bytes=40 * MIB),
        cost_estimate=pl.CostEstimate(flops=4 * t * d * f, bytes_accessed=6 * MIB, transcendentals=0),
        name="last",
    )(info, masked, grad_n, start, grad_mid, feats, frame, patch, table)


LANES = 256
SEGMENT = 128
SMEM = pl.BlockSpec(memory_space=pltpu.SMEM)
HBM = pl.BlockSpec(memory_space=pltpu.HBM)


def pinned(array):
    return pltpu.with_memory_space_constraint(array, pltpu.HBM)


def place_of(info, chip, x_first):
    rel = jnp.bitwise_xor(chip, info[1] // 2)
    return (rel % 2) * 2 + rel // 2 if x_first else rel


def is_first_core(info):
    return info[1] % 2 == 0


def spread(value, rows, at, send, keep, info, x_first):
    first = is_first_core(info)
    for chip in range(4):
        even = value[2 * chip * rows : (2 * chip + 1) * rows]
        odd = value[(2 * chip + 1) * rows : (2 * chip + 2) * rows]
        place = place_of(info, chip, x_first)
        keep[pl.ds(place, 1), at : at + rows, :] = jnp.where(first, even, odd)[None]
        send[pl.ds(place, 1), at : at + rows, :] = jnp.where(first, odd, even)[None]


def spread_halves(value, at, send, keep, info):
    first = is_first_core(info)
    rows = value.shape[0] // 8
    half = rows // 2
    for i in range(2):
        for chip in range(4):
            begin = 2 * chip * rows + i * half
            even, odd = value[begin : begin + half], value[begin + rows : begin + rows + half]
            place = pl.ds(place_of(info, chip, i == 0), 1)
            keep[i, place, at : at + half, :] = jnp.where(first, even, odd)[None]
            send[i, place, at : at + half, :] = jnp.where(first, odd, even)[None]


def stacked(refs):
    return jnp.concatenate([r[...] for r in refs], axis=0)


def clip_mask(info, masked, size, rows):
    return masked_column(info[0], masked.at[pl.ds(info[0], 1)], size, rows)


def forward_kernel(
    size, rows, info, kinds, masked, *refs,
):
    feats, refs = refs[:size], refs[size:]
    (
        table, frame, patch, w_qkv, w_out,
        hat, inverse_t, normed_t, qkv_a, qkv_b, qkv_c, probs_a, probs_b, probs_c, att_t,
        middle, normed_two, normed_two_t, feats_t,
        start, normed, att, projs, w_in, w_back, sems,
    ) = refs
    qkvs, all_probs = (qkv_a, qkv_b, qkv_c), (probs_a, probs_b, probs_c)
    d = att.shape[1]
    third = d // LANES

    def weight_copy(group, i):
        cols = pl.ds(i * d + group * LANES, LANES)
        return pltpu.make_async_copy(w_qkv.at[:, cols], w_in.at[group, :, pl.ds(i * LANES, LANES)], sems.at[group, i])

    proj_copies = [pltpu.make_async_copy(p, projs.at[i], sems.at[third, i]) for i, p in enumerate((frame, patch))]
    out_copy = pltpu.make_async_copy(w_out, w_back, sems.at[third, 2])
    for copy in proj_copies:
        copy.start()
    for group in range(third):
        for i in range(3):
            weight_copy(group, i).start()
    out_copy.start()
    is_masked = clip_mask(info, masked, size, rows)
    features = stacked(feats)
    feats_t[...] = features.T
    for copy in proj_copies:
        copy.wait()
    chosen = jnp.where(kinds[info[0]] == 1, projs[1], projs[0])
    start_now = jnp.where(is_masked, table[MASK_EMBED : MASK_EMBED + 1, :], mm(features, chosen))
    start[...] = start_now
    centred, inverse = norm_stats(start_now)
    hat[...] = centred.astype(BF16)
    inverse_t[...] = jnp.broadcast_to(inverse, inverse_t.shape)
    out = (centred * table[GAIN_ONE : GAIN_ONE + 1, :] + table[BIAS_ONE : BIAS_ONE + 1, :]).astype(BF16)
    normed[...] = out
    normed_t[...] = out.T
    for group in range(third):
        for i in range(3):
            weight_copy(group, i).wait()
    out_copy.wait()

    def project(group):
        lanes = slice(group * LANES, (group + 1) * LANES)
        projected = mm(normed[...], w_in[group])
        q = ((projected[:, :LANES] + table[Q_BIAS : Q_BIAS + 1, lanes]) * SCALE).astype(BF16)
        k = projected[:, LANES : 2 * LANES].astype(BF16)
        v = (projected[:, 2 * LANES :] + table[V_BIAS : V_BIAS + 1, lanes]).astype(BF16)
        for i, value in enumerate((q, k, v)):
            qkvs[group][:, i * LANES : (i + 1) * LANES] = value
        return q, k, v.T

    def scores_of(h):
        q, k, _v = held[h // 4]
        pair = slice((h % 4 // 2) * PAIR, (h % 4 // 2 + 1) * PAIR)
        return mm_nt(k[:, pair], half_of(q[:, pair], h % 2))

    held = {0: project(0)}
    upcoming = scores_of(0)
    parts = []
    for h in range(HEADS):
        group = h // 4
        scores = upcoming
        if h % 4 == 2 and group + 1 < third:
            held[group + 1] = project(group + 1)
        if h + 1 < HEADS:
            upcoming = scores_of(h + 1)
        top = jnp.max(scores, axis=0, keepdims=True)
        e = jnp.exp(scores - top)
        total = jnp.sum(e, axis=0, keepdims=True)
        low = (e * (1.0 / total)).astype(BF16)
        all_probs[group][h % 4] = low
        v_t = held[group][2]
        parts.append(mm(v_t[h % 4 * HEAD_DIM : (h % 4 + 1) * HEAD_DIM, :], low))
        if h % 4 == 3:
            out_t = jnp.concatenate(parts, axis=0).astype(BF16)
            parts = []
            lanes = slice(group * LANES, (group + 1) * LANES)
            att_t[lanes, :] = out_t
            att[:, lanes] = out_t.T
    mid = start[...] + mm(att[...], w_back[...]) + table[OUT_BIAS : OUT_BIAS + 1, :]
    middle[...] = mid
    centred, _inv = norm_stats(mid)
    out = (centred * table[GAIN_TWO : GAIN_TWO + 1, :] + table[BIAS_TWO : BIAS_TWO + 1, :]).astype(BF16)
    normed_two[...] = out
    normed_two_t[...] = out.T


def forward_call(info, kinds, masked, feats, frame, patch, table, w_qkv, w_out, size, rows):
    f, d = frame.shape
    t = size * rows
    third = d // LANES
    return pl.pallas_call(
        functools.partial(forward_kernel, size, rows),
        in_specs=[SMEM, SMEM] + [pl.BlockSpec(memory_space=pltpu.VMEM)] * (size + 2) + [HBM] * 4,
        out_shape=[
            jax.ShapeDtypeStruct((t, d), BF16),
            jax.ShapeDtypeStruct((t, 128), F32),
            jax.ShapeDtypeStruct((d, t), BF16),
            *([jax.ShapeDtypeStruct((t, 3 * LANES), BF16)] * third),
            *([jax.ShapeDtypeStruct((4, t, t), BF16)] * third),
            jax.ShapeDtypeStruct((d, t), BF16),
            jax.ShapeDtypeStruct((t, d), F32),
            jax.ShapeDtypeStruct((t, d), BF16),
            jax.ShapeDtypeStruct((d, t), BF16),
            jax.ShapeDtypeStruct((f, t), BF16),
        ],
        scratch_shapes=[
            pltpu.VMEM((t, d), F32),
            pltpu.VMEM((t, d), BF16),
            pltpu.VMEM((t, d), BF16),
            pltpu.VMEM((2, f, d), BF16),
            pltpu.VMEM((third, d, 3 * LANES), BF16),
            pltpu.VMEM((d, d), BF16),
            pltpu.SemaphoreType.DMA((third + 1, 3)),
        ],
        compiler_params=pltpu.CompilerParams(vmem_limit_bytes=FORWARD_MIB * MIB),
        cost_estimate=pl.CostEstimate(
            flops=2 * t * d * (f + 4 * d + 8 * t), bytes_accessed=24 * MIB, transcendentals=HEADS * t * t
        ),
        name="forward",
    )(info, kinds, masked, *feats, table, *(pinned(w) for w in (frame, patch, w_qkv, w_out)))


def feed_forward_kernel(info, normed, middle, table, b_up, w_up, w_down, out, actives, slopes, ups, downs, sems):
    step = downs.shape[0] // 4

    def copies(c):
        at = pl.ds(c * step, step)
        return (
            pltpu.make_async_copy(w_up.at[:, at], ups.at[:, at], sems.at[0, c]),
            pltpu.make_async_copy(w_down.at[at], downs.at[at], sems.at[1, c]),
        )

    for c in range(4):
        for copy in copies(c):
            copy.start()

    def before(c):
        cols = slice(c * step, (c + 1) * step)
        for copy in copies(c):
            copy.wait()
        return mm(normed[...], ups[:, cols]) + b_up[:, cols]

    total = middle[...] + table[DOWN_BIAS : DOWN_BIAS + 1, :]
    upcoming = before(0)
    for c in range(4):
        cols = slice(c * step, (c + 1) * step)
        hidden = upcoming
        if c < 3:
            upcoming = before(c + 1)
        phi = 0.5 * (1.0 + lax.erf(hidden * 0.7071067811865476))
        slopes[:, cols] = (phi + hidden * jnp.exp(-0.5 * hidden * hidden) * 0.3989422804014327).astype(BF16)
        active = (hidden * phi).astype(BF16)
        actives[:, cols] = active
        total = total + mm(active, downs[cols])
    out[...] = total.astype(BF16)


def down_kernel(size, info, actives, *refs):
    dy_pieces, (dy, send, keep) = refs[:size], refs[size:]
    first = is_first_core(info)
    step = actives.shape[1] // 4
    half = step // 4
    grad_rows = stacked(dy_pieces)
    dy[...] = grad_rows
    for c in range(4):
        down_g = mm(actives[:, c * step : (c + 1) * step].T, grad_rows).astype(BF16)
        for i in range(2):
            even = down_g[i * half : (i + 1) * half]
            odd = down_g[(2 + i) * half : (3 + i) * half]
            place = pl.ds(place_of(info, c, i == 0), 1)
            keep[i, place] = jnp.where(first, even, odd)[None]
            send[i, place] = jnp.where(first, odd, even)[None]


def feed_back_kernel(info, normed_t, dy, slopes, ups, downs, grad_n, send, keep, up_b):
    first = is_first_core(info)
    step = downs.shape[0] // 4
    rows = normed_t.shape[0] // 8
    grad_n[...] = jnp.zeros_like(grad_n)

    @pl.loop(0, 4)
    def _(c):
        cols = pl.ds(pl.multiple_of(c * step, step), step)
        low = (mm_nt(dy[...], downs[cols, :]) * slopes[:, cols].astype(F32)).astype(BF16)
        up_b[:, cols] = jnp.sum(low.astype(F32), axis=0, keepdims=True)
        up_g = mm(normed_t[...], low).astype(BF16)
        at = pl.ds(pl.multiple_of((c % 2) * rows, rows), rows)
        for chip in range(4):
            even = up_g[2 * chip * rows : (2 * chip + 1) * rows]
            odd = up_g[(2 * chip + 1) * rows : (2 * chip + 2) * rows]
            place = jnp.where(c < 2, place_of(info, chip, True), place_of(info, chip, False))
            where = (pl.ds(c // 2, 1), pl.ds(place, 1), at)
            keep[where] = jnp.where(first, even, odd)[None, None]
            send[where] = jnp.where(first, odd, even)[None, None]
        grad_n[...] += mm_nt(low, ups[:, cols])


VMEM = pl.BlockSpec(memory_space=pltpu.VMEM)


def feed_forward_call(info, normed, middle, table, b_up, w_up, w_down):
    t, d = normed.shape
    ff = w_up.shape[1]
    return pl.pallas_call(
        feed_forward_kernel,
        in_specs=[SMEM] + [VMEM] * 4 + [HBM] * 2,
        out_shape=[
            jax.ShapeDtypeStruct((t, d), BF16),
            jax.ShapeDtypeStruct((t, ff), BF16),
            jax.ShapeDtypeStruct((t, ff), BF16),
            jax.ShapeDtypeStruct((d, ff), BF16),
            jax.ShapeDtypeStruct((ff, d), BF16),
        ],
        scratch_shapes=[pltpu.SemaphoreType.DMA((2, 4))],
        compiler_params=pltpu.CompilerParams(vmem_limit_bytes=FEED_MIB * MIB),
        cost_estimate=pl.CostEstimate(flops=4 * t * d * ff, bytes_accessed=18 * MIB, transcendentals=2 * t * ff),
        name="feed_forward",
    )(info, normed, middle, table, b_up, pinned(w_up), pinned(w_down))


def down_call(info, actives, dy):
    t, ff = actives.shape
    d = dy[0].shape[1]
    held = jax.ShapeDtypeStruct((2, 4, ff // 16, d), BF16)
    return pl.pallas_call(
        functools.partial(down_kernel, len(dy)),
        in_specs=[SMEM] + [VMEM] * (1 + len(dy)),
        out_shape=[jax.ShapeDtypeStruct((t, d), BF16), held, held],
        compiler_params=pltpu.CompilerParams(vmem_limit_bytes=FEED_MIB * MIB),
        cost_estimate=pl.CostEstimate(flops=2 * t * d * ff, bytes_accessed=9 * MIB, transcendentals=0),
        name="down",
    )(info, actives, *dy)


def feed_back_call(info, normed_t, dy, slopes, ups, downs):
    d, t = normed_t.shape
    ff = ups.shape[1]
    held = jax.ShapeDtypeStruct((2, 4, 2 * d // 8, ff // 4), BF16)
    return pl.pallas_call(
        feed_back_kernel,
        in_specs=[SMEM] + [VMEM] * 5,
        out_shape=[
            jax.ShapeDtypeStruct((t, d), F32),
            held,
            held,
            jax.ShapeDtypeStruct((1, ff), F32),
        ],
        compiler_params=pltpu.CompilerParams(vmem_limit_bytes=FEED_MIB * MIB),
        cost_estimate=pl.CostEstimate(flops=6 * t * d * ff, bytes_accessed=18 * MIB, transcendentals=0),
        name="feed_back",
    )(info, normed_t, dy, slopes, ups, downs)


def middle_kernel_fast(info, grad_n, middle, dy, att_t, table, w_out, grad_mid, grad_att, send, keep, sums, w, sem):
    copy = pltpu.make_async_copy(w_out, w, sem)
    copy.start()
    centred, inverse = norm_stats(middle[...])
    grad = grad_n[...]
    dy_f = dy[...].astype(F32)
    mid = dy_f + norm_back(grad, centred, inverse, table[GAIN_TWO : GAIN_TWO + 1, :])
    grad_mid[...] = mid.astype(BF16)
    low = mid.astype(BF16)
    sums[...] = jnp.concatenate(
        [
            jnp.sum(low.astype(F32), axis=0, keepdims=True),
            jnp.sum(grad * centred, axis=0, keepdims=True),
            jnp.sum(grad, axis=0, keepdims=True),
            jnp.sum(dy_f, axis=0, keepdims=True),
            jnp.zeros((4, mid.shape[1]), F32),
        ],
        axis=0,
    )
    out_g = mm(att_t[...], low).astype(BF16)
    spread(out_g, out_g.shape[0] // 8, 0, send, keep, info, True)
    copy.wait()
    grad_att[...] = mm_nt(low, w[...]).astype(BF16)


def middle_call_fast(info, grad_n, middle, dy, att_t, table, w_out):
    t, d = middle.shape
    vmem = pl.BlockSpec(memory_space=pltpu.VMEM)
    held = jax.ShapeDtypeStruct((4, d // 8, d), BF16)
    return pl.pallas_call(
        middle_kernel_fast,
        in_specs=[SMEM] + [vmem] * 5 + [HBM],
        out_shape=[
            jax.ShapeDtypeStruct((t, d), BF16),
            jax.ShapeDtypeStruct((t, d), BF16),
            held,
            held,
            jax.ShapeDtypeStruct((8, d), F32),
        ],
        scratch_shapes=[pltpu.VMEM((d, d), BF16), pltpu.SemaphoreType.DMA],
        compiler_params=pltpu.CompilerParams(vmem_limit_bytes=OTHER_MIB * MIB),
        cost_estimate=pl.CostEstimate(flops=4 * t * d * d, bytes_accessed=10 * MIB, transcendentals=0),
        name="middle",
    )(info, grad_n, middle, dy, att_t, table, pinned(w_out))


def back_group(group, qkv, probs, grad_a, normed_t, w_qkv, w, sems):
    d = w.shape[0]
    copies = [
        pltpu.make_async_copy(
            w_qkv.at[:, pl.ds(i * d + group * LANES, LANES)], w.at[:, pl.ds(i * LANES, LANES)], sems.at[i]
        )
        for i in range(3)
    ]
    for copy in copies:
        copy.start()
    q, k, v = (qkv[:, i * LANES : (i + 1) * LANES] for i in range(3))
    k_t = k.T
    dq_t, dks, dvs = [], [], []
    for pair in range(2):
        lanes = slice(pair * PAIR, (pair + 1) * PAIR)
        qp, vp, gp = q[:, lanes], v[:, lanes], grad_a[:, lanes]
        dk = dv = None
        for h in range(2):
            low = probs[2 * pair + h]
            grad_h = half_of(gp, h)
            grad_p = mm_nt(vp, grad_h)
            wide = low.astype(F32)
            inner = jnp.sum(wide * grad_p, axis=0, keepdims=True)
            grad_s = (wide * (grad_p - inner)).astype(BF16)
            dv_h = mm(low, grad_h)
            dk_h = mm(grad_s, half_of(qp, h))
            dv = dv_h if dv is None else dv + dv_h
            dk = dk_h if dk is None else dk + dk_h
            head = 2 * pair + h
            dq_t.append(mm(k_t[head * HEAD_DIM : (head + 1) * HEAD_DIM, :], grad_s))
        dks.append(dk.astype(BF16))
        dvs.append(dv.astype(BF16))
    dq = (jnp.concatenate(dq_t, axis=0) * SCALE).astype(BF16).T
    grads = jnp.concatenate([dq] + dks + dvs, axis=1)
    sums = jnp.sum(grads.astype(F32), axis=0, keepdims=True)
    weight_grad = mm(normed_t[...], grads).astype(BF16)
    for copy in copies:
        copy.wait()
    return weight_grad, mm_nt(grads, w[...]), sums


def back_kernel_fast(group, info, qkv, probs, grad_a, normed_t, w_qkv, *refs):
    opens = group == 0
    if not opens:
        grad_in, send_o, keep_o, send_a, keep_a, *refs = refs
    grad_n, sums, send, keep, w, sems = refs
    g, grad, total = back_group(group, qkv, probs, grad_a, normed_t, w_qkv, w, sems)
    grad_n[...] = grad if opens else grad_in[...] + grad
    sums[...] = total
    if opens:
        spread(g, g.shape[0] // 8, 0, send, keep, info, False)
    else:
        rows = g.shape[0] // 8
        for ref, one, two in ((send, send_o, send_a), (keep, keep_o, keep_a)):
            ref[0, :, :rows] = one[...]
            ref[1, :, :rows] = two[...]
        spread_halves(g, rows, send, keep, info)


def back_specs(t, d, group):
    return [
        SMEM,
        whole((t, 3 * LANES)),
        whole((4, t, t)),
        pl.BlockSpec((t, LANES), lambda s: (0, group)),
        whole((d, t)),
        HBM,
    ]


def back_scratch(d):
    return [pltpu.VMEM((d, 3 * LANES), BF16), pltpu.SemaphoreType.DMA((3,))]


def back_call_fast(info, qkv, probs, grad_att, normed_t, w_qkv, group, carried):
    t, d = grad_att.shape
    held = (4, d // 8, d) if group == 0 else (2, 4, 3 * d // 16, d)
    return pl.pallas_call(
        functools.partial(back_kernel_fast, group),
        grid=(1,),
        in_specs=back_specs(t, d, group) + [whole(a.shape) for a in carried],
        out_specs=[whole((t, d)), whole((1, d)), whole(held), whole(held)],
        out_shape=[
            jax.ShapeDtypeStruct((t, d), F32),
            jax.ShapeDtypeStruct((1, d), F32),
            jax.ShapeDtypeStruct(held, BF16),
            jax.ShapeDtypeStruct(held, BF16),
        ],
        scratch_shapes=back_scratch(d),
        compiler_params=pltpu.CompilerParams(vmem_limit_bytes=OTHER_MIB * MIB),
        cost_estimate=pl.CostEstimate(flops=2 * t * d * (16 * t + 6 * d) // 3, bytes_accessed=9 * MIB, transcendentals=0),
        name="back",
    )(info, qkv, probs, grad_att, normed_t, pinned(w_qkv), *carried)


def last_kernel_fast(
    size, rows, group, info, qkv, probs, grad_a, normed_t, w_qkv, grad_in, kinds, masked, hat, inverse_t, grad_mid, *refs
):
    feats_t, frame, patch, table, sums_two, sums_a, sums_b, *refs = refs
    up_b, feats_g, send, keep, w, sems = refs
    g, grad, sums_c = back_group(group, qkv, probs, grad_a, normed_t, w_qkv, w, sems)
    d = g.shape[0]
    half = d // 16
    (send_x, send_y), (keep_x, keep_y) = ((r.at[0], r.at[1]) for r in (send, keep))
    spread_halves(g, 0, send, keep, info)
    grad = grad_in[...] + grad
    centred, inverse = hat[...].astype(F32), inverse_t[:, :1]
    total = grad_mid[...].astype(F32) + norm_back(grad, centred, inverse, table[GAIN_ONE : GAIN_ONE + 1, :])
    is_masked = clip_mask(info, masked, size, rows)
    low = jnp.where(is_masked, 0.0, total).astype(BF16)
    is_patch = kinds[info[0]] == 1
    chosen = jnp.where(is_patch, patch[...], frame[...])
    feats_g[...] = mm_nt(low, chosen).astype(BF16)
    g = mm(feats_t[...], low).astype(BF16)
    none = jnp.zeros_like(g)
    b = g.shape[0] // 8
    spread(jnp.where(is_patch, none, g), b, half, send_x, keep_x, info, True)
    spread(jnp.where(is_patch, g, none), b, half, send_y, keep_y, info, False)
    for ref in (send_y, keep_y):
        ref[:, half + b :, :] = jnp.zeros((4, 16, d), BF16)
    sums = [sums_a[...], sums_b[...], sums_c]
    vectors = jnp.concatenate(
        [
            jnp.sum(jnp.where(is_masked, total, 0.0), axis=0, keepdims=True),
            jnp.sum(grad * centred, axis=0, keepdims=True),
            jnp.sum(grad, axis=0, keepdims=True),
            jnp.concatenate([s[:, :LANES] for s in sums], axis=1),
            jnp.concatenate([s[:, 2 * LANES :] for s in sums], axis=1),
            sums_two[0:4, :],
            jnp.zeros((7, d), F32),
        ],
        axis=0,
    )
    width = d // 8
    wide = up_b.shape[1] // 8
    blocks = []
    for r in range(8):
        rolled = vectors if r == 0 else pltpu.roll(vectors, d - r * width, 1)
        up = jnp.concatenate([up_b[:, r * wide : (r + 1) * wide], jnp.zeros((1, d - wide), F32)], axis=1)
        blocks.append(jnp.concatenate([rolled[:9], up, jnp.zeros((6, d), F32)], axis=0))
    spread(jnp.concatenate(blocks, axis=0).astype(BF16), 16, half + b, send_x, keep_x, info, True)


def last_call_fast(
    info, qkv, probs, grad_att, normed_t, w_qkv, carried, kinds, masked, hat, inverse_t, grad_mid, feats_t, frame, patch, table,
    sums_two, sums_a, sums_b, up_b, size, rows,
):
    t, d = grad_att.shape
    f = frame.shape[0]
    held = (2, 4, d // 16 + f // 8 + 16, d)
    more = (masked, hat, inverse_t, grad_mid, feats_t, frame, patch, table, sums_two, sums_a, sums_b, up_b)
    group = d // LANES - 1
    return pl.pallas_call(
        functools.partial(last_kernel_fast, size, rows, group),
        grid=(1,),
        in_specs=back_specs(t, d, group) + [whole(carried.shape), SMEM] + [whole(a.shape) for a in more],
        out_specs=[whole((t, f)), whole(held), whole(held)],
        out_shape=[
            jax.ShapeDtypeStruct((t, f), BF16),
            jax.ShapeDtypeStruct(held, BF16),
            jax.ShapeDtypeStruct(held, BF16),
        ],
        scratch_shapes=back_scratch(d),
        compiler_params=pltpu.CompilerParams(vmem_limit_bytes=OTHER_MIB * MIB),
        cost_estimate=pl.CostEstimate(flops=2 * t * d * (16 * t + 6 * d) // 3, bytes_accessed=16 * MIB, transcendentals=0),
        name="last",
    )(info, qkv, probs, grad_att, normed_t, pinned(w_qkv), carried, kinds, *more)


def settle_kernel(one, two, down, up):
    down[...] = one[...].astype(F32)
    b = up.shape[0]
    for c in range(4):
        up[:, c * two.shape[1] : (c + 1) * two.shape[1]] = two[c * b : (c + 1) * b].astype(F32)


def settle(one, two, b):
    d = one.shape[1]
    vmem = pl.BlockSpec(memory_space=pltpu.VMEM)
    return pl.pallas_call(
        settle_kernel,
        in_specs=[vmem] * 2,
        out_shape=[jax.ShapeDtypeStruct(one.shape, F32), jax.ShapeDtypeStruct((b, 4 * d), F32)],
        cost_estimate=pl.CostEstimate(flops=0, bytes_accessed=6 * MIB, transcendentals=0),
        compiler_params=pltpu.CompilerParams(vmem_limit_bytes=8 * MIB),
        name="settle",
    )(one, two)


def settle_last_kernel(za, zb, out_g, qkv_g, frame_g, patch_g, vec):
    b, d = out_g.shape
    fr = frame_g.shape[0]
    one, two = za[...].astype(F32), zb[...].astype(F32)
    x1, y1 = one[: one.shape[0] // 2], one[one.shape[0] // 2 :]
    x2, y2 = two[: two.shape[0] // 2], two[two.shape[0] // 2 :]
    out_g[...] = x1[:b]
    half = b // 2
    groups = (y1[:b],), (x1[b:], y1[b:]), (x2[:half], y2[:half])
    for s, pieces in enumerate(groups):
        at = 0
        for value in pieces:
            for i in range(3):
                lane = i * d + s * LANES
                qkv_g[at : at + value.shape[0], lane : lane + LANES] = value[:, i * LANES : (i + 1) * LANES]
            at += value.shape[0]
    frame_g[...] = x2[half : half + fr]
    patch_g[...] = y2[half : half + fr]
    vec[...] = x2[half + fr :]


def settle_last(za, zb, b, fr):
    d = za.shape[1]
    vmem = pl.BlockSpec(memory_space=pltpu.VMEM)
    return pl.pallas_call(
        settle_last_kernel,
        in_specs=[vmem] * 2,
        out_shape=[
            jax.ShapeDtypeStruct((b, d), F32),
            jax.ShapeDtypeStruct((b, 3 * d), F32),
            jax.ShapeDtypeStruct((fr, d), F32),
            jax.ShapeDtypeStruct((fr, d), F32),
            jax.ShapeDtypeStruct((16, d), F32),
        ],
        cost_estimate=pl.CostEstimate(flops=0, bytes_accessed=4 * MIB, transcendentals=0),
        compiler_params=pltpu.CompilerParams(vmem_limit_bytes=8 * MIB),
        name="settle_last",
    )(za, zb)


def place_kernel(size, info, *refs):
    out = refs[size]
    for i in range(size):

        @pl.when(pl.program_id(0) == i)
        def _():
            out[0] = refs[i][...]


def place(info, pieces):
    size = len(pieces)
    shape = pieces[0].shape
    return pl.pallas_call(
        functools.partial(place_kernel, size),
        grid_spec=pltpu.PrefetchScalarGridSpec(
            num_scalar_prefetch=1,
            grid=(size,),
            in_specs=[pl.BlockSpec(shape, lambda i, info: (0, 0))] * size,
            out_specs=pl.BlockSpec((1,) + shape, lambda i, info: (jnp.bitwise_xor(info[0], i), 0, 0)),
        ),
        out_shape=jax.ShapeDtypeStruct((size,) + shape, pieces[0].dtype),
        cost_estimate=pl.CostEstimate(flops=0, bytes_accessed=4 * size * pieces[0].size, transcendentals=0),
        compiler_params=pltpu.CompilerParams(vmem_limit_bytes=8 * MIB),
        name="place",
    )(info, *pieces)


def swap(block, axis, size, flip):
    return lax.ppermute(block, axis, [(i, i ^ flip) for i in range(size)])


def to_clip(pieces, me, size):
    out = [lax.dynamic_index_in_dim(pieces, me, 0, keepdims=False)]
    for d in range(1, size):
        out.append(swap(lax.dynamic_index_in_dim(pieces, me ^ d, 0, keepdims=False), "seq", size, d))
    return jnp.concatenate(out, axis=0)


def to_pieces(clip_rows, me, size):
    rel = clip_rows.reshape(size, -1, clip_rows.shape[-1])
    got = [rel[0]] + [swap(rel[d], "seq", size, d) for d in range(1, size)]
    out = jnp.zeros_like(rel)
    for d in range(size):
        out = lax.dynamic_update_index_in_dim(out, got[d], me ^ d, 0)
    return out


def bits_of(n):
    return n.bit_length() - 1


def fold_clips(grad, order, n):
    count = bits_of(n)
    me = lax.axis_index("clips")
    rows, width = grad.shape
    held = grad.reshape((2,) * count + (rows // n, width))
    left = list(range(count - 1, -1, -1))
    for bit in order:
        axis = left.index(bit)
        mine = (me >> bit) & 1
        send = lax.dynamic_index_in_dim(held, 1 - mine, axis, keepdims=False)
        keep = lax.dynamic_index_in_dim(held, mine, axis, keepdims=False)
        held = keep + swap(send, "clips", n, 1 << bit)
        left.pop(axis)
    return held


def sum_seq(part, size):
    me = lax.axis_index("seq")
    count = bits_of(size)
    held = part
    for bit in range(count):
        half = held.shape[1] // 2
        mine = (me >> bit) & 1
        send = lax.dynamic_slice_in_dim(held, (1 - mine) * half, half, 1)
        keep = lax.dynamic_slice_in_dim(held, mine * half, half, 1)
        held = keep + swap(send, "seq", size, 1 << bit)
    for bit in reversed(range(count)):
        got = swap(held, "seq", size, 1 << bit)
        mine = (me >> bit) & 1
        held = jnp.where(
            mine == 0, jnp.concatenate([held, got], axis=1), jnp.concatenate([got, held], axis=1)
        )
    return held


def clip_orders(n):
    count = bits_of(n)
    low = [0] if count else []
    rest = list(range(1, count))
    return low + rest, low + rest[::-1]


def reduce_grad(grad, n, size):
    first, second = clip_orders(n)
    half = grad.shape[1] // 2
    a = fold_clips(grad[:, :half], first, n)
    b = fold_clips(grad[:, half:], second, n)
    return sum_seq(jnp.concatenate([a, b], axis=1), size).astype(F32)


FORWARD_MIB, FEED_MIB, OTHER_MIB = 20, 16, 14


def tie(*values):
    return lax.optimization_barrier(values)


def over(block, bit):
    return swap(block, "clips", 8, 1 << bit)


def hop(block, pairs):
    return lax.ppermute(block, "seq", pairs)


INWARD, ACROSS, OUTWARD = [(0, 1), (3, 2)], [(1, 2), (2, 1)], [(1, 0), (2, 3)]
NEAR, FAR = [(i, i ^ 1) for i in range(4)], [(i, i ^ 2) for i in range(4)]


def add(*terms):
    total = terms[0].astype(F32)
    for term in terms[1:]:
        total = total + term.astype(F32)
    return total.astype(BF16)


class Item:
    def __init__(self, send, keep):
        self.keep = keep
        self.got = over(send, 0)

    def first(self):
        self.rest = [add(self.keep[i, :2], self.got[i, :2]) for i in range(2)]
        return [add(self.keep[i, 2:], self.got[i, 2:]) for i in range(2)]

    def send_first(self, parts):
        self.one = (over(parts[0], 1), over(parts[1], 2))

    def second(self):
        self.mine = [add(self.rest[i][0], self.one[i][0]) for i in range(2)]
        return [add(self.rest[i][1], self.one[i][1]) for i in range(2)]

    def send_second(self, parts):
        self.two = (over(parts[0], 2), over(parts[1], 1))

    def line(self):
        return jnp.concatenate([add(self.mine[i], self.two[i]) for i in range(2)], axis=0)


def fast_path(features, clip_kind, masked_positions, weights, cotangent):
    (
        frame_proj,
        patch_proj,
        mask_embed,
        norm1_gain,
        norm1_bias,
        w_qkv,
        q_bias,
        v_bias,
        w_out,
        out_bias,
        norm2_gain,
        norm2_bias,
        w_up,
        up_bias,
        w_down,
        down_bias,
    ) = weights
    size = 4
    me = lax.axis_index("seq")
    rows = features.shape[1]
    d = w_out.shape[0]

    def from_pieces(array):
        mine = [lax.dynamic_index_in_dim(array, me ^ i, 0, keepdims=False) for i in range(size)]
        return [mine[0]] + [swap(mine[i], "seq", size, i) for i in range(1, size)]

    def to_owners(array):
        rel = array.reshape(size, rows, -1)
        return [rel[0]] + [swap(rel[i], "seq", size, i) for i in range(1, size)]

    info = jnp.stack([me, lax.axis_index("clips")])
    outer = (me == 0) | (me == 3)
    features, info, outer = tie(features, info, outer)
    feats = from_pieces(features)
    dy = from_pieces(cotangent)
    zero = jnp.zeros_like(q_bias)
    table = jnp.stack(
        [q_bias, zero, v_bias, mask_embed, norm1_gain, norm1_bias, out_bias, norm2_gain, norm2_bias, down_bias]
        + [zero] * 6
    ).astype(F32)
    b_up = up_bias.astype(F32)[None, :]

    hat, inverse_t, normed_one_t, *groups, att_t, middle, normed_two, normed_two_t, feats_t = forward_call(
        info, clip_kind, masked_positions, feats, frame_proj, patch_proj, table, w_qkv, w_out, size, rows
    )
    output, actives, slopes, ups, downs = feed_forward_call(info, normed_two, middle, table, b_up, w_up, w_down)
    dy, send, keep = down_call(info, actives, dy)
    i1 = Item(send, keep)
    out_pieces = to_owners(output)
    p = i1.first()
    info, slopes, p, i1.rest = tie(info, slopes, p, i1.rest)
    i1.send_first(p)
    grad_n2, send, keep, up_b = feed_back_call(info, normed_two_t, dy, slopes, ups, downs)

    info, send, grad_n2, out_pieces, i1.one = tie(info, send, grad_n2, out_pieces, i1.one)
    i1.send_second(i1.second())
    i2 = Item(send, keep)
    grad_mid, grad_att, send_o, keep_o, sums_two = middle_call_fast(info, grad_n2, middle, dy, att_t, table, w_out)
    p = i2.first()
    info, grad_att, p, i2.rest, i1.two = tie(info, grad_att, p, i2.rest, i1.two)
    i2.send_first(p)
    z1 = i1.line()
    got1 = hop(z1, INWARD)
    grad_a, sums_a, send_a, keep_a = back_call_fast(info, groups[0], groups[3], grad_att, normed_one_t, w_qkv, 0, ())
    grad_b, sums_b, send, keep = back_call_fast(
        info, groups[1], groups[4], grad_att, normed_one_t, w_qkv, 1, (grad_a, send_o, keep_o, send_a, keep_a)
    )

    info, send, i2.one, got1 = tie(info, send, i2.one, got1)
    i4 = Item(send, keep)
    i2.send_second(i2.second())
    z1 = add(z1, got1)
    got1 = hop(z1, ACROSS)
    p = i4.first()
    info, grad_b, p, i4.rest = tie(info, grad_b, p, i4.rest)
    i4.send_first(p)
    feats_grad, send, keep = last_call_fast(
        info, groups[2], groups[5], grad_att, normed_one_t, w_qkv, grad_b, clip_kind, masked_positions, hat, inverse_t,
        grad_mid, feats_t, frame_proj, patch_proj, table, sums_two, sums_a, sums_b, up_b, size, rows,
    )

    info, send, feats_grad, i2.two, i4.one, got1 = tie(info, send, feats_grad, i2.two, i4.one, got1)
    i5 = Item(send, keep)
    i4.send_second(i4.second())
    z2 = i2.line()
    z1 = add(z1, got1)
    both = hop(jnp.where(outer, z2, z1), INWARD + OUTWARD)
    p = i5.first()
    info, p, i5.rest = tie(info, p, i5.rest)
    i5.send_first(p)
    info, i4.two = tie(info, i4.two)
    z4 = i4.line()
    info, i5.one, both = tie(info, i5.one, both)
    i5.send_second(i5.second())
    z1 = jnp.where(outer, both, z1)
    z2 = jnp.where(outer, z2, add(z2, both))
    got2 = hop(z2, ACROSS)
    got4 = hop(z4, INWARD)
    output = place(info, out_pieces)
    info, i5.two = tie(info, i5.two)
    z5 = i5.line()
    got5 = hop(z5, NEAR)
    info, got2, got4, output = tie(info, got2, got4, output)
    z4 = add(z4, got4)
    got4 = hop(z4, ACROSS)
    z2 = add(z2, got2)
    got2 = hop(z2, OUTWARD)
    info, feats_grad, got5 = tie(info, feats_grad, got5)
    z5 = add(z5, got5)
    got5 = hop(z5, FAR)
    info, feats_grad, got4 = tie(info, feats_grad, got4)
    z4 = add(z4, got4)
    got4 = hop(z4, OUTWARD)
    feat_pieces = to_owners(feats_grad)
    info, got2, feat_pieces = tie(info, got2, feat_pieces)
    down_grad, up_grad = settle(z1, jnp.where(outer, got2, z2), d // 8)
    features_grad = place(info, feat_pieces)
    info, features_grad, down_grad, got4, got5 = tie(info, features_grad, down_grad, got4, got5)
    out_grad, qkv_grad, frame_grad, patch_grad, vec = settle_last(
        jnp.where(outer, got4, z4), add(z5, got5), d // 8, frame_proj.shape[0] // 8
    )
    b = d // 8
    return (
        output,
        features_grad,
        frame_grad,
        patch_grad,
        vec[0, :b],
        vec[1, :b],
        vec[2, :b],
        qkv_grad,
        vec[3, :b],
        vec[4, :b],
        out_grad,
        vec[5, :b],
        vec[6, :b],
        vec[7, :b],
        up_grad,
        vec[9, : up_bias.shape[0] // 8],
        down_grad,
        vec[8, :b],
    )


def body(
    features,
    clip_kind,
    masked_positions,
    frame_proj,
    patch_proj,
    mask_embed,
    norm1_gain,
    norm1_bias,
    w_qkv,
    q_bias,
    v_bias,
    w_out,
    out_bias,
    norm2_gain,
    norm2_bias,
    w_up,
    up_bias,
    w_down,
    down_bias,
    cotangent,
):
    n = lax.axis_size("clips")
    size = lax.axis_size("seq")
    me = lax.axis_index("seq")
    clips_here, rows, _ = features.shape
    assert clips_here == size
    d = w_out.shape[0]
    if n == 8 and size == 4:
        weights = (
            frame_proj,
            patch_proj,
            mask_embed,
            norm1_gain,
            norm1_bias,
            w_qkv,
            q_bias,
            v_bias,
            w_out,
            out_bias,
            norm2_gain,
            norm2_bias,
            w_up,
            up_bias,
            w_down,
            down_bias,
        )
        return fast_path(features, clip_kind, masked_positions, weights, cotangent)

    feats = to_clip(features, me, size)
    dy = to_clip(cotangent, me, size)
    kind = lax.dynamic_index_in_dim(clip_kind, me, 0, keepdims=False)
    info = jnp.stack([me, kind])
    masked = lax.dynamic_index_in_dim(masked_positions, me, 0, keepdims=True)
    zero = jnp.zeros_like(q_bias)
    table = jnp.stack(
        [q_bias, zero, v_bias, mask_embed, norm1_gain, norm1_bias, out_bias, norm2_gain, norm2_bias, down_bias]
        + [zero] * 6
    ).astype(F32)
    b_up = up_bias.astype(F32)[None, :]

    start, normed_one_t, qkv = embed_call(info, masked, feats, frame_proj, patch_proj, table, w_qkv, size, rows)
    probs, att_t, middle, normed_two, normed_two_t = attend_call(qkv, start, table, w_out)
    output, grad_n2, down_grad, up_grad, up_b = feed_call(
        normed_two, normed_two_t, dy, middle, table, w_up, b_up, w_down, 512
    )
    down_grad = reduce_grad(down_grad, n, size)
    up_grad = reduce_grad(up_grad, n, size)
    output = to_pieces(output, me, size)
    grad_mid, grad_att, out_grad, sums_two = middle_call(grad_n2, middle, dy, att_t, table, w_out)
    out_grad = reduce_grad(out_grad, n, size)
    gq, gk, gv, grad_n1, sums_qkv = back_call(qkv, probs, grad_att, normed_one_t, w_qkv)
    qkv_grad = reduce_grad(jnp.concatenate([gq, gk, gv], axis=1), n, size)
    feats_grad, chosen_grad, sums_one = last_call(
        info, masked, grad_n1, start, grad_mid, feats, frame_proj, patch_proj, table, size, rows
    )
    features_grad = to_pieces(feats_grad, me, size)

    vectors = (
        sums_one[0],
        sums_one[1],
        sums_one[2],
        sums_qkv[:, 0, :PAIR].reshape(-1),
        sums_qkv[:, 0, 2 * PAIR :].reshape(-1),
        sums_two[0],
        sums_two[1],
        sums_two[2],
        up_b[0],
        sums_two[3],
    )
    flat = jnp.concatenate([v.reshape(n, -1) for v in vectors], axis=1)
    feat_rows = frame_proj.shape[0] // n
    lanes = -(-flat.shape[1] // (feat_rows * 128)) * 128
    small = jnp.pad(flat, ((0, 0), (0, feat_rows * lanes - flat.shape[1])))
    small = small.reshape(n * feat_rows, lanes).astype(BF16)
    none = jnp.zeros_like(chosen_grad)
    is_patch = kind == 1
    last = jnp.concatenate(
        [jnp.where(is_patch, none, chosen_grad), jnp.where(is_patch, chosen_grad, none), small], axis=1
    )
    last = sum_seq(fold_clips(last, clip_orders(n)[0], n), size).astype(F32)
    frame_grad = last[:, :d]
    patch_grad = last[:, d : 2 * d]
    flat = last[:, 2 * d :].reshape(-1)
    small_out = []
    at = 0
    for v in vectors:
        small_out.append(flat[at : at + v.shape[0] // n])
        at += v.shape[0] // n
    (
        mask_out,
        gain1_out,
        bias1_out,
        q_out,
        v_out,
        outb_out,
        gain2_out,
        bias2_out,
        upb_out,
        downb_out,
    ) = small_out
    return (
        output,
        features_grad,
        frame_grad,
        patch_grad,
        mask_out,
        gain1_out,
        bias1_out,
        qkv_grad,
        q_out,
        v_out,
        out_grad,
        outb_out,
        gain2_out,
        bias2_out,
        up_grad,
        upb_out,
        down_grad,
        downb_out,
    )


def solution(mesh):
    tokens = P("clips", "seq", None)
    rows = P("clips", None)
    vec = P("clips")
    return jax.shard_map(
        body,
        mesh=mesh,
        in_specs=(tokens, P("clips"), rows) + (P(),) * 16 + (tokens,),
        out_specs=(tokens, tokens, rows, rows, vec, vec, vec, rows, vec, vec, rows, vec, vec, vec, rows, vec, rows, vec),
        check_vma=False,
    )
```

```python
import functools

import jax
import jax.numpy as jnp
from jax import lax
from jax.experimental import pallas as pl
from jax.experimental.pallas import tpu as pltpu
from jax.sharding import PartitionSpec as P

HEADS = 12
HEAD_DIM = 64
EPSILON = 1e-06
F32 = jnp.float32
BF16 = jnp.bfloat16
MIB = 1 << 20
SCALE = HEAD_DIM ** (-0.5)
Q_BIAS, NO_BIAS, V_BIAS, MASK_EMBED, GAIN_ONE, BIAS_ONE, OUT_BIAS, GAIN_TWO, BIAS_TWO, DOWN_BIAS = range(10)
PAIR = 2 * HEAD_DIM


def norm_stats(values_in):
    centre = values_in - jnp.mean(values_in, axis=-1, keepdims=True)
    inverse = lax.rsqrt(jnp.mean(centre * centre, axis=-1, keepdims=True) + EPSILON)
    return (centre * inverse, inverse)


def norm_back(grad_normed, centred, inverse, gain):
    scaled = grad_normed * gain
    return inverse * (
        scaled
        - jnp.mean(scaled, axis=-1, keepdims=True)
        - centred * jnp.mean(scaled * centred, axis=-1, keepdims=True)
    )


def mm(a, b):
    return jnp.dot(a, b, preferred_element_type=F32)


def mm_nt(a, b):
    return lax.dot_general(a, b, (((1,), (1,)), ((), ())), preferred_element_type=F32)


def whole(shape):
    return pl.BlockSpec(shape, lambda *_: (0,) * len(shape))


def masked_column(place, masked_ref, size, rows):
    marks = masked_ref[...]
    cols = []
    for d in range(size):
        spot = (place ^ d) * rows + lax.broadcasted_iota(jnp.int32, (rows, marks.shape[1]), 0)
        cols.append(jnp.max(jnp.where(spot == marks, 1.0, 0.0), axis=1, keepdims=True))
    return jnp.concatenate(cols, axis=0) > 0.5


def half_of(pair_block, h):
    lane = lax.broadcasted_iota(jnp.int32, pair_block.shape, 1)
    inside = (lane < HEAD_DIM) if h == 0 else (lane >= HEAD_DIM)
    return jnp.where(inside, pair_block, jnp.zeros_like(pair_block))


def embed_kernel(size, rows, info, masked, feats, frame, patch, table, w, start, normed_t, qkv, normed):
    j = pl.program_id(0)

    @pl.when(j == 0)
    def _():
        chosen = jnp.where(info[1] == 1, patch[...], frame[...])
        embedded = mm(feats[...], chosen)
        is_masked = masked_column(info[0], masked, size, rows)
        start_now = jnp.where(is_masked, table[MASK_EMBED : MASK_EMBED + 1, :], embedded)
        start[...] = start_now
        centred, _inv = norm_stats(start_now)
        out = (centred * table[GAIN_ONE : GAIN_ONE + 1, :] + table[BIAS_ONE : BIAS_ONE + 1, :]).astype(BF16)
        normed[...] = out
        normed_t[...] = out.T

    projected = mm(normed[...], w[...]) + table[pl.ds(j, 1), :]
    qkv[...] = (projected * jnp.where(j == 0, SCALE, 1.0)).astype(BF16)


def embed_call(info, masked, feats, frame, patch, table, w_qkv, size, rows):
    t, f = feats.shape
    d = frame.shape[1]
    smem = pl.BlockSpec(memory_space=pltpu.SMEM)
    return pl.pallas_call(
        functools.partial(embed_kernel, size, rows),
        grid=(3,),
        in_specs=[
            smem,
            whole(masked.shape),
            whole((t, f)),
            whole((f, d)),
            whole((f, d)),
            whole(table.shape),
            pl.BlockSpec((d, d), lambda j: (0, j)),
        ],
        out_specs=[whole((t, d)), whole((d, t)), pl.BlockSpec((t, d), lambda j: (0, j))],
        out_shape=[
            jax.ShapeDtypeStruct((t, d), F32),
            jax.ShapeDtypeStruct((d, t), BF16),
            jax.ShapeDtypeStruct((t, 3 * d), BF16),
        ],
        scratch_shapes=[pltpu.VMEM((t, d), BF16)],
        compiler_params=pltpu.CompilerParams(vmem_limit_bytes=40 * MIB),
        cost_estimate=pl.CostEstimate(flops=2 * t * d * (f + 3 * d), bytes_accessed=12 * MIB, transcendentals=0),
        name="embed",
    )(info, masked, feats, frame, patch, table, w_qkv)


def attend_kernel(q, k, v, start, table, w_out, probs, att_t, middle, normed, normed_t, att):
    p = pl.program_id(0)
    v_t = v[...].T
    parts = []
    for h in range(2):
        scores = mm_nt(k[...], half_of(q[...], h))
        top = jnp.max(scores, axis=0, keepdims=True)
        e = jnp.exp(scores - top)
        total = jnp.sum(e, axis=0, keepdims=True)
        low = (e * (1.0 / total)).astype(BF16)
        probs[h] = low
        parts.append(mm(v_t[h * HEAD_DIM : (h + 1) * HEAD_DIM, :], low))
    out_t = jnp.concatenate(parts, axis=0)
    att_t[...] = out_t.astype(BF16)
    att[:, pl.ds(pl.multiple_of(p * PAIR, PAIR), PAIR)] = out_t.T.astype(BF16)

    @pl.when(p == pl.num_programs(0) - 1)
    def _():
        mid = start[...] + mm(att[...], w_out[...]) + table[OUT_BIAS : OUT_BIAS + 1, :]
        middle[...] = mid
        centred, _inv = norm_stats(mid)
        out = (centred * table[GAIN_TWO : GAIN_TWO + 1, :] + table[BIAS_TWO : BIAS_TWO + 1, :]).astype(BF16)
        normed[...] = out
        normed_t[...] = out.T


def attend_call(qkv, start, table, w_out):
    t, d = start.shape
    pairs = HEADS // 2

    def block(base):
        return pl.BlockSpec((t, PAIR), lambda p: (0, base + p))

    return pl.pallas_call(
        attend_kernel,
        grid=(pairs,),
        in_specs=[
            block(0),
            block(pairs),
            block(2 * pairs),
            whole((t, d)),
            whole(table.shape),
            whole((d, d)),
        ],
        out_specs=[
            pl.BlockSpec((2, t, t), lambda p: (p, 0, 0)),
            pl.BlockSpec((PAIR, t), lambda p: (p, 0)),
            whole((t, d)),
            whole((t, d)),
            whole((d, t)),
        ],
        out_shape=[
            jax.ShapeDtypeStruct((HEADS, t, t), BF16),
            jax.ShapeDtypeStruct((d, t), BF16),
            jax.ShapeDtypeStruct((t, d), F32),
            jax.ShapeDtypeStruct((t, d), BF16),
            jax.ShapeDtypeStruct((d, t), BF16),
        ],
        scratch_shapes=[pltpu.VMEM((t, d), BF16)],
        compiler_params=pltpu.CompilerParams(vmem_limit_bytes=40 * MIB),
        cost_estimate=pl.CostEstimate(
            flops=2 * t * d * (8 * t + d), bytes_accessed=20 * MIB, transcendentals=HEADS * t * t
        ),
        name="attend",
    )(qkv, qkv, qkv, start, table, w_out)


def feed_kernel(normed, normed_t, dy, middle, table, w_up, b_up, w_down, out, grad_n, down_g, up_g, up_b, total):
    c = pl.program_id(0)

    @pl.when(c == 0)
    def _():
        total[...] = middle[...] + table[DOWN_BIAS : DOWN_BIAS + 1, :]
        grad_n[...] = jnp.zeros_like(grad_n)

    hidden = mm(normed[...], w_up[...]) + b_up[...]
    phi = 0.5 * (1.0 + lax.erf(hidden * 0.7071067811865476))
    slope = phi + hidden * jnp.exp(-0.5 * hidden * hidden) * 0.3989422804014327
    active = (hidden * phi).astype(BF16)
    total[...] += mm(active, w_down[...])
    down_g[...] = mm(active.T, dy[...]).astype(BF16)
    grad_h = mm_nt(dy[...], w_down[...]) * slope
    low = grad_h.astype(BF16)
    up_b[...] = jnp.sum(low.astype(F32), axis=0, keepdims=True)
    up_g[...] = mm(normed_t[...], low).astype(BF16)
    grad_n[...] += mm_nt(low, w_up[...])

    @pl.when(c == pl.num_programs(0) - 1)
    def _():
        out[...] = total[...].astype(BF16)


def feed_call(normed, normed_t, dy, middle, table, w_up, b_up, w_down, step):
    t, d = normed.shape
    ff = w_up.shape[1]
    return pl.pallas_call(
        feed_kernel,
        grid=(ff // step,),
        in_specs=[
            whole((t, d)),
            whole((d, t)),
            whole((t, d)),
            whole((t, d)),
            whole(table.shape),
            pl.BlockSpec((d, step), lambda c: (0, c)),
            pl.BlockSpec((1, step), lambda c: (0, c)),
            pl.BlockSpec((step, d), lambda c: (c, 0)),
        ],
        out_specs=[
            whole((t, d)),
            whole((t, d)),
            pl.BlockSpec((step, d), lambda c: (c, 0)),
            pl.BlockSpec((d, step), lambda c: (0, c)),
            pl.BlockSpec((1, step), lambda c: (0, c)),
        ],
        out_shape=[
            jax.ShapeDtypeStruct((t, d), BF16),
            jax.ShapeDtypeStruct((t, d), F32),
            jax.ShapeDtypeStruct((ff, d), BF16),
            jax.ShapeDtypeStruct((d, ff), BF16),
            jax.ShapeDtypeStruct((1, ff), F32),
        ],
        scratch_shapes=[pltpu.VMEM((t, d), F32)],
        compiler_params=pltpu.CompilerParams(vmem_limit_bytes=44 * MIB),
        cost_estimate=pl.CostEstimate(flops=12 * t * d * ff, bytes_accessed=26 * MIB, transcendentals=2 * t * ff),
        name="feed",
    )(normed, normed_t, dy, middle, table, w_up, b_up, w_down)


def middle_kernel(grad_n, middle, dy, att_t, table, w_out, grad_mid, grad_att, out_g, sums):
    centred, inverse = norm_stats(middle[...])
    grad = grad_n[...]
    dy_f = dy[...].astype(F32)
    mid = dy_f + norm_back(grad, centred, inverse, table[GAIN_TWO : GAIN_TWO + 1, :])
    grad_mid[...] = mid
    low = mid.astype(BF16)
    sums[...] = jnp.concatenate(
        [
            jnp.sum(low.astype(F32), axis=0, keepdims=True),
            jnp.sum(grad * centred, axis=0, keepdims=True),
            jnp.sum(grad, axis=0, keepdims=True),
            jnp.sum(dy_f, axis=0, keepdims=True),
            jnp.zeros((4, mid.shape[1]), F32),
        ],
        axis=0,
    )
    grad_att[...] = mm_nt(low, w_out[...]).astype(BF16)
    out_g[...] = mm(att_t[...], low).astype(BF16)


def middle_call(grad_n, middle, dy, att_t, table, w_out):
    t, d = middle.shape
    return pl.pallas_call(
        middle_kernel,
        out_shape=[
            jax.ShapeDtypeStruct((t, d), F32),
            jax.ShapeDtypeStruct((t, d), BF16),
            jax.ShapeDtypeStruct((d, d), BF16),
            jax.ShapeDtypeStruct((8, d), F32),
        ],
        compiler_params=pltpu.CompilerParams(vmem_limit_bytes=40 * MIB),
        cost_estimate=pl.CostEstimate(flops=4 * t * d * d, bytes_accessed=10 * MIB, transcendentals=0),
        name="middle",
    )(grad_n, middle, dy, att_t, table, w_out)


def back_kernel(q, k, v, probs, grad_a, normed_t, wq, wk, wv, gq, gk, gv, grad_n, sums):
    p = pl.program_id(0)

    @pl.when(p == 0)
    def _():
        grad_n[...] = jnp.zeros_like(grad_n)

    k_t = k[...].T
    dk = dv = None
    dq_t = []
    for h in range(2):
        low = probs[h]
        grad_h = half_of(grad_a[...], h)
        grad_p = mm_nt(v[...], grad_h)
        wide = low.astype(F32)
        inner = jnp.sum(wide * grad_p, axis=0, keepdims=True)
        grad_s = (wide * (grad_p - inner)).astype(BF16)
        dv_h = mm(low, grad_h)
        dk_h = mm(grad_s, half_of(q[...], h))
        dv = dv_h if dv is None else dv + dv_h
        dk = dk_h if dk is None else dk + dk_h
        dq_t.append(mm(k_t[h * HEAD_DIM : (h + 1) * HEAD_DIM, :], grad_s))
    dq = (jnp.concatenate(dq_t, axis=0).T * SCALE).astype(BF16)
    grads = jnp.concatenate([dq, dk.astype(BF16), dv.astype(BF16)], axis=1)
    weights = jnp.concatenate([wq[...], wk[...], wv[...]], axis=1)
    sums[...] = jnp.sum(grads.astype(F32), axis=0, keepdims=True)[None]
    g = mm(normed_t[...], grads).astype(BF16)
    gq[...] = g[:, :PAIR]
    gk[...] = g[:, PAIR : 2 * PAIR]
    gv[...] = g[:, 2 * PAIR :]
    grad_n[...] += mm_nt(grads, weights)


def back_call(qkv, probs, grad_att, normed_t, w_qkv):
    t, d = grad_att.shape
    pairs = HEADS // 2

    def block(rows, base):
        return pl.BlockSpec((rows, PAIR), lambda p: (0, base + p))

    return pl.pallas_call(
        back_kernel,
        grid=(pairs,),
        in_specs=[
            block(t, 0),
            block(t, pairs),
            block(t, 2 * pairs),
            pl.BlockSpec((2, t, t), lambda p: (p, 0, 0)),
            block(t, 0),
            whole((d, t)),
            block(d, 0),
            block(d, pairs),
            block(d, 2 * pairs),
        ],
        out_specs=[
            block(d, 0),
            block(d, 0),
            block(d, 0),
            whole((t, d)),
            pl.BlockSpec((1, 1, 3 * PAIR), lambda p: (p, 0, 0)),
        ],
        out_shape=[jax.ShapeDtypeStruct((d, d), BF16)] * 3
        + [jax.ShapeDtypeStruct((t, d), F32), jax.ShapeDtypeStruct((pairs, 1, 3 * PAIR), F32)],
        compiler_params=pltpu.CompilerParams(vmem_limit_bytes=40 * MIB),
        cost_estimate=pl.CostEstimate(flops=2 * t * d * (16 * t + 6 * d), bytes_accessed=24 * MIB, transcendentals=0),
        name="back",
    )(qkv, qkv, qkv, probs, grad_att, normed_t, w_qkv, w_qkv, w_qkv)


def last_kernel(size, rows, info, masked, grad_n, start, grad_mid, feats, frame, patch, table, feats_g, chosen_g, sums):
    centred, inverse = norm_stats(start[...])
    grad = grad_n[...]
    total = grad_mid[...] + norm_back(grad, centred, inverse, table[GAIN_ONE : GAIN_ONE + 1, :])
    is_masked = masked_column(info[0], masked, size, rows)
    kept = jnp.where(is_masked, 0.0, total)
    sums[...] = jnp.concatenate(
        [
            jnp.sum(jnp.where(is_masked, total, 0.0), axis=0, keepdims=True),
            jnp.sum(grad * centred, axis=0, keepdims=True),
            jnp.sum(grad, axis=0, keepdims=True),
            jnp.zeros((5, total.shape[1]), F32),
        ],
        axis=0,
    )
    low = kept.astype(BF16)
    chosen = jnp.where(info[1] == 1, patch[...], frame[...])
    feats_g[...] = mm_nt(low, chosen).astype(BF16)
    chosen_g[...] = mm(feats[...].T, low).astype(BF16)


def last_call(info, masked, grad_n, start, grad_mid, feats, frame, patch, table, size, rows):
    t, d = start.shape
    f = feats.shape[1]
    vmem = pl.BlockSpec(memory_space=pltpu.VMEM)
    return pl.pallas_call(
        functools.partial(last_kernel, size, rows),
        in_specs=[pl.BlockSpec(memory_space=pltpu.SMEM)] + [vmem] * 8,
        out_shape=[
            jax.ShapeDtypeStruct((t, f), BF16),
            jax.ShapeDtypeStruct((f, d), BF16),
            jax.ShapeDtypeStruct((8, d), F32),
        ],
        compiler_params=pltpu.CompilerParams(vmem_limit_bytes=40 * MIB),
        cost_estimate=pl.CostEstimate(flops=4 * t * d * f, bytes_accessed=6 * MIB, transcendentals=0),
        name="last",
    )(info, masked, grad_n, start, grad_mid, feats, frame, patch, table)


LANES = 256
SEGMENT = 128
SMEM = pl.BlockSpec(memory_space=pltpu.SMEM)
HBM = pl.BlockSpec(memory_space=pltpu.HBM)


def pinned(array):
    return pltpu.with_memory_space_constraint(array, pltpu.HBM)


def place_of(info, chip, x_first):
    rel = jnp.bitwise_xor(chip, info[1] // 2)
    return (rel % 2) * 2 + rel // 2 if x_first else rel


def is_first_core(info):
    return info[1] % 2 == 0


def spread(value, rows, at, send, keep, info, x_first):
    first = is_first_core(info)
    for chip in range(4):
        even = value[2 * chip * rows : (2 * chip + 1) * rows]
        odd = value[(2 * chip + 1) * rows : (2 * chip + 2) * rows]
        place = place_of(info, chip, x_first)
        keep[pl.ds(place, 1), at : at + rows, :] = jnp.where(first, even, odd)[None]
        send[pl.ds(place, 1), at : at + rows, :] = jnp.where(first, odd, even)[None]


def spread_halves(value, at, send, keep, info):
    first = is_first_core(info)
    rows = value.shape[0] // 8
    half = rows // 2
    for i in range(2):
        for chip in range(4):
            begin = 2 * chip * rows + i * half
            even, odd = value[begin : begin + half], value[begin + rows : begin + rows + half]
            place = pl.ds(place_of(info, chip, i == 0), 1)
            keep[i, place, at : at + half, :] = jnp.where(first, even, odd)[None]
            send[i, place, at : at + half, :] = jnp.where(first, odd, even)[None]


def stacked(refs):
    return jnp.concatenate([r[...] for r in refs], axis=0)


def clip_mask(info, masked, size, rows):
    return masked_column(info[0], masked.at[pl.ds(info[0], 1)], size, rows)


def forward_kernel(
    size, rows, info, kinds, masked, *refs,
):
    feats, refs = refs[:size], refs[size:]
    (
        table, frame, patch, w_qkv, w_out, w_up, w_down,
        hat, inverse_t, normed_t, qkv_a, qkv_b, qkv_c, probs_a, probs_b, probs_c, att_t,
        middle, normed_two, normed_two_t, feats_t, ups, downs,
        start, normed, att, projs, w_in, w_back, sems, feed_sems,
    ) = refs
    qkvs, all_probs = (qkv_a, qkv_b, qkv_c), (probs_a, probs_b, probs_c)
    d = att.shape[1]
    third = d // LANES

    def weight_copy(group, i):
        cols = pl.ds(i * d + group * LANES, LANES)
        return pltpu.make_async_copy(w_qkv.at[:, cols], w_in.at[group, :, pl.ds(i * LANES, LANES)], sems.at[group, i])

    proj_copies = [pltpu.make_async_copy(p, projs.at[i], sems.at[third, i]) for i, p in enumerate((frame, patch))]
    out_copy = pltpu.make_async_copy(w_out, w_back, sems.at[third, 2])
    for copy in proj_copies:
        copy.start()
    for group in range(third):
        for i in range(3):
            weight_copy(group, i).start()
    out_copy.start()
    feed_copies = [pltpu.make_async_copy(w, v, feed_sems.at[i]) for i, (w, v) in enumerate(((w_up, ups), (w_down, downs)))]
    is_masked = clip_mask(info, masked, size, rows)
    features = stacked(feats)
    feats_t[...] = features.T
    for copy in proj_copies:
        copy.wait()
    chosen = jnp.where(kinds[info[0]] == 1, projs[1], projs[0])
    start_now = jnp.where(is_masked, table[MASK_EMBED : MASK_EMBED + 1, :], mm(features, chosen))
    start[...] = start_now
    centred, inverse = norm_stats(start_now)
    hat[...] = centred.astype(BF16)
    inverse_t[...] = jnp.broadcast_to(inverse, inverse_t.shape)
    out = (centred * table[GAIN_ONE : GAIN_ONE + 1, :] + table[BIAS_ONE : BIAS_ONE + 1, :]).astype(BF16)
    normed[...] = out
    normed_t[...] = out.T
    for group in range(third):
        for i in range(3):
            weight_copy(group, i).wait()
    out_copy.wait()
    for copy in feed_copies:
        copy.start()

    def project(group):
        lanes = slice(group * LANES, (group + 1) * LANES)
        projected = mm(normed[...], w_in[group])
        q = ((projected[:, :LANES] + table[Q_BIAS : Q_BIAS + 1, lanes]) * SCALE).astype(BF16)
        k = projected[:, LANES : 2 * LANES].astype(BF16)
        v = (projected[:, 2 * LANES :] + table[V_BIAS : V_BIAS + 1, lanes]).astype(BF16)
        for i, value in enumerate((q, k, v)):
            qkvs[group][:, i * LANES : (i + 1) * LANES] = value
        return q, k, v.T

    def scores_of(h):
        q, k, _v = held[h // 4]
        pair = slice((h % 4 // 2) * PAIR, (h % 4 // 2 + 1) * PAIR)
        return mm_nt(k[:, pair], half_of(q[:, pair], h % 2))

    held = {0: project(0)}
    upcoming = scores_of(0)
    parts = []
    for h in range(HEADS):
        group = h // 4
        scores = upcoming
        if h % 4 == 2 and group + 1 < third:
            held[group + 1] = project(group + 1)
        if h + 1 < HEADS:
            upcoming = scores_of(h + 1)
        top = jnp.max(scores, axis=0, keepdims=True)
        e = jnp.exp(scores - top)
        total = jnp.sum(e, axis=0, keepdims=True)
        low = (e * (1.0 / total)).astype(BF16)
        all_probs[group][h % 4] = low
        v_t = held[group][2]
        parts.append(mm(v_t[h % 4 * HEAD_DIM : (h % 4 + 1) * HEAD_DIM, :], low))
        if h % 4 == 3:
            out_t = jnp.concatenate(parts, axis=0).astype(BF16)
            parts = []
            lanes = slice(group * LANES, (group + 1) * LANES)
            att_t[lanes, :] = out_t
            att[:, lanes] = out_t.T
    mid = start[...] + mm(att[...], w_back[...]) + table[OUT_BIAS : OUT_BIAS + 1, :]
    middle[...] = mid
    centred, _inv = norm_stats(mid)
    out = (centred * table[GAIN_TWO : GAIN_TWO + 1, :] + table[BIAS_TWO : BIAS_TWO + 1, :]).astype(BF16)
    normed_two[...] = out
    normed_two_t[...] = out.T
    for copy in feed_copies:
        copy.wait()


def forward_call(info, kinds, masked, feats, frame, patch, table, w_qkv, w_out, w_up, w_down, size, rows):
    f, d = frame.shape
    t = size * rows
    third = d // LANES
    return pl.pallas_call(
        functools.partial(forward_kernel, size, rows),
        in_specs=[SMEM, SMEM] + [pl.BlockSpec(memory_space=pltpu.VMEM)] * (size + 2) + [HBM] * 6,
        out_shape=[
            jax.ShapeDtypeStruct((t, d), BF16),
            jax.ShapeDtypeStruct((t, 128), F32),
            jax.ShapeDtypeStruct((d, t), BF16),
            *([jax.ShapeDtypeStruct((t, 3 * LANES), BF16)] * third),
            *([jax.ShapeDtypeStruct((4, t, t), BF16)] * third),
            jax.ShapeDtypeStruct((d, t), BF16),
            jax.ShapeDtypeStruct((t, d), F32),
            jax.ShapeDtypeStruct((t, d), BF16),
            jax.ShapeDtypeStruct((d, t), BF16),
            jax.ShapeDtypeStruct((f, t), BF16),
            jax.ShapeDtypeStruct(w_up.shape, BF16),
            jax.ShapeDtypeStruct(w_down.shape, BF16),
        ],
        scratch_shapes=[
            pltpu.VMEM((t, d), F32),
            pltpu.VMEM((t, d), BF16),
            pltpu.VMEM((t, d), BF16),
            pltpu.VMEM((2, f, d), BF16),
            pltpu.VMEM((third, d, 3 * LANES), BF16),
            pltpu.VMEM((d, d), BF16),
            pltpu.SemaphoreType.DMA((third + 1, 3)),
            pltpu.SemaphoreType.DMA((2,)),
        ],
        compiler_params=pltpu.CompilerParams(vmem_limit_bytes=FORWARD_MIB * MIB),
        cost_estimate=pl.CostEstimate(
            flops=2 * t * d * (f + 4 * d + 8 * t), bytes_accessed=24 * MIB, transcendentals=HEADS * t * t
        ),
        name="forward",
    )(info, kinds, masked, *feats, table, *(pinned(w) for w in (frame, patch, w_qkv, w_out, w_up, w_down)))


def feed_forward_kernel(normed, middle, table, b_up, ups, downs, out, actives, slopes, total):
    step = downs.shape[0] // 2
    total[...] = middle[...] + table[DOWN_BIAS : DOWN_BIAS + 1, :]

    @pl.loop(0, 2)
    def _(c):
        cols = pl.ds(pl.multiple_of(c * step, step), step)
        hidden = mm(normed[...], ups[:, cols]) + b_up[:, cols]
        phi = 0.5 * (1.0 + lax.erf(hidden * 0.7071067811865476))
        slopes[:, cols] = (phi + hidden * jnp.exp(-0.5 * hidden * hidden) * 0.3989422804014327).astype(BF16)
        active = (hidden * phi).astype(BF16)
        actives[:, cols] = active
        total[...] += mm(active, downs[cols, :])

    out[...] = total[...].astype(BF16)


def down_kernel(size, info, actives, *refs):
    dy_pieces, (dy, send, keep) = refs[:size], refs[size:]
    first = is_first_core(info)
    step = actives.shape[1] // 4
    half = step // 4
    grad_rows = stacked(dy_pieces)
    dy[...] = grad_rows
    for c in range(4):
        down_g = mm(actives[:, c * step : (c + 1) * step].T, grad_rows).astype(BF16)
        for i in range(2):
            even = down_g[i * half : (i + 1) * half]
            odd = down_g[(2 + i) * half : (3 + i) * half]
            place = pl.ds(place_of(info, c, i == 0), 1)
            keep[i, place] = jnp.where(first, even, odd)[None]
            send[i, place] = jnp.where(first, odd, even)[None]


def feed_back_kernel(info, normed_t, dy, slopes, ups, downs, grad_n, send, keep, up_b):
    first = is_first_core(info)
    step = downs.shape[0] // 4
    rows = normed_t.shape[0] // 8
    grad_n[...] = jnp.zeros_like(grad_n)

    @pl.loop(0, 2)
    def _(c):
        cols = pl.ds(pl.multiple_of(2 * c * step, 2 * step), 2 * step)
        low = (mm_nt(dy[...], downs[cols, :]) * slopes[:, cols].astype(F32)).astype(BF16)
        up_b[:, cols] = jnp.sum(low.astype(F32), axis=0, keepdims=True)
        up_g = mm(normed_t[...], low).astype(BF16)
        for chip in range(4):
            place = jnp.where(c == 0, place_of(info, chip, True), place_of(info, chip, False))
            for n in range(2):
                lanes = slice(n * step, (n + 1) * step)
                even = up_g[2 * chip * rows : (2 * chip + 1) * rows, lanes]
                odd = up_g[(2 * chip + 1) * rows : (2 * chip + 2) * rows, lanes]
                where = (pl.ds(c, 1), pl.ds(place, 1), pl.ds(n * rows, rows))
                keep[where] = jnp.where(first, even, odd)[None, None]
                send[where] = jnp.where(first, odd, even)[None, None]
        grad_n[...] += mm_nt(low, ups[:, cols])


VMEM = pl.BlockSpec(memory_space=pltpu.VMEM)


def feed_forward_call(normed, middle, table, b_up, ups, downs):
    t, d = normed.shape
    ff = ups.shape[1]
    return pl.pallas_call(
        feed_forward_kernel,
        in_specs=[VMEM] * 6,
        out_shape=[
            jax.ShapeDtypeStruct((t, d), BF16),
            jax.ShapeDtypeStruct((t, ff), BF16),
            jax.ShapeDtypeStruct((t, ff), BF16),
        ],
        scratch_shapes=[pltpu.VMEM((t, d), F32)],
        compiler_params=pltpu.CompilerParams(vmem_limit_bytes=FEED_MIB * MIB),
        cost_estimate=pl.CostEstimate(flops=4 * t * d * ff, bytes_accessed=18 * MIB, transcendentals=2 * t * ff),
        name="feed_forward",
    )(normed, middle, table, b_up, ups, downs)


def down_call(info, actives, dy):
    t, ff = actives.shape
    d = dy[0].shape[1]
    held = jax.ShapeDtypeStruct((2, 4, ff // 16, d), BF16)
    return pl.pallas_call(
        functools.partial(down_kernel, len(dy)),
        in_specs=[SMEM] + [VMEM] * (1 + len(dy)),
        out_shape=[jax.ShapeDtypeStruct((t, d), BF16), held, held],
        compiler_params=pltpu.CompilerParams(vmem_limit_bytes=FEED_MIB * MIB),
        cost_estimate=pl.CostEstimate(flops=2 * t * d * ff, bytes_accessed=9 * MIB, transcendentals=0),
        name="down",
    )(info, actives, *dy)


def feed_back_call(info, normed_t, dy, slopes, ups, downs):
    d, t = normed_t.shape
    ff = ups.shape[1]
    held = jax.ShapeDtypeStruct((2, 4, 2 * d // 8, ff // 4), BF16)
    return pl.pallas_call(
        feed_back_kernel,
        in_specs=[SMEM] + [VMEM] * 5,
        out_shape=[
            jax.ShapeDtypeStruct((t, d), F32),
            held,
            held,
            jax.ShapeDtypeStruct((1, ff), F32),
        ],
        compiler_params=pltpu.CompilerParams(vmem_limit_bytes=FEED_MIB * MIB),
        cost_estimate=pl.CostEstimate(flops=6 * t * d * ff, bytes_accessed=18 * MIB, transcendentals=0),
        name="feed_back",
    )(info, normed_t, dy, slopes, ups, downs)


def middle_kernel_fast(info, grad_n, middle, dy, att_t, table, w_out, grad_mid, grad_att, send, keep, sums, w, sem):
    copy = pltpu.make_async_copy(w_out, w, sem)
    copy.start()
    centred, inverse = norm_stats(middle[...])
    grad = grad_n[...]
    dy_f = dy[...].astype(F32)
    mid = dy_f + norm_back(grad, centred, inverse, table[GAIN_TWO : GAIN_TWO + 1, :])
    grad_mid[...] = mid.astype(BF16)
    low = mid.astype(BF16)
    sums[...] = jnp.concatenate(
        [
            jnp.sum(low.astype(F32), axis=0, keepdims=True),
            jnp.sum(grad * centred, axis=0, keepdims=True),
            jnp.sum(grad, axis=0, keepdims=True),
            jnp.sum(dy_f, axis=0, keepdims=True),
            jnp.zeros((4, mid.shape[1]), F32),
        ],
        axis=0,
    )
    out_g = mm(att_t[...], low).astype(BF16)
    spread(out_g, out_g.shape[0] // 8, 0, send, keep, info, True)
    copy.wait()
    grad_att[...] = mm_nt(low, w[...]).astype(BF16)


def middle_call_fast(info, grad_n, middle, dy, att_t, table, w_out):
    t, d = middle.shape
    vmem = pl.BlockSpec(memory_space=pltpu.VMEM)
    held = jax.ShapeDtypeStruct((4, d // 8, d), BF16)
    return pl.pallas_call(
        middle_kernel_fast,
        in_specs=[SMEM] + [vmem] * 5 + [HBM],
        out_shape=[
            jax.ShapeDtypeStruct((t, d), BF16),
            jax.ShapeDtypeStruct((t, d), BF16),
            held,
            held,
            jax.ShapeDtypeStruct((8, d), F32),
        ],
        scratch_shapes=[pltpu.VMEM((d, d), BF16), pltpu.SemaphoreType.DMA],
        compiler_params=pltpu.CompilerParams(vmem_limit_bytes=OTHER_MIB * MIB),
        cost_estimate=pl.CostEstimate(flops=4 * t * d * d, bytes_accessed=10 * MIB, transcendentals=0),
        name="middle",
    )(info, grad_n, middle, dy, att_t, table, pinned(w_out))


def back_group(group, qkv, probs, grad_a, normed_t, w_qkv, w, sems):
    d = w.shape[0]
    copies = [
        pltpu.make_async_copy(
            w_qkv.at[:, pl.ds(i * d + group * LANES, LANES)], w.at[:, pl.ds(i * LANES, LANES)], sems.at[i]
        )
        for i in range(3)
    ]
    for copy in copies:
        copy.start()
    q, k, v = (qkv[:, i * LANES : (i + 1) * LANES] for i in range(3))
    k_t = k.T
    dq_t, dks, dvs = [], [], []
    for pair in range(2):
        lanes = slice(pair * PAIR, (pair + 1) * PAIR)
        qp, vp, gp = q[:, lanes], v[:, lanes], grad_a[:, lanes]
        dk = dv = None
        for h in range(2):
            low = probs[2 * pair + h]
            grad_h = half_of(gp, h)
            grad_p = mm_nt(vp, grad_h)
            wide = low.astype(F32)
            inner = jnp.sum(wide * grad_p, axis=0, keepdims=True)
            grad_s = (wide * (grad_p - inner)).astype(BF16)
            dv_h = mm(low, grad_h)
            dk_h = mm(grad_s, half_of(qp, h))
            dv = dv_h if dv is None else dv + dv_h
            dk = dk_h if dk is None else dk + dk_h
            head = 2 * pair + h
            dq_t.append(mm(k_t[head * HEAD_DIM : (head + 1) * HEAD_DIM, :], grad_s))
        dks.append(dk.astype(BF16))
        dvs.append(dv.astype(BF16))
    dq = (jnp.concatenate(dq_t, axis=0) * SCALE).astype(BF16).T
    grads = jnp.concatenate([dq] + dks + dvs, axis=1)
    sums = jnp.sum(grads.astype(F32), axis=0, keepdims=True)
    weight_grad = mm(normed_t[...], grads).astype(BF16)
    for copy in copies:
        copy.wait()
    return weight_grad, mm_nt(grads, w[...]), sums


def back_kernel_fast(group, info, qkv, probs, grad_a, normed_t, w_qkv, *refs):
    opens = group == 0
    if not opens:
        grad_in, send_o, keep_o, send_a, keep_a, *refs = refs
    grad_n, sums, send, keep, w, sems = refs
    g, grad, total = back_group(group, qkv, probs, grad_a, normed_t, w_qkv, w, sems)
    grad_n[...] = grad if opens else grad_in[...] + grad
    sums[...] = total
    if opens:
        spread(g, g.shape[0] // 8, 0, send, keep, info, False)
    else:
        rows = g.shape[0] // 8
        for ref, one, two in ((send, send_o, send_a), (keep, keep_o, keep_a)):
            ref[0, :, :rows] = one[...]
            ref[1, :, :rows] = two[...]
        spread_halves(g, rows, send, keep, info)


def back_specs(t, d, group):
    return [
        SMEM,
        whole((t, 3 * LANES)),
        whole((4, t, t)),
        pl.BlockSpec((t, LANES), lambda s: (0, group)),
        whole((d, t)),
        HBM,
    ]


def back_scratch(d):
    return [pltpu.VMEM((d, 3 * LANES), BF16), pltpu.SemaphoreType.DMA((3,))]


def back_call_fast(info, qkv, probs, grad_att, normed_t, w_qkv, group, carried):
    t, d = grad_att.shape
    held = (4, d // 8, d) if group == 0 else (2, 4, 3 * d // 16, d)
    return pl.pallas_call(
        functools.partial(back_kernel_fast, group),
        grid=(1,),
        in_specs=back_specs(t, d, group) + [whole(a.shape) for a in carried],
        out_specs=[whole((t, d)), whole((1, d)), whole(held), whole(held)],
        out_shape=[
            jax.ShapeDtypeStruct((t, d), F32),
            jax.ShapeDtypeStruct((1, d), F32),
            jax.ShapeDtypeStruct(held, BF16),
            jax.ShapeDtypeStruct(held, BF16),
        ],
        scratch_shapes=back_scratch(d),
        compiler_params=pltpu.CompilerParams(vmem_limit_bytes=OTHER_MIB * MIB),
        cost_estimate=pl.CostEstimate(flops=2 * t * d * (16 * t + 6 * d) // 3, bytes_accessed=9 * MIB, transcendentals=0),
        name="back",
    )(info, qkv, probs, grad_att, normed_t, pinned(w_qkv), *carried)


def last_kernel_fast(
    size, rows, group, info, qkv, probs, grad_a, normed_t, w_qkv, grad_in, kinds, masked, hat, inverse_t, grad_mid, *refs
):
    feats_t, frame, patch, table, sums_two, sums_a, sums_b, *refs = refs
    up_b, feats_g, send, keep, w, sems = refs
    g, grad, sums_c = back_group(group, qkv, probs, grad_a, normed_t, w_qkv, w, sems)
    d = g.shape[0]
    half = d // 16
    (send_x, send_y), (keep_x, keep_y) = ((r.at[0], r.at[1]) for r in (send, keep))
    spread_halves(g, 0, send, keep, info)
    grad = grad_in[...] + grad
    centred, inverse = hat[...].astype(F32), inverse_t[:, :1]
    total = grad_mid[...].astype(F32) + norm_back(grad, centred, inverse, table[GAIN_ONE : GAIN_ONE + 1, :])
    is_masked = clip_mask(info, masked, size, rows)
    low = jnp.where(is_masked, 0.0, total).astype(BF16)
    is_patch = kinds[info[0]] == 1
    chosen = jnp.where(is_patch, patch[...], frame[...])
    feats_g[...] = mm_nt(low, chosen).astype(BF16)
    g = mm(feats_t[...], low).astype(BF16)
    none = jnp.zeros_like(g)
    b = g.shape[0] // 8
    spread(jnp.where(is_patch, none, g), b, half, send_x, keep_x, info, True)
    spread(jnp.where(is_patch, g, none), b, half, send_y, keep_y, info, False)
    for ref in (send_y, keep_y):
        ref[:, half + b :, :] = jnp.zeros((4, 16, d), BF16)
    sums = [sums_a[...], sums_b[...], sums_c]
    vectors = jnp.concatenate(
        [
            jnp.sum(jnp.where(is_masked, total, 0.0), axis=0, keepdims=True),
            jnp.sum(grad * centred, axis=0, keepdims=True),
            jnp.sum(grad, axis=0, keepdims=True),
            jnp.concatenate([s[:, :LANES] for s in sums], axis=1),
            jnp.concatenate([s[:, 2 * LANES :] for s in sums], axis=1),
            sums_two[0:4, :],
            jnp.zeros((7, d), F32),
        ],
        axis=0,
    )
    width = d // 8
    wide = up_b.shape[1] // 8
    blocks = []
    for r in range(8):
        rolled = vectors if r == 0 else pltpu.roll(vectors, d - r * width, 1)
        up = jnp.concatenate([up_b[:, r * wide : (r + 1) * wide], jnp.zeros((1, d - wide), F32)], axis=1)
        blocks.append(jnp.concatenate([rolled[:9], up, jnp.zeros((6, d), F32)], axis=0))
    spread(jnp.concatenate(blocks, axis=0).astype(BF16), 16, half + b, send_x, keep_x, info, True)


def last_call_fast(
    info, qkv, probs, grad_att, normed_t, w_qkv, carried, kinds, masked, hat, inverse_t, grad_mid, feats_t, frame, patch, table,
    sums_two, sums_a, sums_b, up_b, size, rows,
):
    t, d = grad_att.shape
    f = frame.shape[0]
    held = (2, 4, d // 16 + f // 8 + 16, d)
    more = (masked, hat, inverse_t, grad_mid, feats_t, frame, patch, table, sums_two, sums_a, sums_b, up_b)
    group = d // LANES - 1
    return pl.pallas_call(
        functools.partial(last_kernel_fast, size, rows, group),
        grid=(1,),
        in_specs=back_specs(t, d, group) + [whole(carried.shape), SMEM] + [whole(a.shape) for a in more],
        out_specs=[whole((t, f)), whole(held), whole(held)],
        out_shape=[
            jax.ShapeDtypeStruct((t, f), BF16),
            jax.ShapeDtypeStruct(held, BF16),
            jax.ShapeDtypeStruct(held, BF16),
        ],
        scratch_shapes=back_scratch(d),
        compiler_params=pltpu.CompilerParams(vmem_limit_bytes=OTHER_MIB * MIB),
        cost_estimate=pl.CostEstimate(flops=2 * t * d * (16 * t + 6 * d) // 3, bytes_accessed=16 * MIB, transcendentals=0),
        name="last",
    )(info, qkv, probs, grad_att, normed_t, pinned(w_qkv), carried, kinds, *more)


def settle_kernel(one, two, down, up):
    down[...] = one[...].astype(F32)
    b = up.shape[0]
    for c in range(4):
        up[:, c * two.shape[1] : (c + 1) * two.shape[1]] = two[c * b : (c + 1) * b].astype(F32)


def settle(one, two, b):
    d = one.shape[1]
    vmem = pl.BlockSpec(memory_space=pltpu.VMEM)
    return pl.pallas_call(
        settle_kernel,
        in_specs=[vmem] * 2,
        out_shape=[jax.ShapeDtypeStruct(one.shape, F32), jax.ShapeDtypeStruct((b, 4 * d), F32)],
        cost_estimate=pl.CostEstimate(flops=0, bytes_accessed=6 * MIB, transcendentals=0),
        compiler_params=pltpu.CompilerParams(vmem_limit_bytes=8 * MIB),
        name="settle",
    )(one, two)


def settle_last_kernel(za, zb, out_g, qkv_g, frame_g, patch_g, vec):
    b, d = out_g.shape
    fr = frame_g.shape[0]
    one, two = za[...].astype(F32), zb[...].astype(F32)
    x1, y1 = one[: one.shape[0] // 2], one[one.shape[0] // 2 :]
    x2, y2 = two[: two.shape[0] // 2], two[two.shape[0] // 2 :]
    out_g[...] = x1[:b]
    half = b // 2
    groups = (y1[:b],), (x1[b:], y1[b:]), (x2[:half], y2[:half])
    for s, pieces in enumerate(groups):
        at = 0
        for value in pieces:
            for i in range(3):
                lane = i * d + s * LANES
                qkv_g[at : at + value.shape[0], lane : lane + LANES] = value[:, i * LANES : (i + 1) * LANES]
            at += value.shape[0]
    frame_g[...] = x2[half : half + fr]
    patch_g[...] = y2[half : half + fr]
    vec[...] = x2[half + fr :]


def settle_last(za, zb, b, fr):
    d = za.shape[1]
    vmem = pl.BlockSpec(memory_space=pltpu.VMEM)
    return pl.pallas_call(
        settle_last_kernel,
        in_specs=[vmem] * 2,
        out_shape=[
            jax.ShapeDtypeStruct((b, d), F32),
            jax.ShapeDtypeStruct((b, 3 * d), F32),
            jax.ShapeDtypeStruct((fr, d), F32),
            jax.ShapeDtypeStruct((fr, d), F32),
            jax.ShapeDtypeStruct((16, d), F32),
        ],
        cost_estimate=pl.CostEstimate(flops=0, bytes_accessed=4 * MIB, transcendentals=0),
        compiler_params=pltpu.CompilerParams(vmem_limit_bytes=8 * MIB),
        name="settle_last",
    )(za, zb)


def place_kernel(size, info, *refs):
    out = refs[size]
    for i in range(size):

        @pl.when(pl.program_id(0) == i)
        def _():
            out[0] = refs[i][...]


def place(info, pieces):
    size = len(pieces)
    shape = pieces[0].shape
    return pl.pallas_call(
        functools.partial(place_kernel, size),
        grid_spec=pltpu.PrefetchScalarGridSpec(
            num_scalar_prefetch=1,
            grid=(size,),
            in_specs=[pl.BlockSpec(shape, lambda i, info: (0, 0))] * size,
            out_specs=pl.BlockSpec((1,) + shape, lambda i, info: (jnp.bitwise_xor(info[0], i), 0, 0)),
        ),
        out_shape=jax.ShapeDtypeStruct((size,) + shape, pieces[0].dtype),
        cost_estimate=pl.CostEstimate(flops=0, bytes_accessed=4 * size * pieces[0].size, transcendentals=0),
        compiler_params=pltpu.CompilerParams(vmem_limit_bytes=8 * MIB),
        name="place",
    )(info, *pieces)


def swap(block, axis, size, flip):
    return lax.ppermute(block, axis, [(i, i ^ flip) for i in range(size)])


def to_clip(pieces, me, size):
    out = [lax.dynamic_index_in_dim(pieces, me, 0, keepdims=False)]
    for d in range(1, size):
        out.append(swap(lax.dynamic_index_in_dim(pieces, me ^ d, 0, keepdims=False), "seq", size, d))
    return jnp.concatenate(out, axis=0)


def to_pieces(clip_rows, me, size):
    rel = clip_rows.reshape(size, -1, clip_rows.shape[-1])
    got = [rel[0]] + [swap(rel[d], "seq", size, d) for d in range(1, size)]
    out = jnp.zeros_like(rel)
    for d in range(size):
        out = lax.dynamic_update_index_in_dim(out, got[d], me ^ d, 0)
    return out


def bits_of(n):
    return n.bit_length() - 1


def fold_clips(grad, order, n):
    count = bits_of(n)
    me = lax.axis_index("clips")
    rows, width = grad.shape
    held = grad.reshape((2,) * count + (rows // n, width))
    left = list(range(count - 1, -1, -1))
    for bit in order:
        axis = left.index(bit)
        mine = (me >> bit) & 1
        send = lax.dynamic_index_in_dim(held, 1 - mine, axis, keepdims=False)
        keep = lax.dynamic_index_in_dim(held, mine, axis, keepdims=False)
        held = keep + swap(send, "clips", n, 1 << bit)
        left.pop(axis)
    return held


def sum_seq(part, size):
    me = lax.axis_index("seq")
    count = bits_of(size)
    held = part
    for bit in range(count):
        half = held.shape[1] // 2
        mine = (me >> bit) & 1
        send = lax.dynamic_slice_in_dim(held, (1 - mine) * half, half, 1)
        keep = lax.dynamic_slice_in_dim(held, mine * half, half, 1)
        held = keep + swap(send, "seq", size, 1 << bit)
    for bit in reversed(range(count)):
        got = swap(held, "seq", size, 1 << bit)
        mine = (me >> bit) & 1
        held = jnp.where(
            mine == 0, jnp.concatenate([held, got], axis=1), jnp.concatenate([got, held], axis=1)
        )
    return held


def clip_orders(n):
    count = bits_of(n)
    low = [0] if count else []
    rest = list(range(1, count))
    return low + rest, low + rest[::-1]


def reduce_grad(grad, n, size):
    first, second = clip_orders(n)
    half = grad.shape[1] // 2
    a = fold_clips(grad[:, :half], first, n)
    b = fold_clips(grad[:, half:], second, n)
    return sum_seq(jnp.concatenate([a, b], axis=1), size).astype(F32)


FORWARD_MIB, FEED_MIB, OTHER_MIB = 20, 14, 14


def tie(*values):
    return lax.optimization_barrier(values)


def over(block, bit):
    return swap(block, "clips", 8, 1 << bit)


def hop(block, pairs):
    return lax.ppermute(block, "seq", pairs)


INWARD, ACROSS, OUTWARD = [(0, 1), (3, 2)], [(1, 2), (2, 1)], [(1, 0), (2, 3)]
NEAR, FAR = [(i, i ^ 1) for i in range(4)], [(i, i ^ 2) for i in range(4)]


def add(*terms):
    total = terms[0].astype(F32)
    for term in terms[1:]:
        total = total + term.astype(F32)
    return total.astype(BF16)


class Item:
    def __init__(self, send, keep):
        self.keep = keep
        self.got = over(send, 0)

    def first(self):
        self.rest = [add(self.keep[i, :2], self.got[i, :2]) for i in range(2)]
        return [add(self.keep[i, 2:], self.got[i, 2:]) for i in range(2)]

    def send_first(self, parts):
        self.one = (over(parts[0], 1), over(parts[1], 2))

    def second(self):
        self.mine = [add(self.rest[i][0], self.one[i][0]) for i in range(2)]
        return [add(self.rest[i][1], self.one[i][1]) for i in range(2)]

    def send_second(self, parts):
        self.two = (over(parts[0], 2), over(parts[1], 1))

    def line(self):
        return jnp.concatenate([add(self.mine[i], self.two[i]) for i in range(2)], axis=0)


def fast_path(features, clip_kind, masked_positions, weights, cotangent):
    (
        frame_proj,
        patch_proj,
        mask_embed,
        norm1_gain,
        norm1_bias,
        w_qkv,
        q_bias,
        v_bias,
        w_out,
        out_bias,
        norm2_gain,
        norm2_bias,
        w_up,
        up_bias,
        w_down,
        down_bias,
    ) = weights
    size = 4
    me = lax.axis_index("seq")
    rows = features.shape[1]
    d = w_out.shape[0]

    def from_pieces(array):
        mine = [lax.dynamic_index_in_dim(array, me ^ i, 0, keepdims=False) for i in range(size)]
        return [mine[0]] + [swap(mine[i], "seq", size, i) for i in range(1, size)]

    def to_owners(array):
        rel = array.reshape(size, rows, -1)
        return [rel[0]] + [swap(rel[i], "seq", size, i) for i in range(1, size)]

    info = jnp.stack([me, lax.axis_index("clips")])
    outer = (me == 0) | (me == 3)
    features, info, outer = tie(features, info, outer)
    feats = from_pieces(features)
    dy = from_pieces(cotangent)
    zero = jnp.zeros_like(q_bias)
    table = jnp.stack(
        [q_bias, zero, v_bias, mask_embed, norm1_gain, norm1_bias, out_bias, norm2_gain, norm2_bias, down_bias]
        + [zero] * 6
    ).astype(F32)
    b_up = up_bias.astype(F32)[None, :]

    hat, inverse_t, normed_one_t, *groups, att_t, middle, normed_two, normed_two_t, feats_t, ups, downs = forward_call(
        info, clip_kind, masked_positions, feats, frame_proj, patch_proj, table, w_qkv, w_out, w_up, w_down, size, rows
    )
    output, actives, slopes = feed_forward_call(normed_two, middle, table, b_up, ups, downs)
    dy, send, keep = down_call(info, actives, dy)
    i1 = Item(send, keep)
    out_pieces = to_owners(output)
    p = i1.first()
    info, slopes, p, i1.rest = tie(info, slopes, p, i1.rest)
    i1.send_first(p)
    grad_n2, send, keep, up_b = feed_back_call(info, normed_two_t, dy, slopes, ups, downs)

    info, send, grad_n2, out_pieces, i1.one = tie(info, send, grad_n2, out_pieces, i1.one)
    i1.send_second(i1.second())
    i2 = Item(send, keep)
    grad_mid, grad_att, send_o, keep_o, sums_two = middle_call_fast(info, grad_n2, middle, dy, att_t, table, w_out)
    p = i2.first()
    info, grad_att, p, i2.rest, i1.two = tie(info, grad_att, p, i2.rest, i1.two)
    i2.send_first(p)
    z1 = i1.line()
    got1 = hop(z1, INWARD)
    grad_a, sums_a, send_a, keep_a = back_call_fast(info, groups[0], groups[3], grad_att, normed_one_t, w_qkv, 0, ())
    grad_b, sums_b, send, keep = back_call_fast(
        info, groups[1], groups[4], grad_att, normed_one_t, w_qkv, 1, (grad_a, send_o, keep_o, send_a, keep_a)
    )

    info, send, i2.one, got1 = tie(info, send, i2.one, got1)
    i4 = Item(send, keep)
    i2.send_second(i2.second())
    z1 = add(z1, got1)
    got1 = hop(z1, ACROSS)
    p = i4.first()
    info, grad_b, p, i4.rest = tie(info, grad_b, p, i4.rest)
    i4.send_first(p)
    feats_grad, send, keep = last_call_fast(
        info, groups[2], groups[5], grad_att, normed_one_t, w_qkv, grad_b, clip_kind, masked_positions, hat, inverse_t,
        grad_mid, feats_t, frame_proj, patch_proj, table, sums_two, sums_a, sums_b, up_b, size, rows,
    )

    info, send, feats_grad, i2.two, i4.one, got1 = tie(info, send, feats_grad, i2.two, i4.one, got1)
    i5 = Item(send, keep)
    i4.send_second(i4.second())
    z2 = i2.line()
    z1 = add(z1, got1)
    both = hop(jnp.where(outer, z2, z1), INWARD + OUTWARD)
    p = i5.first()
    info, p, i5.rest = tie(info, p, i5.rest)
    i5.send_first(p)
    info, i4.two = tie(info, i4.two)
    z4 = i4.line()
    info, i5.one, both = tie(info, i5.one, both)
    i5.send_second(i5.second())
    z1 = jnp.where(outer, both, z1)
    z2 = jnp.where(outer, z2, add(z2, both))
    got2 = hop(z2, ACROSS)
    got4 = hop(z4, INWARD)
    output = place(info, out_pieces)
    info, i5.two = tie(info, i5.two)
    z5 = i5.line()
    got5 = hop(z5, NEAR)
    info, got2, got4, output = tie(info, got2, got4, output)
    z4 = add(z4, got4)
    got4 = hop(z4, ACROSS)
    z2 = add(z2, got2)
    got2 = hop(z2, OUTWARD)
    info, feats_grad, got5 = tie(info, feats_grad, got5)
    z5 = add(z5, got5)
    got5 = hop(z5, FAR)
    info, feats_grad, got4 = tie(info, feats_grad, got4)
    z4 = add(z4, got4)
    got4 = hop(z4, OUTWARD)
    feat_pieces = to_owners(feats_grad)
    info, got2, feat_pieces = tie(info, got2, feat_pieces)
    down_grad, up_grad = settle(z1, jnp.where(outer, got2, z2), d // 8)
    features_grad = place(info, feat_pieces)
    info, features_grad, down_grad, got4, got5 = tie(info, features_grad, down_grad, got4, got5)
    out_grad, qkv_grad, frame_grad, patch_grad, vec = settle_last(
        jnp.where(outer, got4, z4), add(z5, got5), d // 8, frame_proj.shape[0] // 8
    )
    b = d // 8
    return (
        output,
        features_grad,
        frame_grad,
        patch_grad,
        vec[0, :b],
        vec[1, :b],
        vec[2, :b],
        qkv_grad,
        vec[3, :b],
        vec[4, :b],
        out_grad,
        vec[5, :b],
        vec[6, :b],
        vec[7, :b],
        up_grad,
        vec[9, : up_bias.shape[0] // 8],
        down_grad,
        vec[8, :b],
    )


def body(
    features,
    clip_kind,
    masked_positions,
    frame_proj,
    patch_proj,
    mask_embed,
    norm1_gain,
    norm1_bias,
    w_qkv,
    q_bias,
    v_bias,
    w_out,
    out_bias,
    norm2_gain,
    norm2_bias,
    w_up,
    up_bias,
    w_down,
    down_bias,
    cotangent,
):
    n = lax.axis_size("clips")
    size = lax.axis_size("seq")
    me = lax.axis_index("seq")
    clips_here, rows, _ = features.shape
    assert clips_here == size
    d = w_out.shape[0]
    if n == 8 and size == 4:
        weights = (
            frame_proj,
            patch_proj,
            mask_embed,
            norm1_gain,
            norm1_bias,
            w_qkv,
            q_bias,
            v_bias,
            w_out,
            out_bias,
            norm2_gain,
            norm2_bias,
            w_up,
            up_bias,
            w_down,
            down_bias,
        )
        return fast_path(features, clip_kind, masked_positions, weights, cotangent)

    feats = to_clip(features, me, size)
    dy = to_clip(cotangent, me, size)
    kind = lax.dynamic_index_in_dim(clip_kind, me, 0, keepdims=False)
    info = jnp.stack([me, kind])
    masked = lax.dynamic_index_in_dim(masked_positions, me, 0, keepdims=True)
    zero = jnp.zeros_like(q_bias)
    table = jnp.stack(
        [q_bias, zero, v_bias, mask_embed, norm1_gain, norm1_bias, out_bias, norm2_gain, norm2_bias, down_bias]
        + [zero] * 6
    ).astype(F32)
    b_up = up_bias.astype(F32)[None, :]

    start, normed_one_t, qkv = embed_call(info, masked, feats, frame_proj, patch_proj, table, w_qkv, size, rows)
    probs, att_t, middle, normed_two, normed_two_t = attend_call(qkv, start, table, w_out)
    output, grad_n2, down_grad, up_grad, up_b = feed_call(
        normed_two, normed_two_t, dy, middle, table, w_up, b_up, w_down, 512
    )
    down_grad = reduce_grad(down_grad, n, size)
    up_grad = reduce_grad(up_grad, n, size)
    output = to_pieces(output, me, size)
    grad_mid, grad_att, out_grad, sums_two = middle_call(grad_n2, middle, dy, att_t, table, w_out)
    out_grad = reduce_grad(out_grad, n, size)
    gq, gk, gv, grad_n1, sums_qkv = back_call(qkv, probs, grad_att, normed_one_t, w_qkv)
    qkv_grad = reduce_grad(jnp.concatenate([gq, gk, gv], axis=1), n, size)
    feats_grad, chosen_grad, sums_one = last_call(
        info, masked, grad_n1, start, grad_mid, feats, frame_proj, patch_proj, table, size, rows
    )
    features_grad = to_pieces(feats_grad, me, size)

    vectors = (
        sums_one[0],
        sums_one[1],
        sums_one[2],
        sums_qkv[:, 0, :PAIR].reshape(-1),
        sums_qkv[:, 0, 2 * PAIR :].reshape(-1),
        sums_two[0],
        sums_two[1],
        sums_two[2],
        up_b[0],
        sums_two[3],
    )
    flat = jnp.concatenate([v.reshape(n, -1) for v in vectors], axis=1)
    feat_rows = frame_proj.shape[0] // n
    lanes = -(-flat.shape[1] // (feat_rows * 128)) * 128
    small = jnp.pad(flat, ((0, 0), (0, feat_rows * lanes - flat.shape[1])))
    small = small.reshape(n * feat_rows, lanes).astype(BF16)
    none = jnp.zeros_like(chosen_grad)
    is_patch = kind == 1
    last = jnp.concatenate(
        [jnp.where(is_patch, none, chosen_grad), jnp.where(is_patch, chosen_grad, none), small], axis=1
    )
    last = sum_seq(fold_clips(last, clip_orders(n)[0], n), size).astype(F32)
    frame_grad = last[:, :d]
    patch_grad = last[:, d : 2 * d]
    flat = last[:, 2 * d :].reshape(-1)
    small_out = []
    at = 0
    for v in vectors:
        small_out.append(flat[at : at + v.shape[0] // n])
        at += v.shape[0] // n
    (
        mask_out,
        gain1_out,
        bias1_out,
        q_out,
        v_out,
        outb_out,
        gain2_out,
        bias2_out,
        upb_out,
        downb_out,
    ) = small_out
    return (
        output,
        features_grad,
        frame_grad,
        patch_grad,
        mask_out,
        gain1_out,
        bias1_out,
        qkv_grad,
        q_out,
        v_out,
        out_grad,
        outb_out,
        gain2_out,
        bias2_out,
        up_grad,
        upb_out,
        down_grad,
        downb_out,
    )


def solution(mesh):
    tokens = P("clips", "seq", None)
    rows = P("clips", None)
    vec = P("clips")
    return jax.shard_map(
        body,
        mesh=mesh,
        in_specs=(tokens, P("clips"), rows) + (P(),) * 16 + (tokens,),
        out_specs=(tokens, tokens, rows, rows, vec, vec, vec, rows, vec, vec, rows, vec, vec, vec, rows, vec, rows, vec),
        check_vma=False,
    )
```

```python
import functools

import jax
import jax.numpy as jnp
from jax import lax
from jax.experimental import pallas as pl
from jax.experimental.pallas import tpu as pltpu
from jax.sharding import PartitionSpec as P

HEADS = 12
HEAD_DIM = 64
EPSILON = 1e-06
F32 = jnp.float32
BF16 = jnp.bfloat16
MIB = 1 << 20
SCALE = HEAD_DIM ** (-0.5)
Q_BIAS, NO_BIAS, V_BIAS, MASK_EMBED, GAIN_ONE, BIAS_ONE, OUT_BIAS, GAIN_TWO, BIAS_TWO, DOWN_BIAS = range(10)
PAIR = 2 * HEAD_DIM


def norm_stats(values_in):
    centre = values_in - jnp.mean(values_in, axis=-1, keepdims=True)
    inverse = lax.rsqrt(jnp.mean(centre * centre, axis=-1, keepdims=True) + EPSILON)
    return (centre * inverse, inverse)


def norm_back(grad_normed, centred, inverse, gain):
    scaled = grad_normed * gain
    return inverse * (
        scaled
        - jnp.mean(scaled, axis=-1, keepdims=True)
        - centred * jnp.mean(scaled * centred, axis=-1, keepdims=True)
    )


def mm(a, b):
    return jnp.dot(a, b, preferred_element_type=F32)


def mm_nt(a, b):
    return lax.dot_general(a, b, (((1,), (1,)), ((), ())), preferred_element_type=F32)


def whole(shape):
    return pl.BlockSpec(shape, lambda *_: (0,) * len(shape))


def masked_column(place, masked_ref, size, rows):
    marks = masked_ref[...]
    cols = []
    for d in range(size):
        spot = (place ^ d) * rows + lax.broadcasted_iota(jnp.int32, (rows, marks.shape[1]), 0)
        cols.append(jnp.max(jnp.where(spot == marks, 1.0, 0.0), axis=1, keepdims=True))
    return jnp.concatenate(cols, axis=0) > 0.5


def half_of(pair_block, h):
    lane = lax.broadcasted_iota(jnp.int32, pair_block.shape, 1)
    inside = (lane < HEAD_DIM) if h == 0 else (lane >= HEAD_DIM)
    return jnp.where(inside, pair_block, jnp.zeros_like(pair_block))


def embed_kernel(size, rows, info, masked, feats, frame, patch, table, w, start, normed_t, qkv, normed):
    j = pl.program_id(0)

    @pl.when(j == 0)
    def _():
        chosen = jnp.where(info[1] == 1, patch[...], frame[...])
        embedded = mm(feats[...], chosen)
        is_masked = masked_column(info[0], masked, size, rows)
        start_now = jnp.where(is_masked, table[MASK_EMBED : MASK_EMBED + 1, :], embedded)
        start[...] = start_now
        centred, _inv = norm_stats(start_now)
        out = (centred * table[GAIN_ONE : GAIN_ONE + 1, :] + table[BIAS_ONE : BIAS_ONE + 1, :]).astype(BF16)
        normed[...] = out
        normed_t[...] = out.T

    projected = mm(normed[...], w[...]) + table[pl.ds(j, 1), :]
    qkv[...] = (projected * jnp.where(j == 0, SCALE, 1.0)).astype(BF16)


def embed_call(info, masked, feats, frame, patch, table, w_qkv, size, rows):
    t, f = feats.shape
    d = frame.shape[1]
    smem = pl.BlockSpec(memory_space=pltpu.SMEM)
    return pl.pallas_call(
        functools.partial(embed_kernel, size, rows),
        grid=(3,),
        in_specs=[
            smem,
            whole(masked.shape),
            whole((t, f)),
            whole((f, d)),
            whole((f, d)),
            whole(table.shape),
            pl.BlockSpec((d, d), lambda j: (0, j)),
        ],
        out_specs=[whole((t, d)), whole((d, t)), pl.BlockSpec((t, d), lambda j: (0, j))],
        out_shape=[
            jax.ShapeDtypeStruct((t, d), F32),
            jax.ShapeDtypeStruct((d, t), BF16),
            jax.ShapeDtypeStruct((t, 3 * d), BF16),
        ],
        scratch_shapes=[pltpu.VMEM((t, d), BF16)],
        compiler_params=pltpu.CompilerParams(vmem_limit_bytes=40 * MIB),
        cost_estimate=pl.CostEstimate(flops=2 * t * d * (f + 3 * d), bytes_accessed=12 * MIB, transcendentals=0),
        name="embed",
    )(info, masked, feats, frame, patch, table, w_qkv)


def attend_kernel(q, k, v, start, table, w_out, probs, att_t, middle, normed, normed_t, att):
    p = pl.program_id(0)
    v_t = v[...].T
    parts = []
    for h in range(2):
        scores = mm_nt(k[...], half_of(q[...], h))
        top = jnp.max(scores, axis=0, keepdims=True)
        e = jnp.exp(scores - top)
        total = jnp.sum(e, axis=0, keepdims=True)
        low = (e * (1.0 / total)).astype(BF16)
        probs[h] = low
        parts.append(mm(v_t[h * HEAD_DIM : (h + 1) * HEAD_DIM, :], low))
    out_t = jnp.concatenate(parts, axis=0)
    att_t[...] = out_t.astype(BF16)
    att[:, pl.ds(pl.multiple_of(p * PAIR, PAIR), PAIR)] = out_t.T.astype(BF16)

    @pl.when(p == pl.num_programs(0) - 1)
    def _():
        mid = start[...] + mm(att[...], w_out[...]) + table[OUT_BIAS : OUT_BIAS + 1, :]
        middle[...] = mid
        centred, _inv = norm_stats(mid)
        out = (centred * table[GAIN_TWO : GAIN_TWO + 1, :] + table[BIAS_TWO : BIAS_TWO + 1, :]).astype(BF16)
        normed[...] = out
        normed_t[...] = out.T


def attend_call(qkv, start, table, w_out):
    t, d = start.shape
    pairs = HEADS // 2

    def block(base):
        return pl.BlockSpec((t, PAIR), lambda p: (0, base + p))

    return pl.pallas_call(
        attend_kernel,
        grid=(pairs,),
        in_specs=[
            block(0),
            block(pairs),
            block(2 * pairs),
            whole((t, d)),
            whole(table.shape),
            whole((d, d)),
        ],
        out_specs=[
            pl.BlockSpec((2, t, t), lambda p: (p, 0, 0)),
            pl.BlockSpec((PAIR, t), lambda p: (p, 0)),
            whole((t, d)),
            whole((t, d)),
            whole((d, t)),
        ],
        out_shape=[
            jax.ShapeDtypeStruct((HEADS, t, t), BF16),
            jax.ShapeDtypeStruct((d, t), BF16),
            jax.ShapeDtypeStruct((t, d), F32),
            jax.ShapeDtypeStruct((t, d), BF16),
            jax.ShapeDtypeStruct((d, t), BF16),
        ],
        scratch_shapes=[pltpu.VMEM((t, d), BF16)],
        compiler_params=pltpu.CompilerParams(vmem_limit_bytes=40 * MIB),
        cost_estimate=pl.CostEstimate(
            flops=2 * t * d * (8 * t + d), bytes_accessed=20 * MIB, transcendentals=HEADS * t * t
        ),
        name="attend",
    )(qkv, qkv, qkv, start, table, w_out)


def feed_kernel(normed, normed_t, dy, middle, table, w_up, b_up, w_down, out, grad_n, down_g, up_g, up_b, total):
    c = pl.program_id(0)

    @pl.when(c == 0)
    def _():
        total[...] = middle[...] + table[DOWN_BIAS : DOWN_BIAS + 1, :]
        grad_n[...] = jnp.zeros_like(grad_n)

    hidden = mm(normed[...], w_up[...]) + b_up[...]
    phi = 0.5 * (1.0 + lax.erf(hidden * 0.7071067811865476))
    slope = phi + hidden * jnp.exp(-0.5 * hidden * hidden) * 0.3989422804014327
    active = (hidden * phi).astype(BF16)
    total[...] += mm(active, w_down[...])
    down_g[...] = mm(active.T, dy[...]).astype(BF16)
    grad_h = mm_nt(dy[...], w_down[...]) * slope
    low = grad_h.astype(BF16)
    up_b[...] = jnp.sum(low.astype(F32), axis=0, keepdims=True)
    up_g[...] = mm(normed_t[...], low).astype(BF16)
    grad_n[...] += mm_nt(low, w_up[...])

    @pl.when(c == pl.num_programs(0) - 1)
    def _():
        out[...] = total[...].astype(BF16)


def feed_call(normed, normed_t, dy, middle, table, w_up, b_up, w_down, step):
    t, d = normed.shape
    ff = w_up.shape[1]
    return pl.pallas_call(
        feed_kernel,
        grid=(ff // step,),
        in_specs=[
            whole((t, d)),
            whole((d, t)),
            whole((t, d)),
            whole((t, d)),
            whole(table.shape),
            pl.BlockSpec((d, step), lambda c: (0, c)),
            pl.BlockSpec((1, step), lambda c: (0, c)),
            pl.BlockSpec((step, d), lambda c: (c, 0)),
        ],
        out_specs=[
            whole((t, d)),
            whole((t, d)),
            pl.BlockSpec((step, d), lambda c: (c, 0)),
            pl.BlockSpec((d, step), lambda c: (0, c)),
            pl.BlockSpec((1, step), lambda c: (0, c)),
        ],
        out_shape=[
            jax.ShapeDtypeStruct((t, d), BF16),
            jax.ShapeDtypeStruct((t, d), F32),
            jax.ShapeDtypeStruct((ff, d), BF16),
            jax.ShapeDtypeStruct((d, ff), BF16),
            jax.ShapeDtypeStruct((1, ff), F32),
        ],
        scratch_shapes=[pltpu.VMEM((t, d), F32)],
        compiler_params=pltpu.CompilerParams(vmem_limit_bytes=44 * MIB),
        cost_estimate=pl.CostEstimate(flops=12 * t * d * ff, bytes_accessed=26 * MIB, transcendentals=2 * t * ff),
        name="feed",
    )(normed, normed_t, dy, middle, table, w_up, b_up, w_down)


def middle_kernel(grad_n, middle, dy, att_t, table, w_out, grad_mid, grad_att, out_g, sums):
    centred, inverse = norm_stats(middle[...])
    grad = grad_n[...]
    dy_f = dy[...].astype(F32)
    mid = dy_f + norm_back(grad, centred, inverse, table[GAIN_TWO : GAIN_TWO + 1, :])
    grad_mid[...] = mid
    low = mid.astype(BF16)
    sums[...] = jnp.concatenate(
        [
            jnp.sum(low.astype(F32), axis=0, keepdims=True),
            jnp.sum(grad * centred, axis=0, keepdims=True),
            jnp.sum(grad, axis=0, keepdims=True),
            jnp.sum(dy_f, axis=0, keepdims=True),
            jnp.zeros((4, mid.shape[1]), F32),
        ],
        axis=0,
    )
    grad_att[...] = mm_nt(low, w_out[...]).astype(BF16)
    out_g[...] = mm(att_t[...], low).astype(BF16)


def middle_call(grad_n, middle, dy, att_t, table, w_out):
    t, d = middle.shape
    return pl.pallas_call(
        middle_kernel,
        out_shape=[
            jax.ShapeDtypeStruct((t, d), F32),
            jax.ShapeDtypeStruct((t, d), BF16),
            jax.ShapeDtypeStruct((d, d), BF16),
            jax.ShapeDtypeStruct((8, d), F32),
        ],
        compiler_params=pltpu.CompilerParams(vmem_limit_bytes=40 * MIB),
        cost_estimate=pl.CostEstimate(flops=4 * t * d * d, bytes_accessed=10 * MIB, transcendentals=0),
        name="middle",
    )(grad_n, middle, dy, att_t, table, w_out)


def back_kernel(q, k, v, probs, grad_a, normed_t, wq, wk, wv, gq, gk, gv, grad_n, sums):
    p = pl.program_id(0)

    @pl.when(p == 0)
    def _():
        grad_n[...] = jnp.zeros_like(grad_n)

    k_t = k[...].T
    dk = dv = None
    dq_t = []
    for h in range(2):
        low = probs[h]
        grad_h = half_of(grad_a[...], h)
        grad_p = mm_nt(v[...], grad_h)
        wide = low.astype(F32)
        inner = jnp.sum(wide * grad_p, axis=0, keepdims=True)
        grad_s = (wide * (grad_p - inner)).astype(BF16)
        dv_h = mm(low, grad_h)
        dk_h = mm(grad_s, half_of(q[...], h))
        dv = dv_h if dv is None else dv + dv_h
        dk = dk_h if dk is None else dk + dk_h
        dq_t.append(mm(k_t[h * HEAD_DIM : (h + 1) * HEAD_DIM, :], grad_s))
    dq = (jnp.concatenate(dq_t, axis=0).T * SCALE).astype(BF16)
    grads = jnp.concatenate([dq, dk.astype(BF16), dv.astype(BF16)], axis=1)
    weights = jnp.concatenate([wq[...], wk[...], wv[...]], axis=1)
    sums[...] = jnp.sum(grads.astype(F32), axis=0, keepdims=True)[None]
    g = mm(normed_t[...], grads).astype(BF16)
    gq[...] = g[:, :PAIR]
    gk[...] = g[:, PAIR : 2 * PAIR]
    gv[...] = g[:, 2 * PAIR :]
    grad_n[...] += mm_nt(grads, weights)


def back_call(qkv, probs, grad_att, normed_t, w_qkv):
    t, d = grad_att.shape
    pairs = HEADS // 2

    def block(rows, base):
        return pl.BlockSpec((rows, PAIR), lambda p: (0, base + p))

    return pl.pallas_call(
        back_kernel,
        grid=(pairs,),
        in_specs=[
            block(t, 0),
            block(t, pairs),
            block(t, 2 * pairs),
            pl.BlockSpec((2, t, t), lambda p: (p, 0, 0)),
            block(t, 0),
            whole((d, t)),
            block(d, 0),
            block(d, pairs),
            block(d, 2 * pairs),
        ],
        out_specs=[
            block(d, 0),
            block(d, 0),
            block(d, 0),
            whole((t, d)),
            pl.BlockSpec((1, 1, 3 * PAIR), lambda p: (p, 0, 0)),
        ],
        out_shape=[jax.ShapeDtypeStruct((d, d), BF16)] * 3
        + [jax.ShapeDtypeStruct((t, d), F32), jax.ShapeDtypeStruct((pairs, 1, 3 * PAIR), F32)],
        compiler_params=pltpu.CompilerParams(vmem_limit_bytes=40 * MIB),
        cost_estimate=pl.CostEstimate(flops=2 * t * d * (16 * t + 6 * d), bytes_accessed=24 * MIB, transcendentals=0),
        name="back",
    )(qkv, qkv, qkv, probs, grad_att, normed_t, w_qkv, w_qkv, w_qkv)


def last_kernel(size, rows, info, masked, grad_n, start, grad_mid, feats, frame, patch, table, feats_g, chosen_g, sums):
    centred, inverse = norm_stats(start[...])
    grad = grad_n[...]
    total = grad_mid[...] + norm_back(grad, centred, inverse, table[GAIN_ONE : GAIN_ONE + 1, :])
    is_masked = masked_column(info[0], masked, size, rows)
    kept = jnp.where(is_masked, 0.0, total)
    sums[...] = jnp.concatenate(
        [
            jnp.sum(jnp.where(is_masked, total, 0.0), axis=0, keepdims=True),
            jnp.sum(grad * centred, axis=0, keepdims=True),
            jnp.sum(grad, axis=0, keepdims=True),
            jnp.zeros((5, total.shape[1]), F32),
        ],
        axis=0,
    )
    low = kept.astype(BF16)
    chosen = jnp.where(info[1] == 1, patch[...], frame[...])
    feats_g[...] = mm_nt(low, chosen).astype(BF16)
    chosen_g[...] = mm(feats[...].T, low).astype(BF16)


def last_call(info, masked, grad_n, start, grad_mid, feats, frame, patch, table, size, rows):
    t, d = start.shape
    f = feats.shape[1]
    vmem = pl.BlockSpec(memory_space=pltpu.VMEM)
    return pl.pallas_call(
        functools.partial(last_kernel, size, rows),
        in_specs=[pl.BlockSpec(memory_space=pltpu.SMEM)] + [vmem] * 8,
        out_shape=[
            jax.ShapeDtypeStruct((t, f), BF16),
            jax.ShapeDtypeStruct((f, d), BF16),
            jax.ShapeDtypeStruct((8, d), F32),
        ],
        compiler_params=pltpu.CompilerParams(vmem_limit_bytes=40 * MIB),
        cost_estimate=pl.CostEstimate(flops=4 * t * d * f, bytes_accessed=6 * MIB, transcendentals=0),
        name="last",
    )(info, masked, grad_n, start, grad_mid, feats, frame, patch, table)


LANES = 256
SEGMENT = 128
SMEM = pl.BlockSpec(memory_space=pltpu.SMEM)
HBM = pl.BlockSpec(memory_space=pltpu.HBM)


def pinned(array):
    return pltpu.with_memory_space_constraint(array, pltpu.HBM)


def place_of(info, chip, x_first):
    rel = jnp.bitwise_xor(chip, info[1] // 2)
    return (rel % 2) * 2 + rel // 2 if x_first else rel


def is_first_core(info):
    return info[1] % 2 == 0


def spread(value, rows, at, send, keep, info, x_first):
    first = is_first_core(info)
    for chip in range(4):
        even = value[2 * chip * rows : (2 * chip + 1) * rows]
        odd = value[(2 * chip + 1) * rows : (2 * chip + 2) * rows]
        place = place_of(info, chip, x_first)
        keep[pl.ds(place, 1), at : at + rows, :] = jnp.where(first, even, odd)[None]
        send[pl.ds(place, 1), at : at + rows, :] = jnp.where(first, odd, even)[None]


def spread_halves(value, at, send, keep, info):
    first = is_first_core(info)
    rows = value.shape[0] // 8
    half = rows // 2
    for i in range(2):
        for chip in range(4):
            begin = 2 * chip * rows + i * half
            even, odd = value[begin : begin + half], value[begin + rows : begin + rows + half]
            place = pl.ds(place_of(info, chip, i == 0), 1)
            keep[i, place, at : at + half, :] = jnp.where(first, even, odd)[None]
            send[i, place, at : at + half, :] = jnp.where(first, odd, even)[None]


def stacked(refs):
    return jnp.concatenate([r[...] for r in refs], axis=0)


def clip_mask(info, masked, size, rows):
    return masked_column(info[0], masked.at[pl.ds(info[0], 1)], size, rows)


def forward_kernel(
    size, rows, info, kinds, masked, *refs,
):
    feats, refs = refs[:size], refs[size:]
    (
        table, frame, patch, w_qkv, w_out, w_up, w_down,
        hat, inverse_t, normed_t, qkv_a, qkv_b, qkv_c, probs_a, probs_b, probs_c, att_t,
        middle, normed_two, normed_two_t, feats_t, ups, downs,
        start, normed, att, projs, w_in, w_back, sems, feed_sems,
    ) = refs
    qkvs, all_probs = (qkv_a, qkv_b, qkv_c), (probs_a, probs_b, probs_c)
    d = att.shape[1]
    third = d // LANES

    def weight_copy(group, i):
        cols = pl.ds(i * d + group * LANES, LANES)
        return pltpu.make_async_copy(w_qkv.at[:, cols], w_in.at[group, :, pl.ds(i * LANES, LANES)], sems.at[group, i])

    proj_copies = [pltpu.make_async_copy(p, projs.at[i], sems.at[third, i]) for i, p in enumerate((frame, patch))]
    out_copy = pltpu.make_async_copy(w_out, w_back, sems.at[third, 2])
    for copy in proj_copies:
        copy.start()
    for group in range(third):
        for i in range(3):
            weight_copy(group, i).start()
    out_copy.start()
    feed_copies = [pltpu.make_async_copy(w, v, feed_sems.at[i]) for i, (w, v) in enumerate(((w_up, ups), (w_down, downs)))]
    is_masked = clip_mask(info, masked, size, rows)
    features = stacked(feats)
    feats_t[...] = features.T
    for copy in proj_copies:
        copy.wait()
    chosen = jnp.where(kinds[info[0]] == 1, projs[1], projs[0])
    start_now = jnp.where(is_masked, table[MASK_EMBED : MASK_EMBED + 1, :], mm(features, chosen))
    start[...] = start_now
    centred, inverse = norm_stats(start_now)
    hat[...] = centred.astype(BF16)
    inverse_t[...] = jnp.broadcast_to(inverse, inverse_t.shape)
    out = (centred * table[GAIN_ONE : GAIN_ONE + 1, :] + table[BIAS_ONE : BIAS_ONE + 1, :]).astype(BF16)
    normed[...] = out
    normed_t[...] = out.T
    for group in range(third):
        for i in range(3):
            weight_copy(group, i).wait()
    out_copy.wait()
    for copy in feed_copies:
        copy.start()

    def project(group):
        lanes = slice(group * LANES, (group + 1) * LANES)
        projected = mm(normed[...], w_in[group])
        q = ((projected[:, :LANES] + table[Q_BIAS : Q_BIAS + 1, lanes]) * SCALE).astype(BF16)
        k = projected[:, LANES : 2 * LANES].astype(BF16)
        v = (projected[:, 2 * LANES :] + table[V_BIAS : V_BIAS + 1, lanes]).astype(BF16)
        for i, value in enumerate((q, k, v)):
            qkvs[group][:, i * LANES : (i + 1) * LANES] = value
        return q, k, v.T

    def scores_of(h):
        q, k, _v = held[h // 4]
        pair = slice((h % 4 // 2) * PAIR, (h % 4 // 2 + 1) * PAIR)
        return mm_nt(k[:, pair], half_of(q[:, pair], h % 2))

    held = {0: project(0)}
    upcoming = scores_of(0)
    parts = []
    for h in range(HEADS):
        group = h // 4
        scores = upcoming
        if h % 4 == 2 and group + 1 < third:
            held[group + 1] = project(group + 1)
        if h + 1 < HEADS:
            upcoming = scores_of(h + 1)
        top = jnp.max(scores, axis=0, keepdims=True)
        e = jnp.exp(scores - top)
        total = jnp.sum(e, axis=0, keepdims=True)
        low = (e * (1.0 / total)).astype(BF16)
        all_probs[group][h % 4] = low
        v_t = held[group][2]
        parts.append(mm(v_t[h % 4 * HEAD_DIM : (h % 4 + 1) * HEAD_DIM, :], low))
        if h % 4 == 3:
            out_t = jnp.concatenate(parts, axis=0).astype(BF16)
            parts = []
            lanes = slice(group * LANES, (group + 1) * LANES)
            att_t[lanes, :] = out_t
            att[:, lanes] = out_t.T
    mid = start[...] + mm(att[...], w_back[...]) + table[OUT_BIAS : OUT_BIAS + 1, :]
    middle[...] = mid
    centred, _inv = norm_stats(mid)
    out = (centred * table[GAIN_TWO : GAIN_TWO + 1, :] + table[BIAS_TWO : BIAS_TWO + 1, :]).astype(BF16)
    normed_two[...] = out
    normed_two_t[...] = out.T
    for copy in feed_copies:
        copy.wait()


def forward_call(info, kinds, masked, feats, frame, patch, table, w_qkv, w_out, w_up, w_down, size, rows):
    f, d = frame.shape
    t = size * rows
    third = d // LANES
    return pl.pallas_call(
        functools.partial(forward_kernel, size, rows),
        in_specs=[SMEM, SMEM] + [pl.BlockSpec(memory_space=pltpu.VMEM)] * (size + 2) + [HBM] * 6,
        out_shape=[
            jax.ShapeDtypeStruct((t, d), BF16),
            jax.ShapeDtypeStruct((t, 128), F32),
            jax.ShapeDtypeStruct((d, t), BF16),
            *([jax.ShapeDtypeStruct((t, 3 * LANES), BF16)] * third),
            *([jax.ShapeDtypeStruct((4, t, t), BF16)] * third),
            jax.ShapeDtypeStruct((d, t), BF16),
            jax.ShapeDtypeStruct((t, d), F32),
            jax.ShapeDtypeStruct((t, d), BF16),
            jax.ShapeDtypeStruct((d, t), BF16),
            jax.ShapeDtypeStruct((f, t), BF16),
            jax.ShapeDtypeStruct(w_up.shape, BF16),
            jax.ShapeDtypeStruct(w_down.shape, BF16),
        ],
        scratch_shapes=[
            pltpu.VMEM((t, d), F32),
            pltpu.VMEM((t, d), BF16),
            pltpu.VMEM((t, d), BF16),
            pltpu.VMEM((2, f, d), BF16),
            pltpu.VMEM((third, d, 3 * LANES), BF16),
            pltpu.VMEM((d, d), BF16),
            pltpu.SemaphoreType.DMA((third + 1, 3)),
            pltpu.SemaphoreType.DMA((2,)),
        ],
        compiler_params=pltpu.CompilerParams(vmem_limit_bytes=FORWARD_MIB * MIB),
        cost_estimate=pl.CostEstimate(
            flops=2 * t * d * (f + 4 * d + 8 * t), bytes_accessed=24 * MIB, transcendentals=HEADS * t * t
        ),
        name="forward",
    )(info, kinds, masked, *feats, table, *(pinned(w) for w in (frame, patch, w_qkv, w_out, w_up, w_down)))


def feed_forward_kernel(normed, middle, table, b_up, ups, downs, out, actives, slopes, total):
    step = downs.shape[0] // 2
    total[...] = middle[...] + table[DOWN_BIAS : DOWN_BIAS + 1, :]

    @pl.loop(0, 2)
    def _(c):
        cols = pl.ds(pl.multiple_of(c * step, step), step)
        hidden = mm(normed[...], ups[:, cols]) + b_up[:, cols]
        phi = 0.5 * (1.0 + lax.erf(hidden * 0.7071067811865476))
        slopes[:, cols] = (phi + hidden * jnp.exp(-0.5 * hidden * hidden) * 0.3989422804014327).astype(BF16)
        active = (hidden * phi).astype(BF16)
        actives[:, cols] = active
        total[...] += mm(active, downs[cols, :])

    out[...] = total[...].astype(BF16)


def down_kernel(size, info, actives, *refs):
    dy_pieces, (dy, send, keep) = refs[:size], refs[size:]
    first = is_first_core(info)
    step = actives.shape[1] // 4
    half = step // 4
    grad_rows = stacked(dy_pieces)
    dy[...] = grad_rows
    for c in range(4):
        down_g = mm(actives[:, c * step : (c + 1) * step].T, grad_rows).astype(BF16)
        for i in range(2):
            even = down_g[i * half : (i + 1) * half]
            odd = down_g[(2 + i) * half : (3 + i) * half]
            place = pl.ds(place_of(info, c, i == 0), 1)
            keep[i, place] = jnp.where(first, even, odd)[None]
            send[i, place] = jnp.where(first, odd, even)[None]


def feed_back_kernel(info, normed_t, dy, slopes, ups, downs, grad_n, send, keep, up_b):
    first = is_first_core(info)
    step = downs.shape[0] // 4
    rows = normed_t.shape[0] // 8
    grad_n[...] = jnp.zeros_like(grad_n)

    @pl.loop(0, 2)
    def _(c):
        cols = pl.ds(pl.multiple_of(2 * c * step, 2 * step), 2 * step)
        low = (mm_nt(dy[...], downs[cols, :]) * slopes[:, cols].astype(F32)).astype(BF16)
        up_b[:, cols] = jnp.sum(low.astype(F32), axis=0, keepdims=True)
        up_g = mm(normed_t[...], low).astype(BF16)
        for chip in range(4):
            place = jnp.where(c == 0, place_of(info, chip, True), place_of(info, chip, False))
            for n in range(2):
                lanes = slice(n * step, (n + 1) * step)
                even = up_g[2 * chip * rows : (2 * chip + 1) * rows, lanes]
                odd = up_g[(2 * chip + 1) * rows : (2 * chip + 2) * rows, lanes]
                where = (pl.ds(c, 1), pl.ds(place, 1), pl.ds(n * rows, rows))
                keep[where] = jnp.where(first, even, odd)[None, None]
                send[where] = jnp.where(first, odd, even)[None, None]
        grad_n[...] += mm_nt(low, ups[:, cols])


VMEM = pl.BlockSpec(memory_space=pltpu.VMEM)


def feed_forward_call(normed, middle, table, b_up, ups, downs):
    t, d = normed.shape
    ff = ups.shape[1]
    return pl.pallas_call(
        feed_forward_kernel,
        in_specs=[VMEM] * 6,
        out_shape=[
            jax.ShapeDtypeStruct((t, d), BF16),
            jax.ShapeDtypeStruct((t, ff), BF16),
            jax.ShapeDtypeStruct((t, ff), BF16),
        ],
        scratch_shapes=[pltpu.VMEM((t, d), F32)],
        compiler_params=pltpu.CompilerParams(vmem_limit_bytes=FEED_MIB * MIB),
        cost_estimate=pl.CostEstimate(flops=4 * t * d * ff, bytes_accessed=18 * MIB, transcendentals=2 * t * ff),
        name="feed_forward",
    )(normed, middle, table, b_up, ups, downs)


def down_call(info, actives, dy):
    t, ff = actives.shape
    d = dy[0].shape[1]
    held = jax.ShapeDtypeStruct((2, 4, ff // 16, d), BF16)
    return pl.pallas_call(
        functools.partial(down_kernel, len(dy)),
        in_specs=[SMEM] + [VMEM] * (1 + len(dy)),
        out_shape=[jax.ShapeDtypeStruct((t, d), BF16), held, held],
        compiler_params=pltpu.CompilerParams(vmem_limit_bytes=FEED_MIB * MIB),
        cost_estimate=pl.CostEstimate(flops=2 * t * d * ff, bytes_accessed=9 * MIB, transcendentals=0),
        name="down",
    )(info, actives, *dy)


def feed_back_call(info, normed_t, dy, slopes, ups, downs):
    d, t = normed_t.shape
    ff = ups.shape[1]
    held = jax.ShapeDtypeStruct((2, 4, 2 * d // 8, ff // 4), BF16)
    return pl.pallas_call(
        feed_back_kernel,
        in_specs=[SMEM] + [VMEM] * 5,
        out_shape=[
            jax.ShapeDtypeStruct((t, d), F32),
            held,
            held,
            jax.ShapeDtypeStruct((1, ff), F32),
        ],
        compiler_params=pltpu.CompilerParams(vmem_limit_bytes=FEED_MIB * MIB),
        cost_estimate=pl.CostEstimate(flops=6 * t * d * ff, bytes_accessed=18 * MIB, transcendentals=0),
        name="feed_back",
    )(info, normed_t, dy, slopes, ups, downs)


def middle_kernel_fast(info, grad_n, middle, dy, att_t, table, w_out, grad_mid, grad_att, send, keep, sums, w, sem):
    copy = pltpu.make_async_copy(w_out, w, sem)
    copy.start()
    centred, inverse = norm_stats(middle[...])
    grad = grad_n[...]
    dy_f = dy[...].astype(F32)
    mid = dy_f + norm_back(grad, centred, inverse, table[GAIN_TWO : GAIN_TWO + 1, :])
    grad_mid[...] = mid.astype(BF16)
    low = mid.astype(BF16)
    sums[...] = jnp.concatenate(
        [
            jnp.sum(low.astype(F32), axis=0, keepdims=True),
            jnp.sum(grad * centred, axis=0, keepdims=True),
            jnp.sum(grad, axis=0, keepdims=True),
            jnp.sum(dy_f, axis=0, keepdims=True),
            jnp.zeros((4, mid.shape[1]), F32),
        ],
        axis=0,
    )
    out_g = mm(att_t[...], low).astype(BF16)
    spread(out_g, out_g.shape[0] // 8, 0, send, keep, info, True)
    copy.wait()
    grad_att[...] = mm_nt(low, w[...]).astype(BF16)


def middle_call_fast(info, grad_n, middle, dy, att_t, table, w_out):
    t, d = middle.shape
    vmem = pl.BlockSpec(memory_space=pltpu.VMEM)
    held = jax.ShapeDtypeStruct((4, d // 8, d), BF16)
    return pl.pallas_call(
        middle_kernel_fast,
        in_specs=[SMEM] + [vmem] * 5 + [HBM],
        out_shape=[
            jax.ShapeDtypeStruct((t, d), BF16),
            jax.ShapeDtypeStruct((t, d), BF16),
            held,
            held,
            jax.ShapeDtypeStruct((8, d), F32),
        ],
        scratch_shapes=[pltpu.VMEM((d, d), BF16), pltpu.SemaphoreType.DMA],
        compiler_params=pltpu.CompilerParams(vmem_limit_bytes=OTHER_MIB * MIB),
        cost_estimate=pl.CostEstimate(flops=4 * t * d * d, bytes_accessed=10 * MIB, transcendentals=0),
        name="middle",
    )(info, grad_n, middle, dy, att_t, table, pinned(w_out))


def back_group(group, qkv, probs, grad_a, normed_t, w_qkv, w, sems):
    d = w.shape[0]
    copies = [
        pltpu.make_async_copy(
            w_qkv.at[:, pl.ds(i * d + group * LANES, LANES)], w.at[:, pl.ds(i * LANES, LANES)], sems.at[i]
        )
        for i in range(3)
    ]
    for copy in copies:
        copy.start()
    q, k, v = (qkv[:, i * LANES : (i + 1) * LANES] for i in range(3))
    k_t = k.T
    dq_t, dks, dvs = [], [], []
    for pair in range(2):
        lanes = slice(pair * PAIR, (pair + 1) * PAIR)
        qp, vp, gp = q[:, lanes], v[:, lanes], grad_a[:, lanes]
        dk = dv = None
        for h in range(2):
            low = probs[2 * pair + h]
            grad_h = half_of(gp, h)
            grad_p = mm_nt(vp, grad_h)
            wide = low.astype(F32)
            inner = jnp.sum(wide * grad_p, axis=0, keepdims=True)
            grad_s = (wide * (grad_p - inner)).astype(BF16)
            dv_h = mm(low, grad_h)
            dk_h = mm(grad_s, half_of(qp, h))
            dv = dv_h if dv is None else dv + dv_h
            dk = dk_h if dk is None else dk + dk_h
            head = 2 * pair + h
            dq_t.append(mm(k_t[head * HEAD_DIM : (head + 1) * HEAD_DIM, :], grad_s))
        dks.append(dk.astype(BF16))
        dvs.append(dv.astype(BF16))
    dq = (jnp.concatenate(dq_t, axis=0) * SCALE).astype(BF16).T
    grads = jnp.concatenate([dq] + dks + dvs, axis=1)
    sums = jnp.sum(grads.astype(F32), axis=0, keepdims=True)
    weight_grad = mm(normed_t[...], grads).astype(BF16)
    for copy in copies:
        copy.wait()
    return weight_grad, mm_nt(grads, w[...]), sums


def back_kernel_fast(group, info, qkv, probs, grad_a, normed_t, w_qkv, *refs):
    opens = group == 0
    if not opens:
        grad_in, send_o, keep_o, send_a, keep_a, *refs = refs
    grad_n, sums, send, keep, w, sems = refs
    g, grad, total = back_group(group, qkv, probs, grad_a, normed_t, w_qkv, w, sems)
    grad_n[...] = grad if opens else grad_in[...] + grad
    sums[...] = total
    if opens:
        spread(g, g.shape[0] // 8, 0, send, keep, info, False)
    else:
        rows = g.shape[0] // 8
        for ref, one, two in ((send, send_o, send_a), (keep, keep_o, keep_a)):
            ref[0, :, :rows] = one[...]
            ref[1, :, :rows] = two[...]
        spread_halves(g, rows, send, keep, info)


def back_specs(t, d, group):
    return [
        SMEM,
        whole((t, 3 * LANES)),
        whole((4, t, t)),
        pl.BlockSpec((t, LANES), lambda s: (0, group)),
        whole((d, t)),
        HBM,
    ]


def back_scratch(d):
    return [pltpu.VMEM((d, 3 * LANES), BF16), pltpu.SemaphoreType.DMA((3,))]


def back_call_fast(info, qkv, probs, grad_att, normed_t, w_qkv, group, carried):
    t, d = grad_att.shape
    held = (4, d // 8, d) if group == 0 else (2, 4, 3 * d // 16, d)
    return pl.pallas_call(
        functools.partial(back_kernel_fast, group),
        grid=(1,),
        in_specs=back_specs(t, d, group) + [whole(a.shape) for a in carried],
        out_specs=[whole((t, d)), whole((1, d)), whole(held), whole(held)],
        out_shape=[
            jax.ShapeDtypeStruct((t, d), F32),
            jax.ShapeDtypeStruct((1, d), F32),
            jax.ShapeDtypeStruct(held, BF16),
            jax.ShapeDtypeStruct(held, BF16),
        ],
        scratch_shapes=back_scratch(d),
        compiler_params=pltpu.CompilerParams(vmem_limit_bytes=OTHER_MIB * MIB),
        cost_estimate=pl.CostEstimate(flops=2 * t * d * (16 * t + 6 * d) // 3, bytes_accessed=9 * MIB, transcendentals=0),
        name="back",
    )(info, qkv, probs, grad_att, normed_t, pinned(w_qkv), *carried)


def last_kernel_fast(
    size, rows, group, info, qkv, probs, grad_a, normed_t, w_qkv, grad_in, kinds, masked, hat, inverse_t, grad_mid, *refs
):
    feats_t, frame, patch, table, sums_two, sums_a, sums_b, *refs = refs
    up_b, feats_g, send, keep, w, sems = refs
    g, grad, sums_c = back_group(group, qkv, probs, grad_a, normed_t, w_qkv, w, sems)
    d = g.shape[0]
    half = d // 16
    (send_x, send_y), (keep_x, keep_y) = ((r.at[0], r.at[1]) for r in (send, keep))
    spread_halves(g, 0, send, keep, info)
    grad = grad_in[...] + grad
    centred, inverse = hat[...].astype(F32), inverse_t[:, :1]
    total = grad_mid[...].astype(F32) + norm_back(grad, centred, inverse, table[GAIN_ONE : GAIN_ONE + 1, :])
    is_masked = clip_mask(info, masked, size, rows)
    low = jnp.where(is_masked, 0.0, total).astype(BF16)
    is_patch = kinds[info[0]] == 1
    chosen = jnp.where(is_patch, patch[...], frame[...])
    feats_g[...] = mm_nt(low, chosen).astype(BF16)
    g = mm(feats_t[...], low).astype(BF16)
    none = jnp.zeros_like(g)
    b = g.shape[0] // 8
    spread(jnp.where(is_patch, none, g), b, half, send_x, keep_x, info, True)
    spread(jnp.where(is_patch, g, none), b, half, send_y, keep_y, info, False)
    for ref in (send_y, keep_y):
        ref[:, half + b :, :] = jnp.zeros((4, 16, d), BF16)
    sums = [sums_a[...], sums_b[...], sums_c]
    vectors = jnp.concatenate(
        [
            jnp.sum(jnp.where(is_masked, total, 0.0), axis=0, keepdims=True),
            jnp.sum(grad * centred, axis=0, keepdims=True),
            jnp.sum(grad, axis=0, keepdims=True),
            jnp.concatenate([s[:, :LANES] for s in sums], axis=1),
            jnp.concatenate([s[:, 2 * LANES :] for s in sums], axis=1),
            sums_two[0:4, :],
            jnp.zeros((7, d), F32),
        ],
        axis=0,
    )
    width = d // 8
    wide = up_b.shape[1] // 8
    blocks = []
    for r in range(8):
        rolled = vectors if r == 0 else pltpu.roll(vectors, d - r * width, 1)
        up = jnp.concatenate([up_b[:, r * wide : (r + 1) * wide], jnp.zeros((1, d - wide), F32)], axis=1)
        blocks.append(jnp.concatenate([rolled[:9], up, jnp.zeros((6, d), F32)], axis=0))
    spread(jnp.concatenate(blocks, axis=0).astype(BF16), 16, half + b, send_x, keep_x, info, True)


def last_call_fast(
    info, qkv, probs, grad_att, normed_t, w_qkv, carried, kinds, masked, hat, inverse_t, grad_mid, feats_t, frame, patch, table,
    sums_two, sums_a, sums_b, up_b, size, rows,
):
    t, d = grad_att.shape
    f = frame.shape[0]
    held = (2, 4, d // 16 + f // 8 + 16, d)
    more = (masked, hat, inverse_t, grad_mid, feats_t, frame, patch, table, sums_two, sums_a, sums_b, up_b)
    group = d // LANES - 1
    return pl.pallas_call(
        functools.partial(last_kernel_fast, size, rows, group),
        grid=(1,),
        in_specs=back_specs(t, d, group) + [whole(carried.shape), SMEM] + [whole(a.shape) for a in more],
        out_specs=[whole((t, f)), whole(held), whole(held)],
        out_shape=[
            jax.ShapeDtypeStruct((t, f), BF16),
            jax.ShapeDtypeStruct(held, BF16),
            jax.ShapeDtypeStruct(held, BF16),
        ],
        scratch_shapes=back_scratch(d),
        compiler_params=pltpu.CompilerParams(vmem_limit_bytes=OTHER_MIB * MIB),
        cost_estimate=pl.CostEstimate(flops=2 * t * d * (16 * t + 6 * d) // 3, bytes_accessed=16 * MIB, transcendentals=0),
        name="last",
    )(info, qkv, probs, grad_att, normed_t, pinned(w_qkv), carried, kinds, *more)


def settle_kernel(one, two, down, up):
    down[...] = one[...].astype(F32)
    b = up.shape[0]
    for c in range(4):
        up[:, c * two.shape[1] : (c + 1) * two.shape[1]] = two[c * b : (c + 1) * b].astype(F32)


def settle(one, two, b):
    d = one.shape[1]
    vmem = pl.BlockSpec(memory_space=pltpu.VMEM)
    return pl.pallas_call(
        settle_kernel,
        in_specs=[vmem] * 2,
        out_shape=[jax.ShapeDtypeStruct(one.shape, F32), jax.ShapeDtypeStruct((b, 4 * d), F32)],
        cost_estimate=pl.CostEstimate(flops=0, bytes_accessed=6 * MIB, transcendentals=0),
        compiler_params=pltpu.CompilerParams(vmem_limit_bytes=8 * MIB),
        name="settle",
    )(one, two)


def settle_last_kernel(za, zb, out_g, qkv_g, frame_g, patch_g, vec):
    b, d = out_g.shape
    fr = frame_g.shape[0]
    one, two = za[...].astype(F32), zb[...].astype(F32)
    x1, y1 = one[: one.shape[0] // 2], one[one.shape[0] // 2 :]
    x2, y2 = two[: two.shape[0] // 2], two[two.shape[0] // 2 :]
    out_g[...] = x1[:b]
    half = b // 2
    groups = (y1[:b],), (x1[b:], y1[b:]), (x2[:half], y2[:half])
    for s, pieces in enumerate(groups):
        at = 0
        for value in pieces:
            for i in range(3):
                lane = i * d + s * LANES
                qkv_g[at : at + value.shape[0], lane : lane + LANES] = value[:, i * LANES : (i + 1) * LANES]
            at += value.shape[0]
    frame_g[...] = x2[half : half + fr]
    patch_g[...] = y2[half : half + fr]
    vec[...] = x2[half + fr :]


def settle_last(za, zb, b, fr):
    d = za.shape[1]
    vmem = pl.BlockSpec(memory_space=pltpu.VMEM)
    return pl.pallas_call(
        settle_last_kernel,
        in_specs=[vmem] * 2,
        out_shape=[
            jax.ShapeDtypeStruct((b, d), F32),
            jax.ShapeDtypeStruct((b, 3 * d), F32),
            jax.ShapeDtypeStruct((fr, d), F32),
            jax.ShapeDtypeStruct((fr, d), F32),
            jax.ShapeDtypeStruct((16, d), F32),
        ],
        cost_estimate=pl.CostEstimate(flops=0, bytes_accessed=4 * MIB, transcendentals=0),
        compiler_params=pltpu.CompilerParams(vmem_limit_bytes=8 * MIB),
        name="settle_last",
    )(za, zb)


def place_kernel(size, info, *refs):
    out = refs[size]
    for i in range(size):

        @pl.when(pl.program_id(0) == i)
        def _():
            out[0] = refs[i][...]


def place(info, pieces):
    size = len(pieces)
    shape = pieces[0].shape
    return pl.pallas_call(
        functools.partial(place_kernel, size),
        grid_spec=pltpu.PrefetchScalarGridSpec(
            num_scalar_prefetch=1,
            grid=(size,),
            in_specs=[pl.BlockSpec(shape, lambda i, info: (0, 0))] * size,
            out_specs=pl.BlockSpec((1,) + shape, lambda i, info: (jnp.bitwise_xor(info[0], i), 0, 0)),
        ),
        out_shape=jax.ShapeDtypeStruct((size,) + shape, pieces[0].dtype),
        cost_estimate=pl.CostEstimate(flops=0, bytes_accessed=4 * size * pieces[0].size, transcendentals=0),
        compiler_params=pltpu.CompilerParams(vmem_limit_bytes=8 * MIB),
        name="place",
    )(info, *pieces)


def swap(block, axis, size, flip):
    return lax.ppermute(block, axis, [(i, i ^ flip) for i in range(size)])


def to_clip(pieces, me, size):
    out = [lax.dynamic_index_in_dim(pieces, me, 0, keepdims=False)]
    for d in range(1, size):
        out.append(swap(lax.dynamic_index_in_dim(pieces, me ^ d, 0, keepdims=False), "seq", size, d))
    return jnp.concatenate(out, axis=0)


def to_pieces(clip_rows, me, size):
    rel = clip_rows.reshape(size, -1, clip_rows.shape[-1])
    got = [rel[0]] + [swap(rel[d], "seq", size, d) for d in range(1, size)]
    out = jnp.zeros_like(rel)
    for d in range(size):
        out = lax.dynamic_update_index_in_dim(out, got[d], me ^ d, 0)
    return out


def bits_of(n):
    return n.bit_length() - 1


def fold_clips(grad, order, n):
    count = bits_of(n)
    me = lax.axis_index("clips")
    rows, width = grad.shape
    held = grad.reshape((2,) * count + (rows // n, width))
    left = list(range(count - 1, -1, -1))
    for bit in order:
        axis = left.index(bit)
        mine = (me >> bit) & 1
        send = lax.dynamic_index_in_dim(held, 1 - mine, axis, keepdims=False)
        keep = lax.dynamic_index_in_dim(held, mine, axis, keepdims=False)
        held = keep + swap(send, "clips", n, 1 << bit)
        left.pop(axis)
    return held


def sum_seq(part, size):
    me = lax.axis_index("seq")
    count = bits_of(size)
    held = part
    for bit in range(count):
        half = held.shape[1] // 2
        mine = (me >> bit) & 1
        send = lax.dynamic_slice_in_dim(held, (1 - mine) * half, half, 1)
        keep = lax.dynamic_slice_in_dim(held, mine * half, half, 1)
        held = keep + swap(send, "seq", size, 1 << bit)
    for bit in reversed(range(count)):
        got = swap(held, "seq", size, 1 << bit)
        mine = (me >> bit) & 1
        held = jnp.where(
            mine == 0, jnp.concatenate([held, got], axis=1), jnp.concatenate([got, held], axis=1)
        )
    return held


def clip_orders(n):
    count = bits_of(n)
    low = [0] if count else []
    rest = list(range(1, count))
    return low + rest, low + rest[::-1]


def reduce_grad(grad, n, size):
    first, second = clip_orders(n)
    half = grad.shape[1] // 2
    a = fold_clips(grad[:, :half], first, n)
    b = fold_clips(grad[:, half:], second, n)
    return sum_seq(jnp.concatenate([a, b], axis=1), size).astype(F32)


FORWARD_MIB, FEED_MIB, OTHER_MIB = 18, 14, 12


def tie(*values):
    return lax.optimization_barrier(values)


def over(block, bit):
    return swap(block, "clips", 8, 1 << bit)


def hop(block, pairs):
    return lax.ppermute(block, "seq", pairs)


INWARD, ACROSS, OUTWARD = [(0, 1), (3, 2)], [(1, 2), (2, 1)], [(1, 0), (2, 3)]
NEAR, FAR = [(i, i ^ 1) for i in range(4)], [(i, i ^ 2) for i in range(4)]


def add(*terms):
    total = terms[0].astype(F32)
    for term in terms[1:]:
        total = total + term.astype(F32)
    return total.astype(BF16)


class Item:
    def __init__(self, send, keep):
        self.keep = keep
        self.got = over(send, 0)

    def first(self):
        self.rest = [add(self.keep[i, :2], self.got[i, :2]) for i in range(2)]
        return [add(self.keep[i, 2:], self.got[i, 2:]) for i in range(2)]

    def send_first(self, parts):
        self.one = (over(parts[0], 1), over(parts[1], 2))

    def second(self):
        self.mine = [add(self.rest[i][0], self.one[i][0]) for i in range(2)]
        return [add(self.rest[i][1], self.one[i][1]) for i in range(2)]

    def send_second(self, parts):
        self.two = (over(parts[0], 2), over(parts[1], 1))

    def line(self):
        return jnp.concatenate([add(self.mine[i], self.two[i]) for i in range(2)], axis=0)


def fast_path(features, clip_kind, masked_positions, weights, cotangent):
    (
        frame_proj,
        patch_proj,
        mask_embed,
        norm1_gain,
        norm1_bias,
        w_qkv,
        q_bias,
        v_bias,
        w_out,
        out_bias,
        norm2_gain,
        norm2_bias,
        w_up,
        up_bias,
        w_down,
        down_bias,
    ) = weights
    size = 4
    me = lax.axis_index("seq")
    rows = features.shape[1]
    d = w_out.shape[0]

    def from_pieces(array):
        mine = [lax.dynamic_index_in_dim(array, me ^ i, 0, keepdims=False) for i in range(size)]
        return [mine[0]] + [swap(mine[i], "seq", size, i) for i in range(1, size)]

    def to_owners(array):
        rel = array.reshape(size, rows, -1)
        return [rel[0]] + [swap(rel[i], "seq", size, i) for i in range(1, size)]

    info = jnp.stack([me, lax.axis_index("clips")])
    outer = (me == 0) | (me == 3)
    features, info, outer = tie(features, info, outer)
    feats = from_pieces(features)
    dy = from_pieces(cotangent)
    zero = jnp.zeros_like(q_bias)
    table = jnp.stack(
        [q_bias, zero, v_bias, mask_embed, norm1_gain, norm1_bias, out_bias, norm2_gain, norm2_bias, down_bias]
        + [zero] * 6
    ).astype(F32)
    b_up = up_bias.astype(F32)[None, :]

    hat, inverse_t, normed_one_t, *groups, att_t, middle, normed_two, normed_two_t, feats_t, ups, downs = forward_call(
        info, clip_kind, masked_positions, feats, frame_proj, patch_proj, table, w_qkv, w_out, w_up, w_down, size, rows
    )
    output, actives, slopes = feed_forward_call(normed_two, middle, table, b_up, ups, downs)
    dy, send, keep = down_call(info, actives, dy)
    i1 = Item(send, keep)
    out_pieces = to_owners(output)
    p = i1.first()
    info, slopes, p, i1.rest = tie(info, slopes, p, i1.rest)
    i1.send_first(p)
    grad_n2, send, keep, up_b = feed_back_call(info, normed_two_t, dy, slopes, ups, downs)

    info, send, grad_n2, out_pieces, i1.one = tie(info, send, grad_n2, out_pieces, i1.one)
    i1.send_second(i1.second())
    i2 = Item(send, keep)
    grad_mid, grad_att, send_o, keep_o, sums_two = middle_call_fast(info, grad_n2, middle, dy, att_t, table, w_out)
    p = i2.first()
    info, grad_att, p, i2.rest, i1.two = tie(info, grad_att, p, i2.rest, i1.two)
    i2.send_first(p)
    z1 = i1.line()
    got1 = hop(z1, INWARD)
    grad_a, sums_a, send_a, keep_a = back_call_fast(info, groups[0], groups[3], grad_att, normed_one_t, w_qkv, 0, ())
    grad_b, sums_b, send, keep = back_call_fast(
        info, groups[1], groups[4], grad_att, normed_one_t, w_qkv, 1, (grad_a, send_o, keep_o, send_a, keep_a)
    )

    info, send, i2.one, got1 = tie(info, send, i2.one, got1)
    i4 = Item(send, keep)
    i2.send_second(i2.second())
    z1 = add(z1, got1)
    got1 = hop(z1, ACROSS)
    p = i4.first()
    info, grad_b, p, i4.rest = tie(info, grad_b, p, i4.rest)
    i4.send_first(p)
    feats_grad, send, keep = last_call_fast(
        info, groups[2], groups[5], grad_att, normed_one_t, w_qkv, grad_b, clip_kind, masked_positions, hat, inverse_t,
        grad_mid, feats_t, frame_proj, patch_proj, table, sums_two, sums_a, sums_b, up_b, size, rows,
    )

    info, send, feats_grad, got1 = tie(info, send, feats_grad, got1)
    i5 = Item(send, keep)
    feat0, feat1, feat2, feats_grad = feats_grad.reshape(size, rows, -1)
    feat1, feat2 = swap(feat1, "seq", size, 1), swap(feat2, "seq", size, 2)
    info, feats_grad, feat1, feat2, i2.two, i4.one = tie(info, feats_grad, feat1, feat2, i2.two, i4.one)
    i4.send_second(i4.second())
    z2 = i2.line()
    z1 = add(z1, got1)
    both = hop(jnp.where(outer, z2, z1), INWARD + OUTWARD)
    p = i5.first()
    info, p, i5.rest = tie(info, p, i5.rest)
    i5.send_first(p)
    info, i4.two = tie(info, i4.two)
    z4 = i4.line()
    info, i5.one, both = tie(info, i5.one, both)
    i5.send_second(i5.second())
    z1 = jnp.where(outer, both, z1)
    z2 = jnp.where(outer, z2, add(z2, both))
    got2 = hop(z2, ACROSS)
    got4 = hop(z4, INWARD)
    output = place(info, out_pieces)
    info, i5.two = tie(info, i5.two)
    z5 = i5.line()
    got5 = hop(z5, NEAR)
    info, got2, got4, output = tie(info, got2, got4, output)
    z4 = add(z4, got4)
    got4 = hop(z4, ACROSS)
    z2 = add(z2, got2)
    got2 = hop(z2, OUTWARD)
    info, feats_grad, got5 = tie(info, feats_grad, got5)
    z5 = add(z5, got5)
    got5 = hop(z5, FAR)
    info, feats_grad, got4 = tie(info, feats_grad, got4)
    z4 = add(z4, got4)
    got4 = hop(z4, OUTWARD)
    feat_pieces = [feat0, feat1, feat2, swap(feats_grad, "seq", size, 3)]
    info, got2, feat_pieces = tie(info, got2, feat_pieces)
    down_grad, up_grad = settle(z1, jnp.where(outer, got2, z2), d // 8)
    features_grad = place(info, feat_pieces)
    info, features_grad, down_grad, got4, got5 = tie(info, features_grad, down_grad, got4, got5)
    out_grad, qkv_grad, frame_grad, patch_grad, vec = settle_last(
        jnp.where(outer, got4, z4), add(z5, got5), d // 8, frame_proj.shape[0] // 8
    )
    b = d // 8
    return (
        output,
        features_grad,
        frame_grad,
        patch_grad,
        vec[0, :b],
        vec[1, :b],
        vec[2, :b],
        qkv_grad,
        vec[3, :b],
        vec[4, :b],
        out_grad,
        vec[5, :b],
        vec[6, :b],
        vec[7, :b],
        up_grad,
        vec[9, : up_bias.shape[0] // 8],
        down_grad,
        vec[8, :b],
    )


def body(
    features,
    clip_kind,
    masked_positions,
    frame_proj,
    patch_proj,
    mask_embed,
    norm1_gain,
    norm1_bias,
    w_qkv,
    q_bias,
    v_bias,
    w_out,
    out_bias,
    norm2_gain,
    norm2_bias,
    w_up,
    up_bias,
    w_down,
    down_bias,
    cotangent,
):
    n = lax.axis_size("clips")
    size = lax.axis_size("seq")
    me = lax.axis_index("seq")
    clips_here, rows, _ = features.shape
    assert clips_here == size
    d = w_out.shape[0]
    if n == 8 and size == 4:
        weights = (
            frame_proj,
            patch_proj,
            mask_embed,
            norm1_gain,
            norm1_bias,
            w_qkv,
            q_bias,
            v_bias,
            w_out,
            out_bias,
            norm2_gain,
            norm2_bias,
            w_up,
            up_bias,
            w_down,
            down_bias,
        )
        return fast_path(features, clip_kind, masked_positions, weights, cotangent)

    feats = to_clip(features, me, size)
    dy = to_clip(cotangent, me, size)
    kind = lax.dynamic_index_in_dim(clip_kind, me, 0, keepdims=False)
    info = jnp.stack([me, kind])
    masked = lax.dynamic_index_in_dim(masked_positions, me, 0, keepdims=True)
    zero = jnp.zeros_like(q_bias)
    table = jnp.stack(
        [q_bias, zero, v_bias, mask_embed, norm1_gain, norm1_bias, out_bias, norm2_gain, norm2_bias, down_bias]
        + [zero] * 6
    ).astype(F32)
    b_up = up_bias.astype(F32)[None, :]

    start, normed_one_t, qkv = embed_call(info, masked, feats, frame_proj, patch_proj, table, w_qkv, size, rows)
    probs, att_t, middle, normed_two, normed_two_t = attend_call(qkv, start, table, w_out)
    output, grad_n2, down_grad, up_grad, up_b = feed_call(
        normed_two, normed_two_t, dy, middle, table, w_up, b_up, w_down, 512
    )
    down_grad = reduce_grad(down_grad, n, size)
    up_grad = reduce_grad(up_grad, n, size)
    output = to_pieces(output, me, size)
    grad_mid, grad_att, out_grad, sums_two = middle_call(grad_n2, middle, dy, att_t, table, w_out)
    out_grad = reduce_grad(out_grad, n, size)
    gq, gk, gv, grad_n1, sums_qkv = back_call(qkv, probs, grad_att, normed_one_t, w_qkv)
    qkv_grad = reduce_grad(jnp.concatenate([gq, gk, gv], axis=1), n, size)
    feats_grad, chosen_grad, sums_one = last_call(
        info, masked, grad_n1, start, grad_mid, feats, frame_proj, patch_proj, table, size, rows
    )
    features_grad = to_pieces(feats_grad, me, size)

    vectors = (
        sums_one[0],
        sums_one[1],
        sums_one[2],
        sums_qkv[:, 0, :PAIR].reshape(-1),
        sums_qkv[:, 0, 2 * PAIR :].reshape(-1),
        sums_two[0],
        sums_two[1],
        sums_two[2],
        up_b[0],
        sums_two[3],
    )
    flat = jnp.concatenate([v.reshape(n, -1) for v in vectors], axis=1)
    feat_rows = frame_proj.shape[0] // n
    lanes = -(-flat.shape[1] // (feat_rows * 128)) * 128
    small = jnp.pad(flat, ((0, 0), (0, feat_rows * lanes - flat.shape[1])))
    small = small.reshape(n * feat_rows, lanes).astype(BF16)
    none = jnp.zeros_like(chosen_grad)
    is_patch = kind == 1
    last = jnp.concatenate(
        [jnp.where(is_patch, none, chosen_grad), jnp.where(is_patch, chosen_grad, none), small], axis=1
    )
    last = sum_seq(fold_clips(last, clip_orders(n)[0], n), size).astype(F32)
    frame_grad = last[:, :d]
    patch_grad = last[:, d : 2 * d]
    flat = last[:, 2 * d :].reshape(-1)
    small_out = []
    at = 0
    for v in vectors:
        small_out.append(flat[at : at + v.shape[0] // n])
        at += v.shape[0] // n
    (
        mask_out,
        gain1_out,
        bias1_out,
        q_out,
        v_out,
        outb_out,
        gain2_out,
        bias2_out,
        upb_out,
        downb_out,
    ) = small_out
    return (
        output,
        features_grad,
        frame_grad,
        patch_grad,
        mask_out,
        gain1_out,
        bias1_out,
        qkv_grad,
        q_out,
        v_out,
        out_grad,
        outb_out,
        gain2_out,
        bias2_out,
        up_grad,
        upb_out,
        down_grad,
        downb_out,
    )


def solution(mesh):
    tokens = P("clips", "seq", None)
    rows = P("clips", None)
    vec = P("clips")
    return jax.shard_map(
        body,
        mesh=mesh,
        in_specs=(tokens, P("clips"), rows) + (P(),) * 16 + (tokens,),
        out_specs=(tokens, tokens, rows, rows, vec, vec, vec, rows, vec, vec, rows, vec, vec, vec, rows, vec, rows, vec),
        check_vma=False,
    )
```
